256 devices in a mesh: blk: 16 (over x, y_lo, core), group: 16 (over y_hi, z).
Axes of the slice: x: 4, y: 4 (y_hi: 2, y_lo: 2; y = y_hi * 2 + y_lo), z: 8, core: 2. Of those that a mesh axis runs over, the one named last changes fastest.
Arguments:
- image_emb: float32 [65536, 1152], P(('blk', 'group')), may hold values from -0.2 to 0.2
- text_emb: float32 [65536, 1152], P(('blk', 'group')), may hold values from -0.2 to 0.2
- log_scale: float32 [], replicated, may hold values from 2 to 2.6
- bias: float32 [], replicated, may hold values from -8 to -5
Outputs:
- loss: float32 [], replicated
- grad_image: float32 [65536, 1152], P(('blk', 'group'))
- grad_text: float32 [65536, 1152], P(('blk', 'group'))
- grad_log_scale: float32 [], replicated
- grad_bias: float32 [], replicated
The draws below stay inside these ranges and needn't reach their ends.
All inputs are finite; a program needn't handle non-finite values.
Results may differ from the reference program's by a relative error of at most 0.0028.
Values may be sent and summed in bfloat16 or wider, within the bound.
No kernel may reach another device: no remote copies, remote signals or barrier semaphores. Data moves between devices by JAX's collectives and lax.ppermute only.
A program may use at most 128 MiB of HBM per device.

```python
import jax
import jax.numpy as jnp
from jax import lax

D = 1152
ROWS = 256
BATCH = 65536
N_BLK = 16
N_GROUP = 16


def shared_direction(key):
    subkeys = jax.random.split(key, 4)
    centers = jax.random.normal(subkeys[0], (32, D), jnp.float32)
    labels = jax.random.randint(subkeys[1], (BATCH,), 0, 32)
    weight = jax.random.uniform(subkeys[2], (BATCH, 1), jnp.float32, 0.55, 0.9)
    row_noise = jax.random.normal(subkeys[3], (BATCH, D), jnp.float32)
    return (jnp.take(centers, labels, axis=0), weight, row_noise)


def blend_rows(center_rows, weight, row_noise):
    return weight * center_rows + jnp.sqrt(1.0 - weight * weight) * row_noise


def draw_image_emb(key, part):
    center_rows, weight, row_noise = shared_direction(key)
    spread = jnp.ones((BATCH, 1), jnp.float32)
    image_dir = blend_rows(center_rows, weight, row_noise)
    return jnp.clip(0.03 * spread * image_dir, -0.2, 0.2)


def draw_text_emb(key, part):
    center_rows, weight, row_noise = shared_direction(key)
    key = jax.random.fold_in(key, 13)
    subkeys = jax.random.split(key, 2)
    align = jax.random.uniform(subkeys[0], (BATCH, 1), jnp.float32, 0.45, 0.85)
    fresh_noise = jax.random.normal(subkeys[1], (BATCH, D), jnp.float32)
    spread = jnp.ones((BATCH, 1), jnp.float32)
    image_dir = blend_rows(center_rows, weight, row_noise)
    text_dir = align * image_dir + jnp.sqrt(1.0 - align * align) * fresh_noise
    return jnp.clip(0.03 * spread * text_dir, -0.2, 0.2)


def setup_inputs(seed: int = 0) -> dict:
    key_list = jax.random.split(jax.random.key(seed), 5)
    image_emb = draw_image_emb(jax.random.fold_in(key_list[4], 71), 0)
    text_emb = draw_text_emb(jax.random.fold_in(key_list[4], 71), 0)
    log_scale = jnp.clip(jax.random.uniform(key_list[2], (), jnp.float32, 2.0, 2.6), 2.0, 2.6)
    bias = jnp.clip(jax.random.uniform(key_list[3], (), jnp.float32, -8.0, -5.0), -8.0, -5.0)
    return {"image_emb": image_emb, "text_emb": text_emb, "log_scale": log_scale, "bias": bias}


def normalize(emb):
    squares = lax.optimization_barrier(jnp.sum(emb * emb, axis=1, keepdims=True))
    inverse = lax.rsqrt(squares + 1e-06)
    return (emb * inverse, inverse)

def backnorm(hat, inverse, upstream):
    along = lax.optimization_barrier(jnp.sum(hat * upstream, axis=1, keepdims=True))
    return inverse * (upstream - hat * along)

def one_set(image_set, text_set, scale, bias):
    set_rows = image_set.shape[0]
    text_ids = jnp.arange(set_rows, dtype=jnp.int32)

    def step(carry, index):
        dtext, loss_sum, scale_sum, bias_sum = carry
        start = (index * ROWS).astype(jnp.int32)
        rows_now = lax.dynamic_slice_in_dim(image_set, start, ROWS, 0)
        image_ids = start + jnp.arange(ROWS, dtype=jnp.int32)
        sim = lax.dot_general(rows_now, text_set, (((1,), (1,)), ((), ())), preferred_element_type=jnp.float32)
        scaled = scale * sim
        logits = scaled + bias
        positive = image_ids[:, None] == text_ids[None, :]
        sign = jnp.where(positive, 1.0, -1.0).astype(jnp.float32)
        loss_sum = loss_sum + jnp.sum(jax.nn.softplus(-sign * logits))
        grad = jax.nn.sigmoid(logits) - positive.astype(jnp.float32)
        scale_sum = scale_sum + jnp.sum(grad * scaled)
        bias_sum = bias_sum + jnp.sum(grad)
        grad_q = grad.astype(jnp.bfloat16)
        dimage = scale * jnp.dot(grad_q, text_set, preferred_element_type=jnp.float32)
        dtext = dtext + scale * lax.dot_general(grad_q, rows_now, (((0,), (0,)), ((), ())), preferred_element_type=jnp.float32)
        return ((dtext, loss_sum, scale_sum, bias_sum), dimage)
    zero = jnp.zeros((), jnp.float32)
    init = (jnp.zeros(text_set.shape, jnp.float32), zero, zero, zero)
    final, blocks_out = lax.scan(step, init, jnp.arange(set_rows // ROWS, dtype=jnp.int32))
    dtext, loss_sum, scale_sum, bias_sum = final
    dimage = blocks_out.reshape(set_rows, image_set.shape[1])
    return (dimage, dtext, loss_sum, scale_sum, bias_sum)

def reference(image_emb, text_emb, log_scale, bias):
    image_hat, image_inv = normalize(image_emb)
    text_hat, text_inv = normalize(text_emb)
    image_norm = image_hat.astype(jnp.bfloat16)
    text_norm = text_hat.astype(jnp.bfloat16)
    scale = jnp.exp(log_scale)
    total_rows = image_emb.shape[0]
    width = image_emb.shape[1]

    def to_sets(array):
        return array.reshape(N_BLK, N_GROUP, ROWS, width).transpose(1, 0, 2, 3).reshape(N_GROUP, N_BLK * ROWS, width)

    def from_sets(array):
        return array.reshape(N_GROUP, N_BLK, ROWS, width).transpose(1, 0, 2, 3).reshape(total_rows, width)

    def outer(carry, pair):
        loss_sum, scale_sum, bias_sum = carry
        dimage, dtext, loss_part, scale_part, bias_part = one_set(pair[0], pair[1], scale, bias)
        return ((loss_sum + loss_part, scale_sum + scale_part, bias_sum + bias_part), (dimage, dtext))
    zero = jnp.zeros((), jnp.float32)
    sums, grads = lax.scan(outer, (zero, zero, zero), (to_sets(image_norm), to_sets(text_norm)))
    loss_sum, scale_sum, bias_sum = sums
    dimage = from_sets(grads[0])
    dtext = from_sets(grads[1])
    grad_image = backnorm(image_hat, image_inv, dimage)
    grad_text = backnorm(text_hat, text_inv, dtext)
    return (loss_sum / total_rows, grad_image, grad_text, scale_sum / total_rows, bias_sum / total_rows)
```

```python
import jax
import jax.numpy as jnp
from jax import lax
from jax.experimental import pallas as pl
from jax.experimental.pallas import tpu as pltpu
from jax.sharding import PartitionSpec as P

F32 = jnp.float32
BF16 = jnp.bfloat16
VMEM = pl.BlockSpec(memory_space=pltpu.VMEM)
SMEM = pl.BlockSpec(memory_space=pltpu.SMEM)


def params(mib):
    return pltpu.CompilerParams(vmem_limit_bytes=mib * 1024 * 1024)


def unit_rows(emb):
    inverse = lax.rsqrt(jnp.sum(emb * emb, axis=1, keepdims=True) + 1e-06)
    return emb * inverse, inverse


def normalize_kernel(image_ref, text_ref, image_out, text_out):
    image_out[...] = unit_rows(image_ref[...])[0].astype(BF16)
    text_out[...] = unit_rows(text_ref[...])[0].astype(BF16)


def normalize(image_emb, text_emb):
    rows, width = image_emb.shape
    return pl.pallas_call(
        normalize_kernel,
        out_shape=(jax.ShapeDtypeStruct((rows, width), BF16),) * 2,
        in_specs=[VMEM] * 2,
        out_specs=(VMEM,) * 2,
        compiler_params=params(16),
        cost_estimate=pl.CostEstimate(
            flops=8 * rows * width, bytes_accessed=12 * rows * width, transcendentals=rows
        ),
        name="normalize",
    )(image_emb, text_emb)


def cut(block, at):
    rows, width = block.shape

    def kernel(block_ref, out_ref):
        out_ref[...] = block_ref[pl.ds(at, rows // 2), :]

    return pl.pallas_call(
        kernel,
        out_shape=jax.ShapeDtypeStruct((rows // 2, width), block.dtype),
        in_specs=[VMEM],
        out_specs=VMEM,
        compiler_params=params(16),
        cost_estimate=pl.CostEstimate(flops=0, bytes_accessed=rows * width, transcendentals=0),
        name="cut",
    )(block)


def sim_tile(image_rows, text_rows):
    return lax.dot_general(
        image_rows, text_rows, (((1,), (1,)), ((), ())), preferred_element_type=F32
    )


def pair_tile(sim, scale, bias, diagonal):
    scaled = scale * sim
    logits = scaled + bias
    rows, columns = sim.shape
    if diagonal:
        positive = lax.broadcasted_iota(jnp.int32, (rows, columns), 0) == (
            lax.broadcasted_iota(jnp.int32, (rows, columns), 1)
        )
        logits = jnp.where(positive, -logits, logits)
    odds = jnp.exp(logits)
    total = 1.0 + odds
    inverse = pl.reciprocal(total, approx=True)
    inverse = inverse * (2.0 - total * inverse)
    grad = odds * inverse
    if diagonal:
        grad = jnp.where(positive, -grad, grad)
    lost = (odds - (total - 1.0)) * inverse
    part = rows // 8
    product = total[:part]
    for i in range(1, 8):
        product = product * total[i * part : (i + 1) * part]

    def fold(values):
        return jnp.sum(values.reshape(values.shape[0] // 8, 8, columns), axis=0)

    loss = fold(jnp.log(product)) + fold(lost)
    return grad.astype(BF16), loss, fold(grad * scaled), fold(grad)


def write_sums(sums_ref, loss, scaled, grad):
    row = lax.broadcasted_iota(jnp.int32, sums_ref.shape, 0)
    sums_ref[...] = jnp.where(
        row == 0, jnp.sum(loss), jnp.where(row == 1, jnp.sum(scaled), jnp.sum(grad))
    )


def write_copies(out, sums):
    for i in range(out.shape[0] // 8):
        out[pl.ds(i * 8, 8), :] = sums


def near_kernel(
    scalars, own_i, left_i, right_i, own_t, core_t, y_t, yc_t,
    own_out, left_top_out, left_bot_out, right_top_out, right_bot_out,
    images, texts, grads, sums_ref,
):
    rows = own_i.shape[0]
    half = rows // 2
    scale, bias = scalars[0], scalars[1]
    for i, src in enumerate((own_i, left_i, right_i)):
        images[pl.ds(i * rows, rows), :] = src[...]
    for i, src in enumerate((own_t, core_t, y_t, yc_t)):
        texts[pl.ds(i * rows, rows), :] = src[...]
    loss = scaled = grad = jnp.zeros((8, rows), F32)
    tiles = [(b, t) for b in range(3) for t in range(4)]

    def sim_of(k):
        b, t = tiles[k]
        return sim_tile(images[pl.ds(b * rows, rows), :], texts[pl.ds(t * rows, rows), :])

    sim = sim_of(0)
    for k, (b, t) in enumerate(tiles):
        sim_next = sim_of(k + 1) if k + 1 < len(tiles) else None
        grad_q, loss_now, scaled_now, grad_now = pair_tile(sim, scale, bias, k == 0)
        grads[pl.ds(b * rows, rows), pl.ds(t * rows, rows)] = grad_q
        loss, scaled, grad = loss + loss_now, scaled + scaled_now, grad + grad_now
        sim = sim_next
        if t == 3:
            partial = jnp.dot(
                grads[pl.ds(b * rows, rows), :], texts[...], preferred_element_type=F32
            )
            if b == 0:
                own_out[...] = partial
            elif b == 1:
                left_top_out[...] = partial[:half].astype(BF16)
                left_bot_out[...] = partial[half:]
            else:
                right_top_out[...] = partial[:half]
                right_bot_out[...] = partial[half:].astype(BF16)
    write_sums(sums_ref, loss, scaled, grad)


def text_grad(grads, near_images, far_grads, far_images, at):
    return lax.dot_general(
        grads[:, at], near_images[...], (((0,), (0,)), ((), ())), preferred_element_type=F32
    ) + lax.dot_general(
        far_grads[:, at], far_images[...], (((0,), (0,)), ((), ())), preferred_element_type=F32
    )


def far_kernel(
    scalars, top_i, bot_i, near_images, texts, near_grads, near_sums,
    far_top, far_bot, y_out, yc_out, images, grads, sums_ref,
):
    half = top_i.shape[0]
    rows = 2 * half
    scale, bias = scalars[0], scalars[1]
    images[pl.ds(0, half), :] = top_i[...]
    images[pl.ds(half, half), :] = bot_i[...]
    loss = scaled = grad = jnp.zeros((8, rows), F32)

    def sim_of(t):
        return sim_tile(images[...], texts[pl.ds(t * rows, rows), :])

    sim = sim_of(0)
    for t in range(4):
        sim_next = sim_of(t + 1) if t < 3 else None
        grad_q, loss_now, scaled_now, grad_now = pair_tile(sim, scale, bias, False)
        grads[:, pl.ds(t * rows, rows)] = grad_q
        loss, scaled, grad = loss + loss_now, scaled + scaled_now, grad + grad_now
        sim = sim_next
    partial = jnp.dot(grads[...], texts[...], preferred_element_type=F32)
    far_top[...] = partial[:half].astype(BF16)
    far_bot[...] = partial[half:].astype(BF16)
    yc_out[...] = text_grad(near_grads, near_images, grads, images, pl.ds(3 * rows, rows)).astype(BF16)
    y_out[...] = text_grad(near_grads, near_images, grads, images, pl.ds(2 * rows, rows))
    write_sums(sums_ref, loss, scaled, grad)
    sums_ref[...] += near_sums[...]


def text_kernel(
    near_grads, far_grads, near_images, far_images, own_p, top_p, bot_p, sums,
    own_out, core_out, own_sum, sums_out,
):
    rows = far_images.shape[0]
    half = rows // 2
    for t, out in ((1, core_out), (0, own_out)):
        out[...] = text_grad(
            near_grads, near_images, far_grads, far_images, pl.ds(t * rows, rows)
        ).astype(out.dtype)
    own_sum[:half, :] = own_p[:half, :] + top_p[...].astype(F32)
    own_sum[half:, :] = own_p[half:, :] + bot_p[...].astype(F32)
    write_copies(sums_out, sums[...])


def near_part(scalars, images, texts):
    rows, width = texts[0].shape
    half = rows // 2
    shape = jax.ShapeDtypeStruct
    return pl.pallas_call(
        near_kernel,
        out_shape=(
            shape((rows, width), F32),
            shape((half, width), BF16),
            shape((half, width), F32),
            shape((half, width), F32),
            shape((half, width), BF16),
            shape((3 * rows, width), BF16),
            shape((4 * rows, width), BF16),
            shape((3 * rows, 4 * rows), BF16),
            shape((8, 128), F32),
        ),
        in_specs=[SMEM] + [VMEM] * 7,
        out_specs=(VMEM,) * 9,
        compiler_params=params(32),
        cost_estimate=pl.CostEstimate(
            flops=2 * 2 * 12 * rows * rows * width,
            bytes_accessed=24 * rows * width,
            transcendentals=3 * 12 * rows * rows,
        ),
        name="near",
    )(scalars, *images, *texts)


def far_part(scalars, far_images, near_images, texts, near_grads, near_sums):
    half, width = far_images[0].shape
    rows = 2 * half
    shape = jax.ShapeDtypeStruct
    return pl.pallas_call(
        far_kernel,
        out_shape=(
            shape((half, width), BF16),
            shape((half, width), BF16),
            shape((rows, width), F32),
            shape((rows, width), BF16),
            shape((rows, width), BF16),
            shape((rows, 4 * rows), BF16),
            shape((8, 128), F32),
        ),
        in_specs=[SMEM] + [VMEM] * 6,
        out_specs=(VMEM,) * 7,
        compiler_params=params(32),
        cost_estimate=pl.CostEstimate(
            flops=rows * rows * width,
            bytes_accessed=2 * rows * width,
            transcendentals=rows * rows,
        ),
        name="far",
    )(scalars, *far_images, near_images, texts, near_grads, near_sums)


def text_part(near_grads, far_grads, near_images, far_images, own_p, top_p, bot_p, sums, copies):
    rows, width = far_images.shape
    shape = jax.ShapeDtypeStruct
    return pl.pallas_call(
        text_kernel,
        out_shape=(
            shape((rows, width), F32), shape((rows, width), BF16), shape((rows, width), F32),
            shape((copies * 8, 128), F32),
        ),
        in_specs=[VMEM] * 8,
        out_specs=(VMEM,) * 4,
        compiler_params=params(32),
        cost_estimate=pl.CostEstimate(
            flops=rows * rows * width, bytes_accessed=rows * width, transcendentals=0
        ),
        name="text",
    )(near_grads, far_grads, near_images, far_images, own_p, top_p, bot_p, sums)


def relay_y_kernel(own, passing, out):
    out[...] = (own[...] + passing[...].astype(F32)).astype(BF16)


def relay_y(own, passing):
    return pl.pallas_call(
        relay_y_kernel,
        out_shape=jax.ShapeDtypeStruct(passing.shape, BF16),
        in_specs=[VMEM] * 2,
        out_specs=VMEM,
        compiler_params=params(16),
        cost_estimate=pl.CostEstimate(flops=passing.size, bytes_accessed=passing.size, transcendentals=0),
        name="relay_y",
    )(own, passing)


def relay_kernel(top, top_passing, bot, bot_passing, own_p, arrived, top_out, bot_out, own_out, sums_out):
    top_out[...] = (top[...] + top_passing[...].astype(F32)).astype(BF16)
    bot_out[...] = (bot[...] + bot_passing[...].astype(F32)).astype(BF16)
    own_out[...] = own_p[...]
    sums = arrived[pl.ds(0, 8), :]
    for i in range(1, arrived.shape[0] // 8):
        sums += arrived[pl.ds(i * 8, 8), :]
    write_copies(sums_out, sums)


def relay(top, top_passing, bot, bot_passing, own_p, arrived, copies):
    shape = jax.ShapeDtypeStruct
    return pl.pallas_call(
        relay_kernel,
        out_shape=(
            shape(top.shape, BF16), shape(bot.shape, BF16), shape(own_p.shape, F32),
            shape((copies * 8, 128), F32),
        ),
        in_specs=[VMEM] * 6,
        out_specs=(VMEM,) * 4,
        compiler_params=params(16),
        cost_estimate=pl.CostEstimate(flops=top.size, bytes_accessed=top.size, transcendentals=0),
        name="relay",
    )(top, top_passing, bot, bot_passing, own_p, arrived)


def backnorm(emb, upstream, scale):
    hat, inverse = unit_rows(emb)
    along = jnp.sum(hat * upstream, axis=1, keepdims=True)
    return (scale * inverse) * (upstream - hat * along)


def image_end_kernel(scalars, emb, own, top, bot, out):
    half = emb.shape[0] // 2
    for at, part in ((0, top), (half, bot)):
        at = pl.ds(at, half)
        out[at, :] = backnorm(emb[at, :], own[at, :] + part[...].astype(F32), scalars[0])


def text_end_kernel(scalars, emb, own, one, two, out):
    upstream = own[...] + one[...].astype(F32) + two[...].astype(F32)
    out[...] = backnorm(emb[...], upstream, scalars[0])


def end_part(kernel, name, scalars, emb, *parts):
    rows, width = emb.shape
    return pl.pallas_call(
        kernel,
        out_shape=jax.ShapeDtypeStruct((rows, width), F32),
        in_specs=[SMEM] + [VMEM] * (1 + len(parts)),
        out_specs=VMEM,
        compiler_params=params(24),
        cost_estimate=pl.CostEstimate(
            flops=10 * rows * width, bytes_accessed=16 * rows * width, transcendentals=rows
        ),
        name=name,
    )(scalars, emb, *parts)


def shards(image_emb, text_emb, log_scale, bias):
    rows = image_emb.shape[0]
    blocks = lax.axis_size("blk")
    groups = lax.axis_size("group")
    ahead = [(i, (i + 4) % blocks) for i in range(blocks)]
    back = [(i, (i - 4) % blocks) for i in range(blocks)]
    across_y = [(i, i ^ 2) for i in range(blocks)]
    across_core = [(i, i ^ 1) for i in range(blocks)]

    def send(value, perm):
        return lax.ppermute(value, "blk", perm)

    scale = jnp.exp(log_scale)
    scalars = jnp.stack([scale, bias])
    own_i, own_t = normalize(image_emb, text_emb)
    left_i = send(own_i, ahead)
    right_i = send(own_i, back)
    y_t = send(own_t, across_y)
    core_t = send(own_t, across_core)
    yc_t = send(y_t, across_core)
    top_i = send(cut(left_i, 0), ahead)
    bot_i = send(cut(right_i, rows // 2), back)

    (
        own_p, left_top_p, left_bot_p, right_top_p, right_bot_p,
        near_images, texts, near_grads, near_sums,
    ) = near_part(scalars, (own_i, left_i, right_i), (own_t, core_t, y_t, yc_t))
    from_left_bot = send(right_bot_p, ahead)
    from_right_top = send(left_top_p, back)

    far_top, far_bot, y_q, yc_q, far_images, far_grads, sums = far_part(
        scalars, (top_i, bot_i), near_images, texts, near_grads, near_sums
    )
    relay_top = send(far_top, ahead)
    relay_bot = send(far_bot, back)
    from_y = send(relay_y(y_q, send(yc_q, across_core)), across_y)
    own_q, core_q, own_p, sums = text_part(
        near_grads, far_grads, near_images, far_images, own_p, from_right_top, from_left_bot, sums, blocks
    )
    from_core = send(core_q, across_core)
    sums = lax.all_to_all(sums, "blk", split_axis=0, concat_axis=0, tiled=True)
    top_sum, bot_sum, own_p, sums = relay(
        right_top_p, relay_top, left_bot_p, relay_bot, own_p, sums, groups
    )
    from_left_top = send(top_sum, ahead)
    from_right_bot = send(bot_sum, back)
    sums = lax.all_to_all(sums, "group", split_axis=0, concat_axis=0, tiled=True)
    sums = jnp.sum(sums.reshape(groups, 8, 128), axis=0)

    grad_text = end_part(text_end_kernel, "text_end", scalars, text_emb, own_q, from_core, from_y)
    grad_image = end_part(
        image_end_kernel, "image_end", scalars, image_emb,
        own_p, from_left_top, from_right_bot,
    )
    totals = sums[:, 0] / (rows * blocks * groups)
    return (totals[0], grad_image, grad_text, totals[1], totals[2])


def solution(mesh):
    in_specs = (P(("blk", "group"), None), P(("blk", "group"), None), P(), P())
    out_specs = (P(), P(("blk", "group"), None), P(("blk", "group"), None), P(), P())
    return jax.shard_map(shards, mesh=mesh, in_specs=in_specs, out_specs=out_specs, check_vma=False)
```

```python
import jax
import jax.numpy as jnp
from jax import lax
from jax.experimental import pallas as pl
from jax.experimental.pallas import tpu as pltpu
from jax.sharding import PartitionSpec as P

F32 = jnp.float32
BF16 = jnp.bfloat16
HBM = pl.BlockSpec(memory_space=pltpu.HBM)
VMEM = pl.BlockSpec(memory_space=pltpu.VMEM)
SMEM = pl.BlockSpec(memory_space=pltpu.SMEM)


def params(mib):
    return pltpu.CompilerParams(vmem_limit_bytes=mib * 1024 * 1024)


def unit_rows(emb):
    inverse = lax.rsqrt(jnp.sum(emb * emb, axis=1, keepdims=True) + 1e-06)
    return emb * inverse, inverse


def normalize_kernel(image_ref, text_ref, image_out, text_out, images, texts, sems):
    rows = image_ref.shape[0]
    step = rows // 4
    pairs = [
        (src.at[pl.ds(i * step, step)], dst.at[pl.ds(i * step, step)])
        for src, dst in ((image_ref, images), (text_ref, texts))
        for i in range(4)
    ]
    copies = [pltpu.make_async_copy(src, dst, sems.at[i]) for i, (src, dst) in enumerate(pairs)]
    for copy in copies:
        copy.start()
    for k, (emb, out) in enumerate(((images, image_out), (texts, text_out))):
        for i in range(4):
            copies[4 * k + i].wait()
            at = pl.ds(i * step, step)
            out[at, :] = unit_rows(emb[at, :])[0].astype(BF16)


def normalize(image_emb, text_emb):
    rows, width = image_emb.shape
    return pl.pallas_call(
        normalize_kernel,
        out_shape=(jax.ShapeDtypeStruct((rows, width), BF16),) * 2,
        in_specs=[HBM] * 2,
        out_specs=(VMEM,) * 2,
        scratch_shapes=[
            pltpu.VMEM((rows, width), F32),
            pltpu.VMEM((rows, width), F32),
            pltpu.SemaphoreType.DMA((8,)),
        ],
        compiler_params=params(16),
        cost_estimate=pl.CostEstimate(
            flops=8 * rows * width, bytes_accessed=12 * rows * width, transcendentals=rows
        ),
        name="normalize",
    )(image_emb, text_emb)


def cut(block, at):
    rows, width = block.shape

    def kernel(block_ref, out_ref):
        out_ref[...] = block_ref[pl.ds(at, rows // 2), :]

    return pl.pallas_call(
        kernel,
        out_shape=jax.ShapeDtypeStruct((rows // 2, width), block.dtype),
        in_specs=[VMEM],
        out_specs=VMEM,
        compiler_params=params(16),
        cost_estimate=pl.CostEstimate(flops=0, bytes_accessed=rows * width, transcendentals=0),
        name="cut",
    )(block)


def sim_tile(image_rows, text_rows):
    return lax.dot_general(
        image_rows, text_rows, (((1,), (1,)), ((), ())), preferred_element_type=F32
    )


def pair_tile(sim, scale, bias, diagonal):
    scaled = scale * sim
    logits = scaled + bias
    rows, columns = sim.shape
    if diagonal:
        positive = lax.broadcasted_iota(jnp.int32, (rows, columns), 0) == (
            lax.broadcasted_iota(jnp.int32, (rows, columns), 1)
        )
        logits = jnp.where(positive, -logits, logits)
    odds = jnp.exp(logits)
    total = 1.0 + odds
    inverse = pl.reciprocal(total, approx=True)
    inverse = inverse * (2.0 - total * inverse)
    grad = odds * inverse
    if diagonal:
        grad = jnp.where(positive, -grad, grad)
    lost = (odds - (total - 1.0)) * inverse
    part = rows // 8
    product = total[:part]
    for i in range(1, 8):
        product = product * total[i * part : (i + 1) * part]

    def fold(values):
        return jnp.sum(values.reshape(values.shape[0] // 8, 8, columns), axis=0)

    loss = fold(jnp.log(product)) + fold(lost)
    return grad.astype(BF16), loss, fold(grad * scaled), fold(grad)


def write_sums(sums_ref, loss, scaled, grad):
    row = lax.broadcasted_iota(jnp.int32, sums_ref.shape, 0)
    sums_ref[...] = jnp.where(
        row == 0, jnp.sum(loss), jnp.where(row == 1, jnp.sum(scaled), jnp.sum(grad))
    )


def near_kernel(
    scalars, own_i, left_i, right_i, own_t, core_t, y_t, yc_t,
    own_out, left_top_out, left_bot_out, right_top_out, right_bot_out,
    images, texts, grads, sums_ref,
):
    rows = own_i.shape[0]
    half = rows // 2
    scale, bias = scalars[0], scalars[1]
    for i, src in enumerate((own_i, left_i, right_i)):
        images[pl.ds(i * rows, rows), :] = src[...]
    for i, src in enumerate((own_t, core_t, y_t, yc_t)):
        texts[pl.ds(i * rows, rows), :] = src[...]
    loss = scaled = grad = jnp.zeros((8, rows), F32)
    tiles = [(b, t) for b in range(3) for t in range(4)]

    def sim_of(k):
        b, t = tiles[k]
        return sim_tile(images[pl.ds(b * rows, rows), :], texts[pl.ds(t * rows, rows), :])

    sim = sim_of(0)
    for k, (b, t) in enumerate(tiles):
        sim_next = sim_of(k + 1) if k + 1 < len(tiles) else None
        grad_q, loss_now, scaled_now, grad_now = pair_tile(sim, scale, bias, k == 0)
        grads[pl.ds(b * rows, rows), pl.ds(t * rows, rows)] = grad_q
        loss, scaled, grad = loss + loss_now, scaled + scaled_now, grad + grad_now
        sim = sim_next
        if t == 3:
            partial = jnp.dot(
                grads[pl.ds(b * rows, rows), :], texts[...], preferred_element_type=F32
            )
            if b == 0:
                own_out[...] = partial
            elif b == 1:
                left_top_out[...] = partial[:half].astype(BF16)
                left_bot_out[...] = partial[half:]
            else:
                right_top_out[...] = partial[:half]
                right_bot_out[...] = partial[half:].astype(BF16)
    write_sums(sums_ref, loss, scaled, grad)


def text_grad(grads, near_images, far_grads, far_images, at):
    return lax.dot_general(
        grads[:, at], near_images[...], (((0,), (0,)), ((), ())), preferred_element_type=F32
    ) + lax.dot_general(
        far_grads[:, at], far_images[...], (((0,), (0,)), ((), ())), preferred_element_type=F32
    )


def far_kernel(
    scalars, top_i, bot_i, near_images, texts, near_grads, near_sums,
    far_top, far_bot, y_out, yc_out, images, grads, sums_ref,
):
    half = top_i.shape[0]
    rows = 2 * half
    scale, bias = scalars[0], scalars[1]
    images[pl.ds(0, half), :] = top_i[...]
    images[pl.ds(half, half), :] = bot_i[...]
    loss = scaled = grad = jnp.zeros((8, rows), F32)

    def sim_of(t):
        return sim_tile(images[...], texts[pl.ds(t * rows, rows), :])

    sim = sim_of(0)
    for t in range(4):
        sim_next = sim_of(t + 1) if t < 3 else None
        grad_q, loss_now, scaled_now, grad_now = pair_tile(sim, scale, bias, False)
        grads[:, pl.ds(t * rows, rows)] = grad_q
        loss, scaled, grad = loss + loss_now, scaled + scaled_now, grad + grad_now
        sim = sim_next
    partial = jnp.dot(grads[...], texts[...], preferred_element_type=F32)
    far_top[...] = partial[:half].astype(BF16)
    far_bot[...] = partial[half:].astype(BF16)
    yc_out[...] = text_grad(near_grads, near_images, grads, images, pl.ds(3 * rows, rows)).astype(BF16)
    y_out[...] = text_grad(near_grads, near_images, grads, images, pl.ds(2 * rows, rows))
    write_sums(sums_ref, loss, scaled, grad)
    sums_ref[...] += near_sums[...]


def text_kernel(near_grads, far_grads, near_images, far_images, own_out, core_out):
    rows = far_images.shape[0]
    for t, out in ((1, core_out), (0, own_out)):
        out[...] = text_grad(
            near_grads, near_images, far_grads, far_images, pl.ds(t * rows, rows)
        ).astype(out.dtype)


def near_part(scalars, images, texts):
    rows, width = texts[0].shape
    half = rows // 2
    shape = jax.ShapeDtypeStruct
    return pl.pallas_call(
        near_kernel,
        out_shape=(
            shape((rows, width), F32),
            shape((half, width), BF16),
            shape((half, width), F32),
            shape((half, width), F32),
            shape((half, width), BF16),
            shape((3 * rows, width), BF16),
            shape((4 * rows, width), BF16),
            shape((3 * rows, 4 * rows), BF16),
            shape((8, 128), F32),
        ),
        in_specs=[SMEM] + [VMEM] * 7,
        out_specs=(VMEM,) * 9,
        compiler_params=params(32),
        cost_estimate=pl.CostEstimate(
            flops=2 * 2 * 12 * rows * rows * width,
            bytes_accessed=24 * rows * width,
            transcendentals=3 * 12 * rows * rows,
        ),
        name="near",
    )(scalars, *images, *texts)


def far_part(scalars, far_images, near_images, texts, near_grads, near_sums):
    half, width = far_images[0].shape
    rows = 2 * half
    shape = jax.ShapeDtypeStruct
    return pl.pallas_call(
        far_kernel,
        out_shape=(
            shape((half, width), BF16),
            shape((half, width), BF16),
            shape((rows, width), F32),
            shape((rows, width), BF16),
            shape((rows, width), BF16),
            shape((rows, 4 * rows), BF16),
            shape((8, 128), F32),
        ),
        in_specs=[SMEM] + [VMEM] * 6,
        out_specs=(VMEM,) * 7,
        compiler_params=params(32),
        cost_estimate=pl.CostEstimate(
            flops=rows * rows * width,
            bytes_accessed=2 * rows * width,
            transcendentals=rows * rows,
        ),
        name="far",
    )(scalars, *far_images, near_images, texts, near_grads, near_sums)


def text_part(near_grads, far_grads, near_images, far_images):
    rows, width = far_images.shape
    shape = jax.ShapeDtypeStruct
    return pl.pallas_call(
        text_kernel,
        out_shape=(shape((rows, width), F32), shape((rows, width), BF16)),
        in_specs=[VMEM] * 4,
        out_specs=(VMEM,) * 2,
        compiler_params=params(32),
        cost_estimate=pl.CostEstimate(
            flops=rows * rows * width, bytes_accessed=rows * width, transcendentals=0
        ),
        name="text",
    )(near_grads, far_grads, near_images, far_images)


def relay_y_kernel(own, passing, sums, out, sums_out):
    out[...] = (own[...] + passing[...].astype(F32)).astype(BF16)
    sums_out[...] = sums[...]


def relay_y(own, passing, sums):
    return pl.pallas_call(
        relay_y_kernel,
        out_shape=(jax.ShapeDtypeStruct(passing.shape, BF16), jax.ShapeDtypeStruct(sums.shape, F32)),
        in_specs=[VMEM] * 3,
        out_specs=(VMEM,) * 2,
        compiler_params=params(16),
        cost_estimate=pl.CostEstimate(flops=passing.size, bytes_accessed=passing.size, transcendentals=0),
        name="relay_y",
    )(own, passing, sums)


def relay_kernel(
    top, top_passing, bot, bot_passing, own_p, top_p, bot_p, sums,
    top_out, bot_out, own_out, sums_out,
):
    half = top.shape[0]
    top_out[...] = (top[...] + top_passing[...].astype(F32)).astype(BF16)
    bot_out[...] = (bot[...] + bot_passing[...].astype(F32)).astype(BF16)
    own_out[:half, :] = own_p[:half, :] + top_p[...].astype(F32)
    own_out[half:, :] = own_p[half:, :] + bot_p[...].astype(F32)
    sums_out[...] = sums[...]


def relay(top, top_passing, bot, bot_passing, own_p, top_p, bot_p, sums):
    shape = jax.ShapeDtypeStruct
    return pl.pallas_call(
        relay_kernel,
        out_shape=(
            shape(top.shape, BF16), shape(bot.shape, BF16), shape(own_p.shape, F32),
            shape(sums.shape, F32),
        ),
        in_specs=[VMEM] * 8,
        out_specs=(VMEM,) * 4,
        compiler_params=params(16),
        cost_estimate=pl.CostEstimate(flops=top.size, bytes_accessed=top.size, transcendentals=0),
        name="relay",
    )(top, top_passing, bot, bot_passing, own_p, top_p, bot_p, sums)


def backnorm(emb, upstream, scale):
    hat, inverse = unit_rows(emb)
    along = jnp.sum(hat * upstream, axis=1, keepdims=True)
    return (scale * inverse) * (upstream - hat * along)


def write_rows(out, values, slots, sems, i):
    rows = values.shape[0]
    at = pl.ds(i * rows, rows)
    slots[at, :] = values
    copy = pltpu.make_async_copy(slots.at[at], out.at[at], sems.at[i])
    copy.start()
    return copy


def image_end_kernel(scalars, emb, own, top, bot, out, slots, sems):
    step = emb.shape[0] // 4
    copies = []
    for i in range(4):
        at = pl.ds(i * step, step)
        part = (top, bot)[i // 2][pl.ds(i % 2 * step, step), :]
        values = backnorm(emb[at, :], own[at, :] + part.astype(F32), scalars[0])
        copies.append(write_rows(out, values, slots, sems, i))
    for copy in copies:
        copy.wait()


def text_end_kernel(scalars, emb, own, one, two, out, slots, sems):
    step = emb.shape[0] // 4
    copies = []
    for i in range(4):
        at = pl.ds(i * step, step)
        upstream = own[at, :] + one[at, :].astype(F32) + two[at, :].astype(F32)
        copies.append(write_rows(out, backnorm(emb[at, :], upstream, scalars[0]), slots, sems, i))
    for copy in copies:
        copy.wait()


def end_part(kernel, name, scalars, emb, *parts):
    rows, width = emb.shape
    return pl.pallas_call(
        kernel,
        out_shape=jax.ShapeDtypeStruct((rows, width), F32),
        in_specs=[SMEM] + [VMEM] * (1 + len(parts)),
        out_specs=HBM,
        scratch_shapes=[pltpu.VMEM((rows, width), F32), pltpu.SemaphoreType.DMA((4,))],
        compiler_params=params(24),
        cost_estimate=pl.CostEstimate(
            flops=rows * width, bytes_accessed=rows * width, transcendentals=rows
        ),
        name=name,
    )(scalars, emb, *parts)


def shards(image_emb, text_emb, log_scale, bias):
    rows = image_emb.shape[0]
    blocks = lax.axis_size("blk")
    groups = lax.axis_size("group")
    ahead = [(i, (i + 4) % blocks) for i in range(blocks)]
    back = [(i, (i - 4) % blocks) for i in range(blocks)]
    across_y = [(i, i ^ 2) for i in range(blocks)]
    across_core = [(i, i ^ 1) for i in range(blocks)]

    def send(value, perm):
        return lax.ppermute(value, "blk", perm)

    scale = jnp.exp(log_scale)
    scalars = jnp.stack([scale, bias])
    own_i, own_t = normalize(image_emb, text_emb)
    left_i = send(own_i, ahead)
    right_i = send(own_i, back)
    y_t = send(own_t, across_y)
    core_t = send(own_t, across_core)
    yc_t = send(y_t, across_core)
    top_i = send(cut(left_i, 0), ahead)
    bot_i = send(cut(right_i, rows // 2), back)

    (
        own_p, left_top_p, left_bot_p, right_top_p, right_bot_p,
        near_images, texts, near_grads, near_sums,
    ) = near_part(scalars, (own_i, left_i, right_i), (own_t, core_t, y_t, yc_t))
    from_left_bot = send(right_bot_p, ahead)
    from_right_top = send(left_top_p, back)

    far_top, far_bot, y_q, yc_q, far_images, far_grads, sums = far_part(
        scalars, (top_i, bot_i), near_images, texts, near_grads, near_sums
    )
    relay_top = send(far_top, ahead)
    relay_bot = send(far_bot, back)
    mate_y = send(yc_q, across_core)
    own_q, core_q = text_part(near_grads, far_grads, near_images, far_images)
    y_sum, sums = relay_y(y_q, mate_y, sums)
    from_y = send(y_sum, across_y)
    from_core = send(core_q, across_core)
    sums = lax.psum(sums, "blk")
    top_sum, bot_sum, own_p, sums = relay(
        right_top_p, relay_top, left_bot_p, relay_bot, own_p, from_right_top, from_left_bot, sums
    )
    from_left_top = send(top_sum, ahead)
    from_right_bot = send(bot_sum, back)
    sums = lax.psum(sums, "group")

    grad_text = end_part(text_end_kernel, "text_end", scalars, text_emb, own_q, from_core, from_y)
    grad_image = end_part(
        image_end_kernel, "image_end", scalars, image_emb,
        own_p, from_left_top, from_right_bot,
    )
    totals = sums[:, 0] / (rows * blocks * groups)
    return (totals[0], grad_image, grad_text, totals[1], totals[2])


def solution(mesh):
    in_specs = (P(("blk", "group"), None), P(("blk", "group"), None), P(), P())
    out_specs = (P(), P(("blk", "group"), None), P(("blk", "group"), None), P(), P())
    return jax.shard_map(shards, mesh=mesh, in_specs=in_specs, out_specs=out_specs, check_vma=False)
```

```python
import jax
import jax.numpy as jnp
from jax import lax
from jax.experimental import pallas as pl
from jax.experimental.pallas import tpu as pltpu
from jax.sharding import PartitionSpec as P

F32 = jnp.float32
BF16 = jnp.bfloat16
HBM = pl.BlockSpec(memory_space=pltpu.HBM)
VMEM = pl.BlockSpec(memory_space=pltpu.VMEM)
SMEM = pl.BlockSpec(memory_space=pltpu.SMEM)


def params(mib):
    return pltpu.CompilerParams(vmem_limit_bytes=mib * 1024 * 1024)


def unit_rows(emb):
    inverse = lax.rsqrt(jnp.sum(emb * emb, axis=1, keepdims=True) + 1e-06)
    return emb * inverse, inverse


def normalize_kernel(emb_ref, *refs):
    norm_ref, token = refs[-2:]
    norm_ref[...] = unit_rows(emb_ref[...])[0].astype(BF16)
    token[...] = jnp.zeros(token.shape, F32)


def normalize(emb, *after):
    rows, width = emb.shape
    return pl.pallas_call(
        normalize_kernel,
        out_shape=(
            jax.ShapeDtypeStruct((rows, width), BF16), jax.ShapeDtypeStruct((8, 128), F32)
        ),
        in_specs=[VMEM] * (1 + len(after)),
        out_specs=(VMEM,) * 2,
        compiler_params=params(16),
        cost_estimate=pl.CostEstimate(
            flops=4 * rows * width, bytes_accessed=6 * rows * width, transcendentals=rows
        ),
        name="normalize",
    )(emb, *after)


def cut(block, at):
    rows, width = block.shape

    def kernel(block_ref, out_ref):
        out_ref[...] = block_ref[pl.ds(at, rows // 2), :]

    return pl.pallas_call(
        kernel,
        out_shape=jax.ShapeDtypeStruct((rows // 2, width), block.dtype),
        in_specs=[VMEM],
        out_specs=VMEM,
        compiler_params=params(16),
        cost_estimate=pl.CostEstimate(flops=0, bytes_accessed=rows * width, transcendentals=0),
        name="cut",
    )(block)


def sim_tile(image_rows, text_rows):
    return lax.dot_general(
        image_rows, text_rows, (((1,), (1,)), ((), ())), preferred_element_type=F32
    )


def pair_tile(sim, scale, bias, diagonal):
    scaled = scale * sim
    logits = scaled + bias
    rows, columns = sim.shape
    if diagonal:
        positive = lax.broadcasted_iota(jnp.int32, (rows, columns), 0) == (
            lax.broadcasted_iota(jnp.int32, (rows, columns), 1)
        )
        logits = jnp.where(positive, -logits, logits)
    odds = jnp.exp(logits)
    total = 1.0 + odds
    inverse = pl.reciprocal(total, approx=True)
    inverse = inverse * (2.0 - total * inverse)
    grad = odds * inverse
    if diagonal:
        grad = jnp.where(positive, -grad, grad)
    lost = (odds - (total - 1.0)) * inverse
    part = rows // 8
    product = total[:part]
    for i in range(1, 8):
        product = product * total[i * part : (i + 1) * part]

    def fold(values):
        return jnp.sum(values.reshape(values.shape[0] // 8, 8, columns), axis=0)

    loss = fold(jnp.log(product)) + fold(lost)
    return grad.astype(BF16), loss, fold(grad * scaled), fold(grad)


def write_sums(sums_ref, loss, scaled, grad):
    column = lax.broadcasted_iota(jnp.int32, sums_ref.shape, 1)
    sums_ref[...] = jnp.where(
        column == 0, jnp.sum(loss), jnp.where(column == 1, jnp.sum(scaled), jnp.sum(grad))
    )


def near_kernel(
    scalars, own_i, left_i, right_i, own_t, core_t, y_t, yc_t,
    own_out, left_top_out, left_bot_out, right_top_out, right_bot_out,
    images, texts, grads, sums_ref,
):
    rows = own_i.shape[0]
    half = rows // 2
    scale, bias = scalars[0], scalars[1]
    for i, src in enumerate((own_i, left_i, right_i)):
        images[pl.ds(i * rows, rows), :] = src[...]
    for i, src in enumerate((own_t, core_t, y_t, yc_t)):
        texts[pl.ds(i * rows, rows), :] = src[...]
    loss = scaled = grad = jnp.zeros((8, rows), F32)
    tiles = [(b, t) for b in range(3) for t in range(4)]

    def sim_of(k):
        b, t = tiles[k]
        return sim_tile(images[pl.ds(b * rows, rows), :], texts[pl.ds(t * rows, rows), :])

    sim = sim_of(0)
    for k, (b, t) in enumerate(tiles):
        sim_next = sim_of(k + 1) if k + 1 < len(tiles) else None
        grad_q, loss_now, scaled_now, grad_now = pair_tile(sim, scale, bias, k == 0)
        grads[pl.ds(b * rows, rows), pl.ds(t * rows, rows)] = grad_q
        loss, scaled, grad = loss + loss_now, scaled + scaled_now, grad + grad_now
        sim = sim_next
        if t == 3:
            partial = jnp.dot(
                grads[pl.ds(b * rows, rows), :], texts[...], preferred_element_type=F32
            )
            if b == 0:
                own_out[...] = partial
            elif b == 1:
                left_top_out[...] = partial[:half].astype(BF16)
                left_bot_out[...] = partial[half:]
            else:
                right_top_out[...] = partial[:half]
                right_bot_out[...] = partial[half:].astype(BF16)
    write_sums(sums_ref, loss, scaled, grad)


def text_grad(grads, near_images, far_grads, far_images, at):
    return lax.dot_general(
        grads[:, at], near_images[...], (((0,), (0,)), ((), ())), preferred_element_type=F32
    ) + lax.dot_general(
        far_grads[:, at], far_images[...], (((0,), (0,)), ((), ())), preferred_element_type=F32
    )


def far_kernel(scalars, top_i, bot_i, texts, near_sums, images, grads, sums_ref):
    half = top_i.shape[0]
    rows = 2 * half
    scale, bias = scalars[0], scalars[1]
    images[pl.ds(0, half), :] = top_i[...]
    images[pl.ds(half, half), :] = bot_i[...]
    loss = scaled = grad = jnp.zeros((8, rows), F32)

    def sim_of(t):
        return sim_tile(images[...], texts[pl.ds(t * rows, rows), :])

    sim = sim_of(0)
    for t in range(4):
        sim_next = sim_of(t + 1) if t < 3 else None
        grad_q, loss_now, scaled_now, grad_now = pair_tile(sim, scale, bias, False)
        grads[:, pl.ds(t * rows, rows)] = grad_q
        loss, scaled, grad = loss + loss_now, scaled + scaled_now, grad + grad_now
        sim = sim_next
    write_sums(sums_ref, loss, scaled, grad)
    sums_ref[...] += near_sums[...]


def far_grad_kernel(far_images, far_grads, near_images, texts, near_grads, far_top, far_bot, y_out, yc_out):
    rows = far_images.shape[0]
    half = rows // 2
    partial = jnp.dot(far_grads[...], texts[...], preferred_element_type=F32)
    far_top[...] = partial[:half].astype(BF16)
    far_bot[...] = partial[half:].astype(BF16)
    for t, out in ((3, yc_out), (2, y_out)):
        out[...] = text_grad(
            near_grads, near_images, far_grads, far_images, pl.ds(t * rows, rows)
        ).astype(out.dtype)


def text_kernel(
    near_grads, far_grads, near_images, far_images, own_p, top_p, bot_p,
    own_out, core_out, own_sum, token,
):
    rows = far_images.shape[0]
    for t, out in ((1, core_out), (0, own_out)):
        out[...] = text_grad(
            near_grads, near_images, far_grads, far_images, pl.ds(t * rows, rows)
        ).astype(out.dtype)
    half = rows // 2
    own_sum[:half, :] = own_p[:half, :] + top_p[...].astype(F32)
    own_sum[half:, :] = own_p[half:, :] + bot_p[...].astype(F32)
    token[...] = jnp.zeros(token.shape, F32)


def near_part(scalars, images, texts):
    rows, width = texts[0].shape
    half = rows // 2
    shape = jax.ShapeDtypeStruct
    return pl.pallas_call(
        near_kernel,
        out_shape=(
            shape((rows, width), F32),
            shape((half, width), BF16),
            shape((half, width), F32),
            shape((half, width), F32),
            shape((half, width), BF16),
            shape((3 * rows, width), BF16),
            shape((4 * rows, width), BF16),
            shape((3 * rows, 4 * rows), BF16),
            shape((8, 128), F32),
        ),
        in_specs=[SMEM] + [VMEM] * 7,
        out_specs=(VMEM,) * 9,
        compiler_params=params(16),
        cost_estimate=pl.CostEstimate(
            flops=8 * 2 * 2 * 12 * rows * rows * width,
            bytes_accessed=24 * rows * width,
            transcendentals=3 * 12 * rows * rows,
        ),
        name="near",
    )(scalars, *images, *texts)


def far_part(scalars, far_images, texts, near_sums):
    half, width = far_images[0].shape
    rows = 2 * half
    shape = jax.ShapeDtypeStruct
    return pl.pallas_call(
        far_kernel,
        out_shape=(
            shape((rows, width), BF16), shape((rows, 4 * rows), BF16), shape((8, 128), F32)
        ),
        in_specs=[SMEM] + [VMEM] * 4,
        out_specs=(VMEM,) * 3,
        compiler_params=params(16),
        cost_estimate=pl.CostEstimate(
            flops=rows * rows * width, bytes_accessed=2 * rows * width, transcendentals=rows * rows
        ),
        name="far",
    )(scalars, *far_images, texts, near_sums)


def far_grad_part(far_images, far_grads, near_images, texts, near_grads):
    rows, width = far_images.shape
    shape = jax.ShapeDtypeStruct
    return pl.pallas_call(
        far_grad_kernel,
        out_shape=(shape((rows // 2, width), BF16),) * 2
        + (shape((rows, width), F32), shape((rows, width), BF16)),
        in_specs=[VMEM] * 5,
        out_specs=(VMEM,) * 4,
        compiler_params=params(16),
        cost_estimate=pl.CostEstimate(
            flops=rows * rows * width, bytes_accessed=2 * rows * width, transcendentals=0
        ),
        name="far_grad",
    )(far_images, far_grads, near_images, texts, near_grads)


def text_part(near_grads, far_grads, near_images, far_images, own_p, top_p, bot_p):
    rows, width = far_images.shape
    shape = jax.ShapeDtypeStruct
    return pl.pallas_call(
        text_kernel,
        out_shape=(
            shape((rows, width), F32), shape((rows, width), BF16), shape((rows, width), F32),
            shape((8, 128), F32),
        ),
        in_specs=[VMEM] * 7,
        out_specs=(VMEM,) * 4,
        compiler_params=params(16),
        cost_estimate=pl.CostEstimate(
            flops=64 * rows * rows * width, bytes_accessed=rows * width, transcendentals=0
        ),
        name="text",
    )(near_grads, far_grads, near_images, far_images, own_p, top_p, bot_p)


def relay_y_kernel(own, passing, after, sums, arrived, out, sums_out):
    out[...] = (own[...] + passing[...].astype(F32)).astype(BF16)
    sums_out[...] = sums[...] + arrived[...]


def relay_y(own, passing, after, sums, arrived):
    return pl.pallas_call(
        relay_y_kernel,
        out_shape=(
            jax.ShapeDtypeStruct(passing.shape, BF16), jax.ShapeDtypeStruct(after.shape, F32)
        ),
        in_specs=[VMEM] * 5,
        out_specs=(VMEM,) * 2,
        compiler_params=params(16),
        cost_estimate=pl.CostEstimate(flops=passing.size, bytes_accessed=passing.size, transcendentals=0),
        name="relay_y",
    )(own, passing, after, sums, arrived)


def relay_kernel(
    top, top_passing, bot, bot_passing, sums, arrived, top_out, bot_out, sums_out
):
    top_out[...] = (top[...] + top_passing[...].astype(F32)).astype(BF16)
    bot_out[...] = (bot[...] + bot_passing[...].astype(F32)).astype(BF16)
    sums_out[...] = sums[...] + arrived[...]


def relay(top, top_passing, bot, bot_passing, sums, arrived):
    shape = jax.ShapeDtypeStruct
    return pl.pallas_call(
        relay_kernel,
        out_shape=(shape(top.shape, BF16), shape(bot.shape, BF16), shape(sums.shape, F32)),
        in_specs=[VMEM] * 6,
        out_specs=(VMEM,) * 3,
        compiler_params=params(16),
        cost_estimate=pl.CostEstimate(flops=top.size, bytes_accessed=top.size, transcendentals=0),
        name="relay",
    )(top, top_passing, bot, bot_passing, sums, arrived)


def backnorm(emb, upstream, scale):
    hat, inverse = unit_rows(emb)
    along = jnp.sum(hat * upstream, axis=1, keepdims=True)
    return (scale * inverse) * (upstream - hat * along)


def write_rows(out, values, slots, sems, i):
    rows = values.shape[0]
    at = pl.ds(i * rows, rows)
    slots[at, :] = values
    copy = pltpu.make_async_copy(slots.at[at], out.at[at], sems.at[i])
    copy.start()
    return copy


def text_end_kernel(scalars, emb, own, one, two, after, out, token, slots, sems):
    step = emb.shape[0] // 4
    copies = []
    for i in range(4):
        at = pl.ds(i * step, step)
        upstream = own[at, :] + one[at, :].astype(F32) + two[at, :].astype(F32)
        copies.append(write_rows(out, backnorm(emb[at, :], upstream, scalars[0]), slots, sems, i))
    token[...] = after[...]
    for copy in copies:
        copy.wait()


def image_end_kernel(scalars, emb, own, top, bot, after, out, token, slots, sems):
    step = emb.shape[0] // 4
    copies = []
    for i in range(4):
        at = pl.ds(i * step, step)
        part = (top, bot)[i // 2][pl.ds(i % 2 * step, step), :]
        values = backnorm(emb[at, :], own[at, :] + part.astype(F32), scalars[0])
        copies.append(write_rows(out, values, slots, sems, i))
    token[...] = after[...]
    for copy in copies:
        copy.wait()


def end_part(kernel, name, cost, scalars, emb, *parts):
    rows, width = emb.shape
    return pl.pallas_call(
        kernel,
        out_shape=(
            jax.ShapeDtypeStruct((rows, width), F32), jax.ShapeDtypeStruct((8, 128), F32)
        ),
        in_specs=[SMEM] + [VMEM] * (1 + len(parts)),
        out_specs=(HBM, VMEM),
        scratch_shapes=[pltpu.VMEM((rows, width), F32), pltpu.SemaphoreType.DMA((4,))],
        compiler_params=params(24),
        cost_estimate=pl.CostEstimate(
            flops=cost * rows * width, bytes_accessed=rows * width, transcendentals=rows
        ),
        name=name,
    )(scalars, emb, *parts)


def shards(image_emb, text_emb, log_scale, bias):
    rows = image_emb.shape[0]
    blocks = lax.axis_size("blk")
    groups = lax.axis_size("group")
    ahead = [(i, (i + 4) % blocks) for i in range(blocks)]
    back = [(i, (i - 4) % blocks) for i in range(blocks)]
    across_y = [(i, i ^ 2) for i in range(blocks)]
    across_core = [(i, i ^ 1) for i in range(blocks)]

    def send(value, perm):
        return lax.ppermute(value, "blk", perm)

    scale = jnp.exp(log_scale)
    scalars = jnp.stack([scale, bias])
    own_i, token = normalize(image_emb)
    own_t, _ = normalize(text_emb, token)
    left_i = send(own_i, ahead)
    right_i = send(own_i, back)
    y_t = send(own_t, across_y)
    core_t = send(own_t, across_core)
    yc_t = send(y_t, across_core)
    top_i = send(cut(left_i, 0), ahead)
    bot_i = send(cut(right_i, rows // 2), back)

    (
        own_p, left_top_p, left_bot_p, right_top_p, right_bot_p,
        near_images, texts, near_grads, near_sums,
    ) = near_part(scalars, (own_i, left_i, right_i), (own_t, core_t, y_t, yc_t))
    from_left_bot = send(right_bot_p, ahead)
    from_right_top = send(left_top_p, back)

    far_images, far_grads, sums = far_part(scalars, (top_i, bot_i), texts, near_sums)

    def pair_group(value, k):
        return lax.ppermute(value, "group", [(i, i ^ k) for i in range(groups)])

    def pair_blk(value, k):
        return send(value, [(i, i ^ k) for i in range(blocks)])

    sums_1 = sums + pair_group(sums, 1)
    far_top, far_bot, y_q, yc_q = far_grad_part(
        far_images, far_grads, near_images, texts, near_grads
    )
    relay_top = send(far_top, ahead)
    relay_bot = send(far_bot, back)
    mate_y = send(yc_q, across_core)
    own_q, core_q, own_p, token = text_part(
        near_grads, far_grads, near_images, far_images, own_p, from_right_top, from_left_bot
    )
    y_sum, sums_2 = relay_y(y_q, mate_y, token, sums_1, pair_group(sums_1, 2))
    from_y = send(y_sum, across_y)
    from_core = send(core_q, across_core)
    sums_3 = sums_2 + pair_group(sums_2, 4)
    top_sum, bot_sum, sums_4 = relay(
        right_top_p, relay_top, left_bot_p, relay_bot, sums_3, pair_group(sums_3, 8)
    )
    from_left_top = send(top_sum, ahead)
    from_right_bot = send(bot_sum, back)

    def over_blk(_, value):
        for k in (1, 2, 4, 8):
            value = value + pair_blk(value, k)
        return value

    sums_8 = lax.fori_loop(0, (scale > 0.0).astype(jnp.int32), over_blk, sums_4)

    grad_text, token = end_part(
        text_end_kernel, "text_end", 8, scalars, text_emb, own_q, from_core, from_y, sums_8
    )
    grad_image, _ = end_part(
        image_end_kernel, "image_end", 8, scalars, image_emb,
        own_p, from_left_top, from_right_bot, token,
    )
    totals = sums_8[0] / (rows * blocks * groups)
    return (totals[0], grad_image, grad_text, totals[1], totals[2])


def solution(mesh):
    in_specs = (P(("blk", "group"), None), P(("blk", "group"), None), P(), P())
    out_specs = (P(), P(("blk", "group"), None), P(("blk", "group"), None), P(), P())
    return jax.shard_map(shards, mesh=mesh, in_specs=in_specs, out_specs=out_specs, check_vma=False)
```

```python
import jax
import jax.numpy as jnp
from jax import lax
from jax.experimental import pallas as pl
from jax.experimental.pallas import tpu as pltpu
from jax.sharding import PartitionSpec as P

F32 = jnp.float32
STEPS = (("blk", 4), ("blk", 8), ("group", 1), ("group", 2), ("group", 4), ("group", 8))
BF16 = jnp.bfloat16
HBM = pl.BlockSpec(memory_space=pltpu.HBM)
VMEM = pl.BlockSpec(memory_space=pltpu.VMEM)
SMEM = pl.BlockSpec(memory_space=pltpu.SMEM)


def params(mib):
    return pltpu.CompilerParams(vmem_limit_bytes=mib * 1024 * 1024)


def unit_rows(emb):
    inverse = lax.rsqrt(jnp.sum(emb * emb, axis=1, keepdims=True) + 1e-06)
    return emb * inverse, inverse


def normalize_kernel(emb_ref, *refs):
    norm_ref, token = refs[-2:]
    norm_ref[...] = unit_rows(emb_ref[...])[0].astype(BF16)
    token[...] = jnp.zeros(token.shape, F32)


def normalize(emb, *after):
    rows, width = emb.shape
    return pl.pallas_call(
        normalize_kernel,
        out_shape=(
            jax.ShapeDtypeStruct((rows, width), BF16), jax.ShapeDtypeStruct((8, 128), F32)
        ),
        in_specs=[VMEM] * (1 + len(after)),
        out_specs=(VMEM,) * 2,
        compiler_params=params(16),
        cost_estimate=pl.CostEstimate(
            flops=4 * rows * width, bytes_accessed=6 * rows * width, transcendentals=rows
        ),
        name="normalize",
    )(emb, *after)


def cut(block, at):
    rows, width = block.shape

    def kernel(block_ref, out_ref):
        out_ref[...] = block_ref[pl.ds(at, rows // 2), :]

    return pl.pallas_call(
        kernel,
        out_shape=jax.ShapeDtypeStruct((rows // 2, width), block.dtype),
        in_specs=[VMEM],
        out_specs=VMEM,
        compiler_params=params(16),
        cost_estimate=pl.CostEstimate(flops=0, bytes_accessed=rows * width, transcendentals=0),
        name="cut",
    )(block)


def sim_tile(image_rows, text_rows):
    return lax.dot_general(
        image_rows, text_rows, (((1,), (1,)), ((), ())), preferred_element_type=F32
    )


def pair_tile(sim, scale, bias, diagonal):
    scaled = scale * sim
    logits = scaled + bias
    rows, columns = sim.shape
    if diagonal:
        positive = lax.broadcasted_iota(jnp.int32, (rows, columns), 0) == (
            lax.broadcasted_iota(jnp.int32, (rows, columns), 1)
        )
        logits = jnp.where(positive, -logits, logits)
    odds = jnp.exp(logits)
    total = 1.0 + odds
    inverse = pl.reciprocal(total, approx=True)
    inverse = inverse * (2.0 - total * inverse)
    grad = odds * inverse
    if diagonal:
        grad = jnp.where(positive, -grad, grad)
    lost = (odds - (total - 1.0)) * inverse
    part = rows // 8
    product = total[:part]
    for i in range(1, 8):
        product = product * total[i * part : (i + 1) * part]

    def fold(values):
        return jnp.sum(values.reshape(values.shape[0] // 8, 8, columns), axis=0)

    loss = fold(jnp.log(product)) + fold(lost)
    return grad.astype(BF16), loss, fold(grad * scaled), fold(grad)


def write_sums(sums_ref, loss, scaled, grad):
    column = lax.broadcasted_iota(jnp.int32, sums_ref.shape, 1)
    sums_ref[...] = jnp.where(
        column == 0, jnp.sum(loss), jnp.where(column == 1, jnp.sum(scaled), jnp.sum(grad))
    )


def near_kernel(
    scalars, own_i, left_i, right_i, own_t, core_t, y_t, yc_t,
    own_out, left_out, right_out, images, texts, grads, sums_ref,
):
    rows = own_i.shape[0]
    scale, bias = scalars[0], scalars[1]
    for i, src in enumerate((own_i, left_i, right_i)):
        images[pl.ds(i * rows, rows), :] = src[...]
    for i, src in enumerate((own_t, core_t, y_t, yc_t)):
        texts[pl.ds(i * rows, rows), :] = src[...]
    loss = scaled = grad = jnp.zeros((8, rows), F32)
    tiles = [(b, t) for b in range(3) for t in range(4)]

    def sim_of(k):
        b, t = tiles[k]
        return sim_tile(images[pl.ds(b * rows, rows), :], texts[pl.ds(t * rows, rows), :])

    sim = sim_of(0)
    for k, (b, t) in enumerate(tiles):
        sim_next = sim_of(k + 1) if k + 1 < len(tiles) else None
        grad_q, loss_now, scaled_now, grad_now = pair_tile(sim, scale, bias, k == 0)
        grads[pl.ds(b * rows, rows), pl.ds(t * rows, rows)] = grad_q
        loss, scaled, grad = loss + loss_now, scaled + scaled_now, grad + grad_now
        sim = sim_next
        if t == 3:
            partial = jnp.dot(
                grads[pl.ds(b * rows, rows), :], texts[...], preferred_element_type=F32
            )
            out = (own_out, left_out, right_out)[b]
            out[...] = partial.astype(out.dtype)
    write_sums(sums_ref, loss, scaled, grad)


def text_grad(grads, near_images, far_grads, far_images, at):
    return lax.dot_general(
        grads[:, at], near_images[...], (((0,), (0,)), ((), ())), preferred_element_type=F32
    ) + lax.dot_general(
        far_grads[:, at], far_images[...], (((0,), (0,)), ((), ())), preferred_element_type=F32
    )


def far_kernel(scalars, top_i, bot_i, texts, near_sums, images, grads, sums_ref):
    half = top_i.shape[0]
    rows = 2 * half
    scale, bias = scalars[0], scalars[1]
    images[pl.ds(0, half), :] = top_i[...]
    images[pl.ds(half, half), :] = bot_i[...]
    loss = scaled = grad = jnp.zeros((8, rows), F32)

    def sim_of(t):
        return sim_tile(images[...], texts[pl.ds(t * rows, rows), :])

    sim = sim_of(0)
    for t in range(4):
        sim_next = sim_of(t + 1) if t < 3 else None
        grad_q, loss_now, scaled_now, grad_now = pair_tile(sim, scale, bias, False)
        grads[:, pl.ds(t * rows, rows)] = grad_q
        loss, scaled, grad = loss + loss_now, scaled + scaled_now, grad + grad_now
        sim = sim_next
    write_sums(sums_ref, loss, scaled, grad)
    sums_ref[...] += near_sums[...]


def far_grad_kernel(
    far_images, far_grads, near_images, texts, near_grads, far_out, y_out, mate_out
):
    rows = far_images.shape[0]
    far_out[...] = jnp.dot(
        far_grads[...], texts[...], preferred_element_type=F32
    ).astype(BF16)
    for t, out in ((3, mate_out.at[pl.ds(0, rows)]), (1, mate_out.at[pl.ds(rows, rows)]), (2, y_out)):
        out[...] = text_grad(
            near_grads, near_images, far_grads, far_images, pl.ds(t * rows, rows)
        ).astype(out.dtype)


def text_kernel(near_grads, far_grads, near_images, far_images, sums, own_out, sums_out):
    rows = far_images.shape[0]
    own_out[...] = text_grad(near_grads, near_images, far_grads, far_images, pl.ds(0, rows))
    sums_out[...] = sums[...]


def near_part(scalars, images, texts):
    rows, width = texts[0].shape
    shape = jax.ShapeDtypeStruct
    return pl.pallas_call(
        near_kernel,
        out_shape=(
            shape((rows, width), F32),
            shape((rows, width), BF16),
            shape((rows, width), BF16),
            shape((3 * rows, width), BF16),
            shape((4 * rows, width), BF16),
            shape((3 * rows, 4 * rows), BF16),
            shape((8, 128), F32),
        ),
        in_specs=[SMEM] + [VMEM] * 7,
        out_specs=(VMEM,) * 7,
        compiler_params=params(16),
        cost_estimate=pl.CostEstimate(
            flops=8 * 2 * 2 * 12 * rows * rows * width,
            bytes_accessed=24 * rows * width,
            transcendentals=3 * 12 * rows * rows,
        ),
        name="near",
    )(scalars, *images, *texts)


def far_part(scalars, far_images, texts, near_sums):
    half, width = far_images[0].shape
    rows = 2 * half
    shape = jax.ShapeDtypeStruct
    return pl.pallas_call(
        far_kernel,
        out_shape=(
            shape((rows, width), BF16), shape((rows, 4 * rows), BF16), shape((8, 128), F32)
        ),
        in_specs=[SMEM] + [VMEM] * 4,
        out_specs=(VMEM,) * 3,
        compiler_params=params(16),
        cost_estimate=pl.CostEstimate(
            flops=rows * rows * width, bytes_accessed=2 * rows * width, transcendentals=rows * rows
        ),
        name="far",
    )(scalars, *far_images, texts, near_sums)


def far_grad_part(far_images, far_grads, near_images, texts, near_grads):
    rows, width = far_images.shape
    shape = jax.ShapeDtypeStruct
    return pl.pallas_call(
        far_grad_kernel,
        out_shape=(
            shape((rows, width), BF16), shape((rows, width), F32), shape((2 * rows, width), BF16)
        ),
        in_specs=[VMEM] * 5,
        out_specs=(VMEM,) * 3,
        compiler_params=params(16),
        cost_estimate=pl.CostEstimate(
            flops=rows * rows * width, bytes_accessed=2 * rows * width, transcendentals=0
        ),
        name="far_grad",
    )(far_images, far_grads, near_images, texts, near_grads)


def text_part(near_grads, far_grads, near_images, far_images, sums):
    rows, width = far_images.shape
    shape = jax.ShapeDtypeStruct
    return pl.pallas_call(
        text_kernel,
        out_shape=(shape((rows, width), F32), shape(sums.shape, F32)),
        in_specs=[VMEM] * 5,
        out_specs=(VMEM,) * 2,
        compiler_params=params(16),
        cost_estimate=pl.CostEstimate(
            flops=64 * rows * rows * width, bytes_accessed=rows * width, transcendentals=0
        ),
        name="text",
    )(near_grads, far_grads, near_images, far_images, sums)


def relay_y_kernel(own, passing, sums, arrived, out, sums_out):
    rows = own.shape[0]
    out[...] = (own[...] + passing[:rows, :].astype(F32)).astype(BF16)
    sums_out[...] = sums[...] + arrived[...]


def relay_y(own, passing, sums, arrived):
    return pl.pallas_call(
        relay_y_kernel,
        out_shape=(
            jax.ShapeDtypeStruct(own.shape, BF16), jax.ShapeDtypeStruct(sums.shape, F32)
        ),
        in_specs=[VMEM] * 4,
        out_specs=(VMEM,) * 2,
        compiler_params=params(16),
        cost_estimate=pl.CostEstimate(flops=own.size, bytes_accessed=own.size, transcendentals=0),
        name="relay_y",
    )(own, passing, sums, arrived)


def backnorm(emb, upstream, scale):
    hat, inverse = unit_rows(emb)
    along = jnp.sum(hat * upstream, axis=1, keepdims=True)
    return (scale * inverse) * (upstream - hat * along)


def write_rows(out, values, slots, sems, i):
    rows = values.shape[0]
    at = pl.ds(i * rows, rows)
    slots[at, :] = values
    copy = pltpu.make_async_copy(slots.at[at], out.at[at], sems.at[i])
    copy.start()
    return copy


def end_kernel(scalars, emb, *refs):
    *parts, sums, out, sums_out, slots, sems = refs
    step = emb.shape[0] // 4
    copies = []
    for i in range(4):
        at = pl.ds(i * step, step)
        upstream = parts[0][at, :]
        for part in parts[1:]:
            skip = part.shape[0] - 4 * step
            upstream += part[pl.ds(skip + i * step, step), :].astype(F32)
        copies.append(write_rows(out, backnorm(emb[at, :], upstream, scalars[0]), slots, sems, i))
    sums_out[...] = sums[...]
    for copy in copies:
        copy.wait()


def end_part(name, scalars, emb, *parts):
    rows, width = emb.shape
    sums = parts[-1]
    return pl.pallas_call(
        end_kernel,
        out_shape=(
            jax.ShapeDtypeStruct((rows, width), F32), jax.ShapeDtypeStruct(sums.shape, F32)
        ),
        in_specs=[SMEM] + [VMEM] * (1 + len(parts)),
        out_specs=(HBM, VMEM),
        scratch_shapes=[pltpu.VMEM((rows, width), F32), pltpu.SemaphoreType.DMA((4,))],
        compiler_params=params(24),
        cost_estimate=pl.CostEstimate(
            flops=8 * rows * width, bytes_accessed=rows * width, transcendentals=rows
        ),
        name=name,
    )(scalars, emb, *parts)


def shards(image_emb, text_emb, log_scale, bias):
    rows = image_emb.shape[0]
    blocks = lax.axis_size("blk")
    groups = lax.axis_size("group")
    ahead = [(i, (i + 4) % blocks) for i in range(blocks)]
    back = [(i, (i - 4) % blocks) for i in range(blocks)]
    across_y = [(i, i ^ 2) for i in range(blocks)]
    across_core = [(i, i ^ 1) for i in range(blocks)]

    def send(value, perm):
        return lax.ppermute(value, "blk", perm)

    scale = jnp.exp(log_scale)
    scalars = jnp.stack([scale, bias])
    own_i, token = normalize(image_emb)
    own_t, _ = normalize(text_emb, token)
    left_i = send(own_i, ahead)
    right_i = send(own_i, back)
    y_t = send(own_t, across_y)
    core_t = send(own_t, across_core)
    yc_t = send(y_t, across_core)
    top_i = send(cut(left_i, 0), ahead)
    bot_i = send(cut(right_i, rows // 2), back)

    own_p, left_p, right_p, near_images, texts, near_grads, near_sums = near_part(
        scalars, (own_i, left_i, right_i), (own_t, core_t, y_t, yc_t)
    )
    from_left = send(right_p, ahead)
    from_right = send(left_p, back)
    far_images, far_grads, sums = far_part(scalars, (top_i, bot_i), texts, near_sums)

    def pair(value, axis, k):
        return lax.ppermute(value, axis, [(i, i ^ k) for i in range(lax.axis_size(axis))])

    sums_1 = sums + pair(sums, "blk", 1)
    far_p, y_q, to_mate = far_grad_part(far_images, far_grads, near_images, texts, near_grads)
    from_far = send(far_p, [(i, (i + 8) % blocks) for i in range(blocks)])
    from_core = send(to_mate, across_core)
    y_sum, sums_2 = relay_y(y_q, from_core, sums_1, pair(sums_1, "blk", 2))
    from_y = send(y_sum, across_y)
    own_q, sums_2 = text_part(near_grads, far_grads, near_images, far_images, sums_2)

    def steps(_, value):
        for axis, k in STEPS:
            value = value + pair(value, axis, k)
        return value

    sums_8 = lax.fori_loop(0, (scale > 0.0).astype(jnp.int32), steps, sums_2)
    grad_text, sums_8 = end_part(
        "text_end", scalars, text_emb, own_q, from_core, from_y, sums_8
    )
    grad_image, sums_8 = end_part(
        "image_end", scalars, image_emb, own_p, from_left, from_right, from_far, sums_8
    )
    totals = sums_8[0] / (rows * blocks * groups)
    return (totals[0], grad_image, grad_text, totals[1], totals[2])


def solution(mesh):
    in_specs = (P(("blk", "group"), None), P(("blk", "group"), None), P(), P())
    out_specs = (P(), P(("blk", "group"), None), P(("blk", "group"), None), P(), P())
    return jax.shard_map(shards, mesh=mesh, in_specs=in_specs, out_specs=out_specs, check_vma=False)
```

```python
import jax
import jax.numpy as jnp
from jax import lax
from jax.experimental import pallas as pl
from jax.experimental.pallas import tpu as pltpu
from jax.sharding import PartitionSpec as P

F32 = jnp.float32
BATCH = 65536
IMAGE_COST = 512
TEXT_COST = 16
STEPS = (("group", 1), ("group", 2), ("group", 4), ("group", 8), ("blk", 4), ("blk", 8))
BF16 = jnp.bfloat16
HBM = pl.BlockSpec(memory_space=pltpu.HBM)
VMEM = pl.BlockSpec(memory_space=pltpu.VMEM)
SMEM = pl.BlockSpec(memory_space=pltpu.SMEM)


def params(mib):
    return pltpu.CompilerParams(vmem_limit_bytes=mib * 1024 * 1024)


def unit_rows(emb):
    inverse = lax.rsqrt(jnp.sum(emb * emb, axis=1, keepdims=True) + 1e-06)
    return emb * inverse, inverse


def normalize_kernel(emb_ref, *refs):
    norm_ref, token = refs[-2:]
    norm_ref[...] = unit_rows(emb_ref[...])[0].astype(BF16)
    token[...] = jnp.zeros(token.shape, F32)


def normalize(emb, *after):
    rows, width = emb.shape
    return pl.pallas_call(
        normalize_kernel,
        out_shape=(
            jax.ShapeDtypeStruct((rows, width), BF16), jax.ShapeDtypeStruct((8, 128), F32)
        ),
        in_specs=[VMEM] * (1 + len(after)),
        out_specs=(VMEM,) * 2,
        compiler_params=params(16),
        cost_estimate=pl.CostEstimate(
            flops=4 * rows * width, bytes_accessed=6 * rows * width, transcendentals=rows
        ),
        name="normalize",
    )(emb, *after)


def cut(block, at):
    rows, width = block.shape

    def kernel(block_ref, out_ref):
        out_ref[...] = block_ref[pl.ds(at, rows // 2), :]

    return pl.pallas_call(
        kernel,
        out_shape=jax.ShapeDtypeStruct((rows // 2, width), block.dtype),
        in_specs=[VMEM],
        out_specs=VMEM,
        compiler_params=params(16),
        cost_estimate=pl.CostEstimate(flops=0, bytes_accessed=rows * width, transcendentals=0),
        name="cut",
    )(block)


def sim_tile(image_rows, text_rows):
    return lax.dot_general(
        image_rows, text_rows, (((1,), (1,)), ((), ())), preferred_element_type=F32
    )


def pair_tile(sim, scale, bias, diagonal):
    scaled = scale * sim
    logits = scaled + bias
    rows, columns = sim.shape
    if diagonal:
        positive = lax.broadcasted_iota(jnp.int32, (rows, columns), 0) == (
            lax.broadcasted_iota(jnp.int32, (rows, columns), 1)
        )
        logits = jnp.where(positive, -logits, logits)
    odds = jnp.exp(logits)
    total = 1.0 + odds
    inverse = pl.reciprocal(total, approx=True)
    inverse = inverse * (2.0 - total * inverse)
    grad = odds * inverse
    if diagonal:
        grad = jnp.where(positive, -grad, grad)
    lost = (odds - (total - 1.0)) * inverse
    part = rows // 8
    product = total[:part]
    for i in range(1, 8):
        product = product * total[i * part : (i + 1) * part]

    def fold(values):
        return jnp.sum(values.reshape(values.shape[0] // 8, 8, columns), axis=0)

    loss = fold(jnp.log(product)) + fold(lost)
    return grad.astype(BF16), loss, fold(grad * scaled), fold(grad)


def write_sums(sums_ref, loss, scaled, grad):
    column = lax.broadcasted_iota(jnp.int32, sums_ref.shape, 1)
    sums_ref[...] = jnp.where(
        column == 0, jnp.sum(loss), jnp.where(column == 1, jnp.sum(scaled), jnp.sum(grad))
    )


def near_kernel(
    log_scale, bias, own_i, left_i, right_i, own_t, core_t, y_t, yc_t,
    own_out, left_out, right_out, images, texts, grads, sums_ref, passes_ref,
):
    rows = own_i.shape[0]
    scale, bias = jnp.exp(jnp.full((1, rows), log_scale[0])), bias[0]
    for i, src in enumerate((own_i, left_i, right_i)):
        images[pl.ds(i * rows, rows), :] = src[...]
    for i, src in enumerate((own_t, core_t, y_t, yc_t)):
        texts[pl.ds(i * rows, rows), :] = src[...]
    loss = scaled = grad = jnp.zeros((8, rows), F32)
    tiles = [(b, t) for b in range(3) for t in range(4)]

    def sim_of(k):
        b, t = tiles[k]
        return sim_tile(images[pl.ds(b * rows, rows), :], texts[pl.ds(t * rows, rows), :])

    sim = sim_of(0)
    for k, (b, t) in enumerate(tiles):
        sim_next = sim_of(k + 1) if k + 1 < len(tiles) else None
        grad_q, loss_now, scaled_now, grad_now = pair_tile(sim, scale, bias, k == 0)
        grads[pl.ds(b * rows, rows), pl.ds(t * rows, rows)] = grad_q
        loss, scaled, grad = loss + loss_now, scaled + scaled_now, grad + grad_now
        sim = sim_next
        if t == 3:
            partial = jnp.dot(
                grads[pl.ds(b * rows, rows), :], texts[...], preferred_element_type=F32
            )
            out = (own_out, left_out, right_out)[b]
            out[...] = partial.astype(out.dtype)
    write_sums(sums_ref, loss, scaled, grad)
    passes_ref[0] = 1


def text_grad(grads, near_images, far_grads, far_images, at):
    return lax.dot_general(
        grads[:, at], near_images[...], (((0,), (0,)), ((), ())), preferred_element_type=F32
    ) + lax.dot_general(
        far_grads[:, at], far_images[...], (((0,), (0,)), ((), ())), preferred_element_type=F32
    )


def far_kernel(log_scale, bias, top_i, bot_i, texts, near_sums, images, grads, sums_ref):
    half = top_i.shape[0]
    rows = 2 * half
    scale, bias = jnp.exp(jnp.full((1, rows), log_scale[0])), bias[0]
    images[pl.ds(0, half), :] = top_i[...]
    images[pl.ds(half, half), :] = bot_i[...]
    loss = scaled = grad = jnp.zeros((8, rows), F32)

    def sim_of(t):
        return sim_tile(images[...], texts[pl.ds(t * rows, rows), :])

    sim = sim_of(0)
    for t in range(4):
        sim_next = sim_of(t + 1) if t < 3 else None
        grad_q, loss_now, scaled_now, grad_now = pair_tile(sim, scale, bias, False)
        grads[:, pl.ds(t * rows, rows)] = grad_q
        loss, scaled, grad = loss + loss_now, scaled + scaled_now, grad + grad_now
        sim = sim_next
    write_sums(sums_ref, loss, scaled, grad)
    sums_ref[...] += near_sums[...]


def far_grad_kernel(
    far_images, far_grads, near_images, texts, near_grads, far_out, y_out, mate_out
):
    rows = far_images.shape[0]
    far_out[...] = jnp.dot(
        far_grads[...], texts[...], preferred_element_type=F32
    ).astype(BF16)
    for t, out in ((3, mate_out.at[pl.ds(0, rows)]), (1, mate_out.at[pl.ds(rows, rows)]), (2, y_out)):
        out[...] = text_grad(
            near_grads, near_images, far_grads, far_images, pl.ds(t * rows, rows)
        ).astype(out.dtype)


def text_kernel(near_grads, far_grads, near_images, far_images, sums, own_out, sums_out):
    rows = far_images.shape[0]
    own_out[...] = text_grad(near_grads, near_images, far_grads, far_images, pl.ds(0, rows))
    sums_out[...] = sums[...]


def near_part(scalars, images, texts):
    rows, width = texts[0].shape
    shape = jax.ShapeDtypeStruct
    return pl.pallas_call(
        near_kernel,
        out_shape=(
            shape((rows, width), F32),
            shape((rows, width), BF16),
            shape((rows, width), BF16),
            shape((3 * rows, width), BF16),
            shape((4 * rows, width), BF16),
            shape((3 * rows, 4 * rows), BF16),
            shape((8, 128), F32),
            shape((1,), jnp.int32),
        ),
        in_specs=[SMEM] * 2 + [VMEM] * 7,
        out_specs=(VMEM,) * 7 + (SMEM,),
        compiler_params=params(16),
        cost_estimate=pl.CostEstimate(
            flops=8 * 2 * 2 * 12 * rows * rows * width,
            bytes_accessed=24 * rows * width,
            transcendentals=3 * 12 * rows * rows,
        ),
        name="near",
    )(*scalars, *images, *texts)


def far_part(scalars, far_images, texts, near_sums):
    half, width = far_images[0].shape
    rows = 2 * half
    shape = jax.ShapeDtypeStruct
    return pl.pallas_call(
        far_kernel,
        out_shape=(
            shape((rows, width), BF16), shape((rows, 4 * rows), BF16), shape((8, 128), F32)
        ),
        in_specs=[SMEM] * 2 + [VMEM] * 4,
        out_specs=(VMEM,) * 3,
        compiler_params=params(16),
        cost_estimate=pl.CostEstimate(
            flops=rows * rows * width, bytes_accessed=2 * rows * width, transcendentals=rows * rows
        ),
        name="far",
    )(*scalars, *far_images, texts, near_sums)


def far_grad_part(far_images, far_grads, near_images, texts, near_grads):
    rows, width = far_images.shape
    shape = jax.ShapeDtypeStruct
    return pl.pallas_call(
        far_grad_kernel,
        out_shape=(
            shape((rows, width), BF16), shape((rows, width), F32), shape((2 * rows, width), BF16)
        ),
        in_specs=[VMEM] * 5,
        out_specs=(VMEM,) * 3,
        compiler_params=params(16),
        cost_estimate=pl.CostEstimate(
            flops=rows * rows * width, bytes_accessed=2 * rows * width, transcendentals=0
        ),
        name="far_grad",
    )(far_images, far_grads, near_images, texts, near_grads)


def text_part(near_grads, far_grads, near_images, far_images, sums):
    rows, width = far_images.shape
    shape = jax.ShapeDtypeStruct
    return pl.pallas_call(
        text_kernel,
        out_shape=(shape((rows, width), F32), shape(sums.shape, F32)),
        in_specs=[VMEM] * 5,
        out_specs=(VMEM,) * 2,
        compiler_params=params(16),
        cost_estimate=pl.CostEstimate(
            flops=TEXT_COST * rows * rows * width, bytes_accessed=rows * width, transcendentals=0
        ),
        name="text",
    )(near_grads, far_grads, near_images, far_images, sums)


def add_kernel(*refs):
    *parts, out = refs
    out[...] = sum((part[...] for part in parts[1:]), parts[0][...])


def add(*parts):
    one = parts[0]
    return pl.pallas_call(
        add_kernel,
        out_shape=jax.ShapeDtypeStruct(one.shape, F32),
        in_specs=[VMEM] * len(parts),
        out_specs=VMEM,
        compiler_params=params(16),
        cost_estimate=pl.CostEstimate(flops=one.size, bytes_accessed=one.size, transcendentals=0),
        name="add",
    )(*parts)


def relay_y_kernel(own, passing, sums, arrived, out, sums_out):
    rows = own.shape[0]
    out[...] = (own[...] + passing[:rows, :].astype(F32)).astype(BF16)
    sums_out[...] = sums[...] + arrived[...]


def relay_y(own, passing, sums, arrived):
    return pl.pallas_call(
        relay_y_kernel,
        out_shape=(
            jax.ShapeDtypeStruct(own.shape, BF16), jax.ShapeDtypeStruct(sums.shape, F32)
        ),
        in_specs=[VMEM] * 4,
        out_specs=(VMEM,) * 2,
        compiler_params=params(16),
        cost_estimate=pl.CostEstimate(flops=own.size, bytes_accessed=own.size, transcendentals=0),
        name="relay_y",
    )(own, passing, sums, arrived)


def backnorm(emb, upstream, scale):
    hat, inverse = unit_rows(emb)
    along = jnp.sum(hat * upstream, axis=1, keepdims=True)
    return (scale * inverse) * (upstream - hat * along)


def write_rows(out, values, slots, sems, i):
    rows = values.shape[0]
    at = pl.ds(i * rows, rows)
    slots[at, :] = values
    copy = pltpu.make_async_copy(slots.at[at], out.at[at], sems.at[i])
    copy.start()
    return copy


def end_kernel(log_scale, emb, *refs):
    *parts, sums, out, sums_out, slots, sems = refs
    scale = jnp.exp(jnp.full((1, 1), log_scale[0]))
    step = emb.shape[0] // 4
    copies = []
    for i in range(4):
        at = pl.ds(i * step, step)
        upstream = parts[0][at, :]
        for part in parts[1:]:
            skip = part.shape[0] - 4 * step
            upstream += part[pl.ds(skip + i * step, step), :].astype(F32)
        copies.append(write_rows(out, backnorm(emb[at, :], upstream, scale), slots, sems, i))
    if sums_out.shape == sums.shape:
        sums_out[...] = sums[...]
    else:
        for i in range(3):
            sums_out[i] = jnp.sum(sums[0:1, i : i + 1]) * (1.0 / BATCH)
    for copy in copies:
        copy.wait()


def end_part(name, cost, sums_shape, log_scale, emb, *parts):
    rows, width = emb.shape
    return pl.pallas_call(
        end_kernel,
        out_shape=(
            jax.ShapeDtypeStruct((rows, width), F32), jax.ShapeDtypeStruct(sums_shape, F32)
        ),
        in_specs=[SMEM] + [VMEM] * (1 + len(parts)),
        out_specs=(HBM, VMEM if len(sums_shape) == 2 else SMEM),
        scratch_shapes=[pltpu.VMEM((rows, width), F32), pltpu.SemaphoreType.DMA((4,))],
        compiler_params=params(24),
        cost_estimate=pl.CostEstimate(
            flops=cost * rows * width, bytes_accessed=rows * width, transcendentals=rows
        ),
        name=name,
    )(log_scale, emb, *parts)


def shards(image_emb, text_emb, log_scale, bias):
    rows = image_emb.shape[0]
    blocks = lax.axis_size("blk")
    ahead = [(i, (i + 4) % blocks) for i in range(blocks)]
    back = [(i, (i - 4) % blocks) for i in range(blocks)]
    across_y = [(i, i ^ 2) for i in range(blocks)]
    across_core = [(i, i ^ 1) for i in range(blocks)]

    def send(value, perm):
        return lax.ppermute(value, "blk", perm)

    scalars = log_scale.reshape(1), bias.reshape(1)
    own_i, token = normalize(image_emb)
    own_t, _ = normalize(text_emb, token)
    left_i = send(own_i, ahead)
    right_i = send(own_i, back)
    y_t = send(own_t, across_y)
    core_t = send(own_t, across_core)
    yc_t = send(y_t, across_core)
    top_i = send(cut(left_i, 0), ahead)
    bot_i = send(cut(right_i, rows // 2), back)

    own_p, left_p, right_p, near_images, texts, near_grads, near_sums, passes = near_part(
        scalars, (own_i, left_i, right_i), (own_t, core_t, y_t, yc_t)
    )
    from_left = send(right_p, ahead)
    from_right = send(left_p, back)
    far_images, far_grads, sums = far_part(scalars, (top_i, bot_i), texts, near_sums)

    def pair(value, axis, k):
        return lax.ppermute(value, axis, [(i, i ^ k) for i in range(lax.axis_size(axis))])

    sums_1 = add(sums, pair(sums, "blk", 1))
    far_p, y_q, to_mate = far_grad_part(far_images, far_grads, near_images, texts, near_grads)
    from_far = send(far_p, [(i, (i + 8) % blocks) for i in range(blocks)])
    from_core = send(to_mate, across_core)
    y_sum, sums_2 = relay_y(y_q, from_core, sums_1, pair(sums_1, "blk", 2))
    from_y = send(y_sum, across_y)
    own_q, sums_2 = text_part(near_grads, far_grads, near_images, far_images, sums_2)

    def steps(carry):
        left, value = carry
        for axis, k in STEPS:
            value = value + pair(value, axis, k)
        return left - 1, value

    _, sums_8 = lax.while_loop(lambda carry: carry[0] > 0, steps, (passes[0], sums_2))
    grad_image, sums_8 = end_part(
        "image_end", IMAGE_COST, (8, 128), scalars[0], image_emb,
        own_p, from_left, from_right, from_far, add(sums_8),
    )
    grad_text, totals = end_part(
        "text_end", 8, (3,), scalars[0], text_emb, own_q, from_core, from_y, sums_8
    )
    return (totals[0], grad_image, grad_text, totals[1], totals[2])


def solution(mesh):
    in_specs = (P(("blk", "group"), None), P(("blk", "group"), None), P(), P())
    out_specs = (P(), P(("blk", "group"), None), P(("blk", "group"), None), P(), P())
    return jax.shard_map(shards, mesh=mesh, in_specs=in_specs, out_specs=out_specs, check_vma=False)
```

```python
import jax
import jax.numpy as jnp
from jax import lax
from jax.experimental import pallas as pl
from jax.experimental.pallas import tpu as pltpu
from jax.sharding import PartitionSpec as P

F32 = jnp.float32
BATCH = 65536
TEXT_COST = 16
STEPS = (("group", 1), ("group", 2), ("group", 4), ("group", 8))
BF16 = jnp.bfloat16
HBM = pl.BlockSpec(memory_space=pltpu.HBM)
VMEM = pl.BlockSpec(memory_space=pltpu.VMEM)
SMEM = pl.BlockSpec(memory_space=pltpu.SMEM)


def params(mib):
    return pltpu.CompilerParams(vmem_limit_bytes=mib * 1024 * 1024)


def unit_rows(emb):
    inverse = lax.rsqrt(jnp.sum(emb * emb, axis=1, keepdims=True) + 1e-06)
    return emb * inverse, inverse


def normalize_kernel(emb_ref, *refs):
    norm_ref, token = refs[-2:]
    norm_ref[...] = unit_rows(emb_ref[...])[0].astype(BF16)
    token[...] = jnp.zeros(token.shape, F32)


def normalize(emb, *after):
    rows, width = emb.shape
    return pl.pallas_call(
        normalize_kernel,
        out_shape=(
            jax.ShapeDtypeStruct((rows, width), BF16), jax.ShapeDtypeStruct((8, 128), F32)
        ),
        in_specs=[VMEM] * (1 + len(after)),
        out_specs=(VMEM,) * 2,
        compiler_params=params(16),
        cost_estimate=pl.CostEstimate(
            flops=4 * rows * width, bytes_accessed=6 * rows * width, transcendentals=rows
        ),
        name="normalize",
    )(emb, *after)


def cut(block, at):
    rows, width = block.shape

    def kernel(block_ref, out_ref):
        out_ref[...] = block_ref[pl.ds(at, rows // 2), :]

    return pl.pallas_call(
        kernel,
        out_shape=jax.ShapeDtypeStruct((rows // 2, width), block.dtype),
        in_specs=[VMEM],
        out_specs=VMEM,
        compiler_params=params(16),
        cost_estimate=pl.CostEstimate(flops=0, bytes_accessed=rows * width, transcendentals=0),
        name="cut",
    )(block)


def sim_tile(image_rows, text_rows):
    return lax.dot_general(
        image_rows, text_rows, (((1,), (1,)), ((), ())), preferred_element_type=F32
    )


def pair_tile(sim, scale, bias, diagonal):
    scaled = scale * sim
    logits = scaled + bias
    rows, columns = sim.shape
    if diagonal:
        positive = lax.broadcasted_iota(jnp.int32, (rows, columns), 0) == (
            lax.broadcasted_iota(jnp.int32, (rows, columns), 1)
        )
        logits = jnp.where(positive, -logits, logits)
    odds = jnp.exp(logits)
    total = 1.0 + odds
    inverse = pl.reciprocal(total, approx=True)
    inverse = inverse * (2.0 - total * inverse)
    grad = odds * inverse
    if diagonal:
        grad = jnp.where(positive, -grad, grad)
    lost = (odds - (total - 1.0)) * inverse
    part = rows // 8
    product = total[:part]
    for i in range(1, 8):
        product = product * total[i * part : (i + 1) * part]

    def fold(values):
        return jnp.sum(values.reshape(values.shape[0] // 8, 8, columns), axis=0)

    loss = fold(jnp.log(product)) + fold(lost)
    return grad.astype(BF16), loss, fold(grad * scaled), fold(grad)


def write_sums(sums_ref, loss, scaled, grad):
    column = lax.broadcasted_iota(jnp.int32, sums_ref.shape, 1)
    sums_ref[...] = jnp.where(
        column == 0, jnp.sum(loss), jnp.where(column == 1, jnp.sum(scaled), jnp.sum(grad))
    )


def near_kernel(
    log_scale, bias, own_i, left_i, right_i, own_t, core_t, y_t, yc_t,
    own_out, left_out, right_out, images, texts, grads, sums_ref, passes_ref,
):
    rows = own_i.shape[0]
    scale, bias = jnp.exp(jnp.full((1, rows), log_scale[0])), bias[0]
    for i, src in enumerate((own_i, left_i, right_i)):
        images[pl.ds(i * rows, rows), :] = src[...]
    for i, src in enumerate((own_t, core_t, y_t, yc_t)):
        texts[pl.ds(i * rows, rows), :] = src[...]
    loss = scaled = grad = jnp.zeros((8, rows), F32)
    tiles = [(b, t) for b in range(3) for t in range(4)]

    def sim_of(k):
        b, t = tiles[k]
        return sim_tile(images[pl.ds(b * rows, rows), :], texts[pl.ds(t * rows, rows), :])

    sim = sim_of(0)
    for k, (b, t) in enumerate(tiles):
        sim_next = sim_of(k + 1) if k + 1 < len(tiles) else None
        grad_q, loss_now, scaled_now, grad_now = pair_tile(sim, scale, bias, k == 0)
        grads[pl.ds(b * rows, rows), pl.ds(t * rows, rows)] = grad_q
        loss, scaled, grad = loss + loss_now, scaled + scaled_now, grad + grad_now
        sim = sim_next
        if t == 3:
            partial = jnp.dot(
                grads[pl.ds(b * rows, rows), :], texts[...], preferred_element_type=F32
            )
            out = (own_out, left_out, right_out)[b]
            out[...] = partial.astype(out.dtype)
    write_sums(sums_ref, loss, scaled, grad)
    passes_ref[0] = 1


def text_grad(grads, near_images, far_grads, far_images, at):
    return lax.dot_general(
        grads[:, at], near_images[...], (((0,), (0,)), ((), ())), preferred_element_type=F32
    ) + lax.dot_general(
        far_grads[:, at], far_images[...], (((0,), (0,)), ((), ())), preferred_element_type=F32
    )


def far_kernel(log_scale, bias, top_i, bot_i, texts, near_sums, images, grads, sums_ref):
    half = top_i.shape[0]
    rows = 2 * half
    scale, bias = jnp.exp(jnp.full((1, rows), log_scale[0])), bias[0]
    images[pl.ds(0, half), :] = top_i[...]
    images[pl.ds(half, half), :] = bot_i[...]
    loss = scaled = grad = jnp.zeros((8, rows), F32)

    def sim_of(t):
        return sim_tile(images[...], texts[pl.ds(t * rows, rows), :])

    sim = sim_of(0)
    for t in range(4):
        sim_next = sim_of(t + 1) if t < 3 else None
        grad_q, loss_now, scaled_now, grad_now = pair_tile(sim, scale, bias, False)
        grads[:, pl.ds(t * rows, rows)] = grad_q
        loss, scaled, grad = loss + loss_now, scaled + scaled_now, grad + grad_now
        sim = sim_next
    write_sums(sums_ref, loss, scaled, grad)
    sums_ref[...] += near_sums[...]


def far_grad_kernel(
    far_images, far_grads, near_images, texts, near_grads, sums, far_out, y_out, mate_out, sums_out
):
    rows = far_images.shape[0]
    far_out[...] = jnp.dot(
        far_grads[...], texts[...], preferred_element_type=F32
    ).astype(BF16)
    for t, out in ((3, mate_out.at[pl.ds(0, rows)]), (1, mate_out.at[pl.ds(rows, rows)]), (2, y_out)):
        out[...] = text_grad(
            near_grads, near_images, far_grads, far_images, pl.ds(t * rows, rows)
        ).astype(out.dtype)
    sums_out[...] = sums[...]


def text_kernel(near_grads, far_grads, near_images, far_images, sums, own_out, sums_out):
    rows = far_images.shape[0]
    own_out[...] = text_grad(near_grads, near_images, far_grads, far_images, pl.ds(0, rows))
    sums_out[...] = sums[...]


def near_part(scalars, images, texts):
    rows, width = texts[0].shape
    shape = jax.ShapeDtypeStruct
    return pl.pallas_call(
        near_kernel,
        out_shape=(
            shape((rows, width), F32),
            shape((rows, width), BF16),
            shape((rows, width), BF16),
            shape((3 * rows, width), BF16),
            shape((4 * rows, width), BF16),
            shape((3 * rows, 4 * rows), BF16),
            shape((8, 128), F32),
            shape((1,), jnp.int32),
        ),
        in_specs=[SMEM] * 2 + [VMEM] * 7,
        out_specs=(VMEM,) * 7 + (SMEM,),
        compiler_params=params(16),
        cost_estimate=pl.CostEstimate(
            flops=8 * 2 * 2 * 12 * rows * rows * width,
            bytes_accessed=24 * rows * width,
            transcendentals=3 * 12 * rows * rows,
        ),
        name="near",
    )(*scalars, *images, *texts)


def far_part(scalars, far_images, texts, near_sums):
    half, width = far_images[0].shape
    rows = 2 * half
    shape = jax.ShapeDtypeStruct
    return pl.pallas_call(
        far_kernel,
        out_shape=(
            shape((rows, width), BF16), shape((rows, 4 * rows), BF16), shape((8, 128), F32)
        ),
        in_specs=[SMEM] * 2 + [VMEM] * 4,
        out_specs=(VMEM,) * 3,
        compiler_params=params(16),
        cost_estimate=pl.CostEstimate(
            flops=rows * rows * width, bytes_accessed=2 * rows * width, transcendentals=rows * rows
        ),
        name="far",
    )(*scalars, *far_images, texts, near_sums)


def far_grad_part(far_images, far_grads, near_images, texts, near_grads, sums):
    rows, width = far_images.shape
    shape = jax.ShapeDtypeStruct
    return pl.pallas_call(
        far_grad_kernel,
        out_shape=(
            shape((rows, width), BF16), shape((rows, width), F32), shape((2 * rows, width), BF16),
            shape(sums.shape, F32),
        ),
        in_specs=[VMEM] * 6,
        out_specs=(VMEM,) * 4,
        compiler_params=params(16),
        cost_estimate=pl.CostEstimate(
            flops=rows * rows * width, bytes_accessed=2 * rows * width, transcendentals=0
        ),
        name="far_grad",
    )(far_images, far_grads, near_images, texts, near_grads, sums)


def text_part(near_grads, far_grads, near_images, far_images, sums):
    rows, width = far_images.shape
    shape = jax.ShapeDtypeStruct
    return pl.pallas_call(
        text_kernel,
        out_shape=(shape((rows, width), F32), shape(sums.shape, F32)),
        in_specs=[VMEM] * 5,
        out_specs=(VMEM,) * 2,
        compiler_params=params(16),
        cost_estimate=pl.CostEstimate(
            flops=TEXT_COST * rows * rows * width, bytes_accessed=rows * width, transcendentals=0
        ),
        name="text",
    )(near_grads, far_grads, near_images, far_images, sums)


def add_kernel(*refs):
    *parts, out = refs
    out[...] = sum((part[...] for part in parts[1:]), parts[0][...])


def add(*parts):
    one = parts[0]
    return pl.pallas_call(
        add_kernel,
        out_shape=jax.ShapeDtypeStruct(one.shape, F32),
        in_specs=[VMEM] * len(parts),
        out_specs=VMEM,
        compiler_params=params(16),
        cost_estimate=pl.CostEstimate(flops=one.size, bytes_accessed=one.size, transcendentals=0),
        name="add",
    )(*parts)


def relay_y_kernel(own, passing, sums, arrived, out, sums_out):
    rows = own.shape[0]
    out[...] = (own[...] + passing[:rows, :].astype(F32)).astype(BF16)
    sums_out[...] = sums[...] + arrived[...]


def relay_y(own, passing, sums, arrived):
    return pl.pallas_call(
        relay_y_kernel,
        out_shape=(
            jax.ShapeDtypeStruct(own.shape, BF16), jax.ShapeDtypeStruct(sums.shape, F32)
        ),
        in_specs=[VMEM] * 4,
        out_specs=(VMEM,) * 2,
        compiler_params=params(16),
        cost_estimate=pl.CostEstimate(flops=own.size, bytes_accessed=own.size, transcendentals=0),
        name="relay_y",
    )(own, passing, sums, arrived)


def backnorm(emb, upstream, scale):
    hat, inverse = unit_rows(emb)
    along = jnp.sum(hat * upstream, axis=1, keepdims=True)
    return (scale * inverse) * (upstream - hat * along)


def end_kernel(
    log_scale, text_emb, own_q, from_core, from_y, image_emb, own_p, from_left, from_right, from_far,
    sums, text_out, image_out, sums_out, text_slots, image_slots, sems,
):
    scale = jnp.exp(jnp.full((1, 1), log_scale[0]))
    step = text_emb.shape[0] // 4
    sets = (
        (text_emb, (own_q, from_core, from_y), text_out, text_slots),
        (image_emb, (own_p, from_left, from_right, from_far), image_out, image_slots),
    )
    copies = []
    for emb, parts, out, slots in sets:
        for i in range(4):
            at = pl.ds(i * step, step)
            upstream = parts[0][at, :]
            for part in parts[1:]:
                skip = part.shape[0] - 4 * step
                upstream += part[pl.ds(skip + i * step, step), :].astype(F32)
            slots[at, :] = backnorm(emb[at, :], upstream, scale)
            copy = pltpu.make_async_copy(slots.at[at], out.at[at], sems.at[len(copies)])
            copy.start()
            copies.append(copy)
    sums_out[...] = sums[...]
    for copy in copies:
        copy.wait()


def end_part(log_scale, text_parts, image_parts, sums):
    rows, width = text_parts[0].shape
    shape = jax.ShapeDtypeStruct
    return pl.pallas_call(
        end_kernel,
        out_shape=(shape((rows, width), F32),) * 2 + (shape(sums.shape, F32),),
        in_specs=[SMEM] + [VMEM] * 10,
        out_specs=(HBM, HBM, VMEM),
        scratch_shapes=[
            pltpu.VMEM((rows, width), F32),
            pltpu.VMEM((rows, width), F32),
            pltpu.SemaphoreType.DMA((8,)),
        ],
        compiler_params=params(24),
        cost_estimate=pl.CostEstimate(
            flops=16 * rows * width, bytes_accessed=2 * rows * width, transcendentals=2 * rows
        ),
        name="end",
    )(log_scale, *text_parts, *image_parts, sums)


def totals_kernel(*refs):
    *parts, out = refs
    total = sum((part[...] for part in parts[1:]), parts[0][...])
    for i in range(3):
        out[i] = jnp.sum(total[0:1, i : i + 1]) * (1.0 / BATCH)


def totals_part(*parts):
    return pl.pallas_call(
        totals_kernel,
        out_shape=jax.ShapeDtypeStruct((3,), F32),
        in_specs=[VMEM] * len(parts),
        out_specs=SMEM,
        compiler_params=params(16),
        cost_estimate=pl.CostEstimate(flops=4096, bytes_accessed=4096, transcendentals=0),
        name="totals",
    )(*parts)


def shards(image_emb, text_emb, log_scale, bias):
    rows = image_emb.shape[0]
    blocks = lax.axis_size("blk")
    ahead = [(i, (i + 4) % blocks) for i in range(blocks)]
    back = [(i, (i - 4) % blocks) for i in range(blocks)]
    across_y = [(i, i ^ 2) for i in range(blocks)]
    across_core = [(i, i ^ 1) for i in range(blocks)]

    def send(value, perm):
        return lax.ppermute(value, "blk", perm)

    scalars = log_scale.reshape(1), bias.reshape(1)
    own_i, token = normalize(image_emb)
    own_t, _ = normalize(text_emb, token)
    left_i = send(own_i, ahead)
    right_i = send(own_i, back)
    y_t = send(own_t, across_y)
    core_t = send(own_t, across_core)
    yc_t = send(y_t, across_core)
    top_i = send(cut(left_i, 0), ahead)
    bot_i = send(cut(right_i, rows // 2), back)

    own_p, left_p, right_p, near_images, texts, near_grads, near_sums, passes = near_part(
        scalars, (own_i, left_i, right_i), (own_t, core_t, y_t, yc_t)
    )
    from_left = send(right_p, ahead)
    from_right = send(left_p, back)
    far_images, far_grads, sums = far_part(scalars, (top_i, bot_i), texts, near_sums)

    def pair(value, axis, k):
        return lax.ppermute(value, axis, [(i, i ^ k) for i in range(lax.axis_size(axis))])

    over_core = pair(sums, "blk", 1)
    far_p, y_q, to_mate, sums = far_grad_part(
        far_images, far_grads, near_images, texts, near_grads, sums
    )
    sums_1 = add(sums, over_core)
    from_far = send(far_p, [(i, (i + 8) % blocks) for i in range(blocks)])
    from_core = send(to_mate, across_core)
    y_sum, sums_2 = relay_y(y_q, from_core, sums_1, pair(sums_1, "blk", 2))
    from_y = send(y_sum, across_y)
    own_q, sums_2 = text_part(near_grads, far_grads, near_images, far_images, sums_2)

    def steps(carry):
        left, value = carry
        for axis, k in STEPS:
            value = value + pair(value, axis, k)
        return left - 1, value

    _, sums_6 = lax.while_loop(lambda carry: carry[0] > 0, steps, (passes[0], sums_2))
    over_x = [pair(sums_6, "blk", k) for k in (4, 8, 12)]
    grad_text, grad_image, sums_6 = end_part(
        scalars[0],
        (text_emb, own_q, from_core, from_y),
        (image_emb, own_p, from_left, from_right, from_far),
        sums_6,
    )
    totals = totals_part(sums_6, *over_x)
    return (totals[0], grad_image, grad_text, totals[1], totals[2])


def solution(mesh):
    in_specs = (P(("blk", "group"), None), P(("blk", "group"), None), P(), P())
    out_specs = (P(), P(("blk", "group"), None), P(("blk", "group"), None), P(), P())
    return jax.shard_map(shards, mesh=mesh, in_specs=in_specs, out_specs=out_specs, check_vma=False)
```

```python
import jax
import jax.numpy as jnp
from jax import lax
from jax.experimental import pallas as pl
from jax.experimental.pallas import tpu as pltpu
from jax.sharding import PartitionSpec as P

F32 = jnp.float32
LOG2E = 1.4426950408889634
BATCH = 65536
GATE_COST = 1
STEPS = (("group", 1), ("group", 2), ("group", 4), ("group", 8))
BF16 = jnp.bfloat16
HBM = pl.BlockSpec(memory_space=pltpu.HBM)
VMEM = pl.BlockSpec(memory_space=pltpu.VMEM)
SMEM = pl.BlockSpec(memory_space=pltpu.SMEM)


def params(mib):
    return pltpu.CompilerParams(vmem_limit_bytes=mib * 1024 * 1024)


def unit_rows(emb):
    inverse = lax.rsqrt(jnp.sum(emb * emb, axis=1, keepdims=True) + 1e-06)
    return emb * inverse, inverse


def normalize_kernel(emb_ref, *refs):
    norm_ref, token = refs[-2:]
    norm_ref[...] = unit_rows(emb_ref[...])[0].astype(BF16)
    token[...] = jnp.zeros(token.shape, F32)


def normalize(emb, *after):
    rows, width = emb.shape
    return pl.pallas_call(
        normalize_kernel,
        out_shape=(
            jax.ShapeDtypeStruct((rows, width), BF16), jax.ShapeDtypeStruct((8, 128), F32)
        ),
        in_specs=[VMEM] * (1 + len(after)),
        out_specs=(VMEM,) * 2,
        compiler_params=params(16),
        cost_estimate=pl.CostEstimate(
            flops=4 * rows * width, bytes_accessed=6 * rows * width, transcendentals=rows
        ),
        name="normalize",
    )(emb, *after)


def cut(block, at):
    rows, width = block.shape

    def kernel(block_ref, out_ref):
        out_ref[...] = block_ref[pl.ds(at, rows // 2), :]

    return pl.pallas_call(
        kernel,
        out_shape=jax.ShapeDtypeStruct((rows // 2, width), block.dtype),
        in_specs=[VMEM],
        out_specs=VMEM,
        compiler_params=params(16),
        cost_estimate=pl.CostEstimate(flops=0, bytes_accessed=rows * width, transcendentals=0),
        name="cut",
    )(block)


def sim_tile(image_rows, text_rows):
    return lax.dot_general(
        image_rows, text_rows, (((1,), (1,)), ((), ())), preferred_element_type=F32
    )


def pair_tile(sim, scale, bias, diagonal):
    logits = sim * scale + bias
    rows, columns = sim.shape
    if diagonal:
        positive = lax.broadcasted_iota(jnp.int32, (rows, columns), 0) == (
            lax.broadcasted_iota(jnp.int32, (rows, columns), 1)
        )
        logits = jnp.where(positive, -logits, logits)
    odds = jnp.exp2(logits)
    total = 1.0 + odds
    inverse = pl.reciprocal(total, approx=True)
    inverse = inverse * (2.0 - total * inverse)
    grad = odds * inverse
    if diagonal:
        grad = jnp.where(positive, -grad, grad)
    part = rows // 8
    product = total[:part]
    for i in range(1, 8):
        product = product * total[i * part : (i + 1) * part]

    def fold(values):
        return jnp.sum(values.reshape(values.shape[0] // 8, 8, columns), axis=0)

    return grad.astype(BF16), fold(jnp.log(product)), fold(grad * sim), fold(grad)


def logit_factors(log_scale, bias, columns):
    scale = jnp.exp(jnp.full((1, columns), log_scale[0]))
    return scale, scale * LOG2E, bias[0] * LOG2E


def write_sums(sums_ref, loss, scaled, grad):
    column = lax.broadcasted_iota(jnp.int32, sums_ref.shape, 1)
    sums_ref[...] = jnp.where(
        column == 0, jnp.sum(loss), jnp.where(column == 1, jnp.sum(scaled), jnp.sum(grad))
    )


def near_kernel(
    log_scale, bias, own_i, left_i, right_i, own_t, core_t, y_t, yc_t,
    own_out, left_out, right_out, images, texts, grads, sums_ref, passes_ref,
):
    rows = own_i.shape[0]
    factor, scale, bias = logit_factors(log_scale, bias, rows)
    for i, src in enumerate((own_i, left_i, right_i)):
        images[pl.ds(i * rows, rows), :] = src[...]
    for i, src in enumerate((own_t, core_t, y_t, yc_t)):
        texts[pl.ds(i * rows, rows), :] = src[...]
    loss = scaled = grad = jnp.zeros((8, rows), F32)
    tiles = [(b, t) for b in range(3) for t in range(4)]

    def sim_of(k):
        b, t = tiles[k]
        return sim_tile(images[pl.ds(b * rows, rows), :], texts[pl.ds(t * rows, rows), :])

    sim = sim_of(0)
    for k, (b, t) in enumerate(tiles):
        sim_next = sim_of(k + 1) if k + 1 < len(tiles) else None
        grad_q, loss_now, scaled_now, grad_now = pair_tile(sim, scale, bias, k == 0)
        grads[pl.ds(b * rows, rows), pl.ds(t * rows, rows)] = grad_q
        loss, scaled, grad = loss + loss_now, scaled + scaled_now, grad + grad_now
        sim = sim_next
        if t == 3:
            partial = jnp.dot(
                grads[pl.ds(b * rows, rows), :], texts[...], preferred_element_type=F32
            )
            out = (own_out, left_out, right_out)[b]
            out[...] = partial.astype(out.dtype)
    write_sums(sums_ref, loss, scaled * factor, grad)
    passes_ref[0] = 1


def text_grad(grads, near_images, far_grads, far_images, at):
    return lax.dot_general(
        grads[:, at], near_images[...], (((0,), (0,)), ((), ())), preferred_element_type=F32
    ) + lax.dot_general(
        far_grads[:, at], far_images[...], (((0,), (0,)), ((), ())), preferred_element_type=F32
    )


def far_kernel(log_scale, bias, top_i, bot_i, texts, near_sums, images, grads, sums_ref):
    half = top_i.shape[0]
    rows = 2 * half
    factor, scale, bias = logit_factors(log_scale, bias, rows)
    images[pl.ds(0, half), :] = top_i[...]
    images[pl.ds(half, half), :] = bot_i[...]
    loss = scaled = grad = jnp.zeros((8, rows), F32)

    def sim_of(t):
        return sim_tile(images[...], texts[pl.ds(t * rows, rows), :])

    sim = sim_of(0)
    for t in range(4):
        sim_next = sim_of(t + 1) if t < 3 else None
        grad_q, loss_now, scaled_now, grad_now = pair_tile(sim, scale, bias, False)
        grads[:, pl.ds(t * rows, rows)] = grad_q
        loss, scaled, grad = loss + loss_now, scaled + scaled_now, grad + grad_now
        sim = sim_next
    write_sums(sums_ref, loss, scaled * factor, grad)
    sums_ref[...] += near_sums[...]


def far_grad_kernel(
    far_images, far_grads, near_images, texts, near_grads, sums,
    far_out, y_out, mate_out, own_out, sums_out,
):
    rows = far_images.shape[0]
    far_out[...] = jnp.dot(
        far_grads[...], texts[...], preferred_element_type=F32
    ).astype(BF16)
    for t, out in (
        (3, mate_out.at[pl.ds(0, rows)]),
        (1, mate_out.at[pl.ds(rows, rows)]),
        (2, y_out),
        (0, own_out),
    ):
        out[...] = text_grad(
            near_grads, near_images, far_grads, far_images, pl.ds(t * rows, rows)
        ).astype(out.dtype)
    sums_out[...] = sums[...]


def near_part(scalars, images, texts):
    rows, width = texts[0].shape
    shape = jax.ShapeDtypeStruct
    return pl.pallas_call(
        near_kernel,
        out_shape=(
            shape((rows, width), BF16),
            shape((rows, width), BF16),
            shape((rows, width), BF16),
            shape((3 * rows, width), BF16),
            shape((4 * rows, width), BF16),
            shape((3 * rows, 4 * rows), BF16),
            shape((8, 128), F32),
            shape((1,), jnp.int32),
        ),
        in_specs=[SMEM] * 2 + [VMEM] * 7,
        out_specs=(VMEM,) * 7 + (SMEM,),
        compiler_params=params(16),
        cost_estimate=pl.CostEstimate(
            flops=8 * 2 * 2 * 12 * rows * rows * width,
            bytes_accessed=24 * rows * width,
            transcendentals=3 * 12 * rows * rows,
        ),
        name="near",
    )(*scalars, *images, *texts)


def far_part(scalars, far_images, texts, near_sums):
    half, width = far_images[0].shape
    rows = 2 * half
    shape = jax.ShapeDtypeStruct
    return pl.pallas_call(
        far_kernel,
        out_shape=(
            shape((rows, width), BF16), shape((rows, 4 * rows), BF16), shape((8, 128), F32)
        ),
        in_specs=[SMEM] * 2 + [VMEM] * 4,
        out_specs=(VMEM,) * 3,
        compiler_params=params(16),
        cost_estimate=pl.CostEstimate(
            flops=rows * rows * width, bytes_accessed=2 * rows * width, transcendentals=rows * rows
        ),
        name="far",
    )(*scalars, *far_images, texts, near_sums)


def far_grad_part(far_images, far_grads, near_images, texts, near_grads, sums):
    rows, width = far_images.shape
    shape = jax.ShapeDtypeStruct
    return pl.pallas_call(
        far_grad_kernel,
        out_shape=(
            shape((rows, width), BF16), shape((rows, width), F32), shape((2 * rows, width), BF16),
            shape((rows, width), BF16), shape(sums.shape, F32),
        ),
        in_specs=[VMEM] * 6,
        out_specs=(VMEM,) * 5,
        compiler_params=params(16),
        cost_estimate=pl.CostEstimate(
            flops=rows * rows * width, bytes_accessed=2 * rows * width, transcendentals=0
        ),
        name="far_grad",
    )(far_images, far_grads, near_images, texts, near_grads, sums)


def add_kernel(*refs):
    *parts, out = refs
    out[...] = sum((part[...] for part in parts[1:]), parts[0][...])


def add(*parts):
    one = parts[0]
    return pl.pallas_call(
        add_kernel,
        out_shape=jax.ShapeDtypeStruct(one.shape, F32),
        in_specs=[VMEM] * len(parts),
        out_specs=VMEM,
        compiler_params=params(16),
        cost_estimate=pl.CostEstimate(
            flops=GATE_COST * one.size, bytes_accessed=one.size, transcendentals=0
        ),
        name="add",
    )(*parts)


def relay_y_kernel(own, passing, sums, arrived, out, sums_out):
    rows = own.shape[0]
    out[...] = (own[...] + passing[:rows, :].astype(F32)).astype(BF16)
    sums_out[...] = sums[...] + arrived[...]


def relay_y(own, passing, sums, arrived):
    return pl.pallas_call(
        relay_y_kernel,
        out_shape=(
            jax.ShapeDtypeStruct(own.shape, BF16), jax.ShapeDtypeStruct(sums.shape, F32)
        ),
        in_specs=[VMEM] * 4,
        out_specs=(VMEM,) * 2,
        compiler_params=params(16),
        cost_estimate=pl.CostEstimate(flops=own.size, bytes_accessed=own.size, transcendentals=0),
        name="relay_y",
    )(own, passing, sums, arrived)


def backnorm(emb, upstream, scale):
    hat, inverse = unit_rows(emb)
    along = jnp.sum(hat * upstream, axis=1, keepdims=True)
    return (scale * inverse) * (upstream - hat * along)


def end_kernel(
    log_scale, text_emb, own_q, from_core, from_y, image_emb, own_p, from_left, from_right, from_far,
    sums, text_out, image_out, sums_out, text_slots, image_slots, sems,
):
    scale = jnp.exp(jnp.full((1, 1), log_scale[0]))
    step = text_emb.shape[0] // 4
    sets = (
        (text_emb, (own_q, from_core, from_y), text_out, text_slots),
        (image_emb, (own_p, from_left, from_right, from_far), image_out, image_slots),
    )
    copies = []
    for emb, parts, out, slots in sets:
        for i in range(4):
            at = pl.ds(i * step, step)
            upstream = jnp.zeros((step, emb.shape[1]), F32)
            for part in parts:
                skip = part.shape[0] - 4 * step
                upstream += part[pl.ds(skip + i * step, step), :].astype(F32)
            slots[at, :] = backnorm(emb[at, :], upstream, scale)
            copy = pltpu.make_async_copy(slots.at[at], out.at[at], sems.at[len(copies)])
            copy.start()
            copies.append(copy)
    sums_out[...] = sums[...]
    for copy in copies:
        copy.wait()


def end_part(log_scale, text_parts, image_parts, sums):
    rows, width = text_parts[0].shape
    shape = jax.ShapeDtypeStruct
    return pl.pallas_call(
        end_kernel,
        out_shape=(shape((rows, width), F32),) * 2 + (shape(sums.shape, F32),),
        in_specs=[SMEM] + [VMEM] * 10,
        out_specs=(HBM, HBM, VMEM),
        scratch_shapes=[
            pltpu.VMEM((rows, width), F32),
            pltpu.VMEM((rows, width), F32),
            pltpu.SemaphoreType.DMA((8,)),
        ],
        compiler_params=params(24),
        cost_estimate=pl.CostEstimate(
            flops=16 * rows * width, bytes_accessed=2 * rows * width, transcendentals=2 * rows
        ),
        name="end",
    )(log_scale, *text_parts, *image_parts, sums)


def totals_kernel(*refs):
    parts, outs = refs[:-3], refs[-3:]
    total = sum((part[...] for part in parts[1:]), parts[0][...])
    for i, out in enumerate(outs):
        out[0] = jnp.sum(total[0:1, i : i + 1]) * (1.0 / BATCH)


def totals_part(*parts):
    return pl.pallas_call(
        totals_kernel,
        out_shape=(jax.ShapeDtypeStruct((1,), F32),) * 3,
        in_specs=[VMEM] * len(parts),
        out_specs=(SMEM,) * 3,
        compiler_params=params(16),
        cost_estimate=pl.CostEstimate(flops=4096, bytes_accessed=4096, transcendentals=0),
        name="totals",
    )(*parts)


def shards(image_emb, text_emb, log_scale, bias):
    rows = image_emb.shape[0]
    blocks = lax.axis_size("blk")
    ahead = [(i, (i + 4) % blocks) for i in range(blocks)]
    back = [(i, (i - 4) % blocks) for i in range(blocks)]
    across_y = [(i, i ^ 2) for i in range(blocks)]
    across_core = [(i, i ^ 1) for i in range(blocks)]

    def send(value, perm):
        return lax.ppermute(value, "blk", perm)

    scalars = log_scale.reshape(1), bias.reshape(1)
    own_i, token = normalize(image_emb)
    own_t, _ = normalize(text_emb, token)
    left_i = send(own_i, ahead)
    right_i = send(own_i, back)
    y_t = send(own_t, across_y)
    core_t = send(own_t, across_core)
    yc_t = send(y_t, across_core)
    top_i = send(cut(left_i, 0), ahead)
    bot_i = send(cut(right_i, rows // 2), back)

    own_p, left_p, right_p, near_images, texts, near_grads, near_sums, passes = near_part(
        scalars, (own_i, left_i, right_i), (own_t, core_t, y_t, yc_t)
    )
    from_left = send(right_p, ahead)
    from_right = send(left_p, back)
    far_images, far_grads, sums = far_part(scalars, (top_i, bot_i), texts, near_sums)

    def pair(value, axis, k):
        return lax.ppermute(value, axis, [(i, i ^ k) for i in range(lax.axis_size(axis))])

    over_y = pair(sums, "blk", 2)
    far_p, y_q, to_mate, own_q, sums = far_grad_part(
        far_images, far_grads, near_images, texts, near_grads, sums
    )
    sums_1 = add(sums, over_y)
    from_far = send(far_p, [(i, (i + 8) % blocks) for i in range(blocks)])
    from_core = send(to_mate, across_core)
    y_sum, sums_2 = relay_y(y_q, from_core, sums_1, pair(sums_1, "blk", 1))
    from_y = send(y_sum, across_y)
    sums_2 = add(sums_2)

    def steps(carry):
        left, value = carry
        for axis, k in STEPS:
            value = value + pair(value, axis, k)
        return left - 1, value

    _, sums_6 = lax.while_loop(lambda carry: carry[0] > 0, steps, (passes[0], sums_2))
    over_x = [pair(sums_6, "blk", k) for k in (4, 8, 12)]
    grad_text, grad_image, sums_6 = end_part(
        scalars[0],
        (text_emb, own_q, from_core, from_y),
        (image_emb, own_p, from_left, from_right, from_far),
        sums_6,
    )
    loss, grad_scale, grad_bias = (total.reshape(()) for total in totals_part(sums_6, *over_x))
    return (loss, grad_image, grad_text, grad_scale, grad_bias)


def solution(mesh):
    in_specs = (P(("blk", "group"), None), P(("blk", "group"), None), P(), P())
    out_specs = (P(), P(("blk", "group"), None), P(("blk", "group"), None), P(), P())
    return jax.shard_map(shards, mesh=mesh, in_specs=in_specs, out_specs=out_specs, check_vma=False)
```

```python
import jax
import jax.numpy as jnp
from jax import lax
from jax.experimental import pallas as pl
from jax.experimental.pallas import tpu as pltpu
from jax.sharding import PartitionSpec as P

F32 = jnp.float32
LOG2E = 1.4426950408889634
BATCH = 65536
GATE_COST = 1
CUT_COST = 1024 * 32
STEPS = (("group", 1), ("group", 2), ("group", 7), (("blk", "group"), 2 * 16 + 8))
BF16 = jnp.bfloat16
ANY = pl.BlockSpec(memory_space=pl.ANY)
HBM = pl.BlockSpec(memory_space=pltpu.HBM)
VMEM = pl.BlockSpec(memory_space=pltpu.VMEM)
SMEM = pl.BlockSpec(memory_space=pltpu.SMEM)


def params(mib):
    return pltpu.CompilerParams(vmem_limit_bytes=mib * 1024 * 1024)


def unit_rows(emb):
    inverse = lax.rsqrt(jnp.sum(emb * emb, axis=1, keepdims=True) + 1e-06)
    return emb * inverse, inverse


def normalize_kernel(emb_ref, *refs):
    norm_ref, token = refs[-2:]
    norm_ref[...] = unit_rows(emb_ref[...])[0].astype(BF16)
    token[...] = jnp.zeros(token.shape, F32)


def normalize(emb, *after):
    rows, width = emb.shape
    return pl.pallas_call(
        normalize_kernel,
        out_shape=(
            jax.ShapeDtypeStruct((rows, width), BF16), jax.ShapeDtypeStruct((8, 128), F32)
        ),
        in_specs=[VMEM] * (1 + len(after)),
        out_specs=(VMEM,) * 2,
        compiler_params=params(16),
        cost_estimate=pl.CostEstimate(
            flops=4 * rows * width, bytes_accessed=6 * rows * width, transcendentals=rows
        ),
        name="normalize",
    )(emb, *after)


def cut(block, at):
    rows, width = block.shape

    def kernel(block_ref, out_ref):
        out_ref[...] = block_ref[pl.ds(at, rows // 2), :]

    return pl.pallas_call(
        kernel,
        out_shape=jax.ShapeDtypeStruct((rows // 2, width), block.dtype),
        in_specs=[VMEM],
        out_specs=VMEM,
        compiler_params=params(16),
        cost_estimate=pl.CostEstimate(
            flops=CUT_COST * rows * width, bytes_accessed=rows * width, transcendentals=0
        ),
        name="cut",
    )(block)


def sim_tile(image_rows, text_rows):
    return lax.dot_general(
        image_rows, text_rows, (((1,), (1,)), ((), ())), preferred_element_type=F32
    )


def pair_tile(sim, scale, bias, diagonal):
    logits = sim * scale + bias
    rows, columns = sim.shape
    if diagonal:
        positive = lax.broadcasted_iota(jnp.int32, (rows, columns), 0) == (
            lax.broadcasted_iota(jnp.int32, (rows, columns), 1)
        )
        logits = jnp.where(positive, -logits, logits)
    odds = jnp.exp2(logits)
    total = 1.0 + odds
    inverse = pl.reciprocal(total, approx=True)
    inverse = inverse * (2.0 - total * inverse)
    grad = odds * inverse
    if diagonal:
        grad = jnp.where(positive, -grad, grad)
    part = rows // 8
    product = total[:part]
    for i in range(1, 8):
        product = product * total[i * part : (i + 1) * part]

    def fold(values):
        return jnp.sum(values.reshape(values.shape[0] // 8, 8, columns), axis=0)

    return grad.astype(BF16), fold(jnp.log(product)), fold(grad * sim), fold(grad)


def logit_factors(log_scale, bias, columns):
    scale = jnp.exp(jnp.full((1, columns), log_scale[0]))
    return scale, scale * LOG2E, bias[0] * LOG2E


def write_sums(sums_ref, loss, scaled, grad):
    column = lax.broadcasted_iota(jnp.int32, sums_ref.shape, 1)
    sums_ref[...] = jnp.where(
        column == 0, jnp.sum(loss), jnp.where(column == 1, jnp.sum(scaled), jnp.sum(grad))
    )


def near_kernel(
    log_scale, bias, own_i, left_i, right_i, own_t, core_t, y_t, yc_t,
    own_out, left_out, right_out, images, texts, grads, sums_ref, passes_ref, sems,
):
    rows = own_i.shape[0]
    factor, scale, bias = logit_factors(log_scale, bias, rows)
    blocks = [(own_i, images, 0), (own_t, texts, 0)]
    blocks += [(src, texts, i) for i, src in enumerate((core_t, y_t, yc_t), 1)]
    blocks += [(src, images, i) for i, src in enumerate((left_i, right_i), 1)]
    copies = [
        pltpu.make_async_copy(src, dst.at[pl.ds(i * rows, rows)], sems.at[k])
        for k, (src, dst, i) in enumerate(blocks)
    ]
    for copy in copies:
        copy.start()
    copies[0].wait()
    copies[1].wait()
    loss = scaled = grad = jnp.zeros((8, rows), F32)
    tiles = [(b, t) for b in range(3) for t in range(4)]

    def sim_of(k):
        b, t = tiles[k]
        return sim_tile(images[pl.ds(b * rows, rows), :], texts[pl.ds(t * rows, rows), :])

    sim = sim_of(0)
    for k, (b, t) in enumerate(tiles):
        if k < 3:
            copies[k + 2].wait()
        elif k in (3, 7):
            copies[5 + k // 7].wait()
        sim_next = sim_of(k + 1) if k + 1 < len(tiles) else None
        grad_q, loss_now, scaled_now, grad_now = pair_tile(sim, scale, bias, k == 0)
        grads[pl.ds(b * rows, rows), pl.ds(t * rows, rows)] = grad_q
        loss, scaled, grad = loss + loss_now, scaled + scaled_now, grad + grad_now
        sim = sim_next
        if t == 3:
            partial = jnp.dot(
                grads[pl.ds(b * rows, rows), :], texts[...], preferred_element_type=F32
            )
            out = (own_out, left_out, right_out)[b]
            out[...] = partial.astype(out.dtype)
    write_sums(sums_ref, loss, scaled * factor, grad)
    passes_ref[0] = 1


def text_grad(grads, near_images, far_grads, far_images, at):
    return lax.dot_general(
        grads[:, at], near_images[...], (((0,), (0,)), ((), ())), preferred_element_type=F32
    ) + lax.dot_general(
        far_grads[:, at], far_images[...], (((0,), (0,)), ((), ())), preferred_element_type=F32
    )


def far_kernel(log_scale, bias, top_i, bot_i, texts, near_sums, images, grads, sums_ref):
    half = top_i.shape[0]
    rows = 2 * half
    factor, scale, bias = logit_factors(log_scale, bias, rows)
    images[pl.ds(0, half), :] = top_i[...]
    images[pl.ds(half, half), :] = bot_i[...]
    loss = scaled = grad = jnp.zeros((8, rows), F32)

    def sim_of(t):
        return sim_tile(images[...], texts[pl.ds(t * rows, rows), :])

    sim = sim_of(0)
    for t in range(4):
        sim_next = sim_of(t + 1) if t < 3 else None
        grad_q, loss_now, scaled_now, grad_now = pair_tile(sim, scale, bias, False)
        grads[:, pl.ds(t * rows, rows)] = grad_q
        loss, scaled, grad = loss + loss_now, scaled + scaled_now, grad + grad_now
        sim = sim_next
    write_sums(sums_ref, loss, scaled * factor, grad)
    sums_ref[...] += near_sums[...]


def far_grad_kernel(
    far_images, far_grads, near_images, texts, near_grads, sums,
    far_out, y_out, mate_out, own_out, sums_out,
):
    rows = far_images.shape[0]
    far_out[...] = jnp.dot(
        far_grads[...], texts[...], preferred_element_type=F32
    ).astype(BF16)
    for t, out in (
        (3, mate_out.at[pl.ds(0, rows)]),
        (1, mate_out.at[pl.ds(rows, rows)]),
        (2, y_out),
        (0, own_out),
    ):
        out[...] = text_grad(
            near_grads, near_images, far_grads, far_images, pl.ds(t * rows, rows)
        ).astype(out.dtype)
    sums_out[...] = sums[...]


def near_part(scalars, images, texts):
    rows, width = texts[0].shape
    shape = jax.ShapeDtypeStruct
    return pl.pallas_call(
        near_kernel,
        out_shape=(
            shape((rows, width), BF16),
            shape((rows, width), BF16),
            shape((rows, width), BF16),
            shape((3 * rows, width), BF16),
            shape((4 * rows, width), BF16),
            shape((3 * rows, 4 * rows), BF16),
            shape((8, 128), F32),
            shape((1,), jnp.int32),
        ),
        in_specs=[SMEM] * 2 + [ANY] * 7,
        out_specs=(VMEM,) * 7 + (SMEM,),
        scratch_shapes=[pltpu.SemaphoreType.DMA((7,))],
        compiler_params=params(16),
        cost_estimate=pl.CostEstimate(
            flops=8 * 2 * 2 * 12 * rows * rows * width,
            bytes_accessed=24 * rows * width,
            transcendentals=3 * 12 * rows * rows,
        ),
        name="near",
    )(*scalars, *images, *texts)


def far_part(scalars, far_images, texts, near_sums):
    half, width = far_images[0].shape
    rows = 2 * half
    shape = jax.ShapeDtypeStruct
    return pl.pallas_call(
        far_kernel,
        out_shape=(
            shape((rows, width), BF16), shape((rows, 4 * rows), BF16), shape((8, 128), F32)
        ),
        in_specs=[SMEM] * 2 + [VMEM] * 4,
        out_specs=(VMEM,) * 3,
        compiler_params=params(16),
        cost_estimate=pl.CostEstimate(
            flops=rows * rows * width, bytes_accessed=2 * rows * width, transcendentals=rows * rows
        ),
        name="far",
    )(*scalars, *far_images, texts, near_sums)


def far_grad_part(far_images, far_grads, near_images, texts, near_grads, sums):
    rows, width = far_images.shape
    shape = jax.ShapeDtypeStruct
    return pl.pallas_call(
        far_grad_kernel,
        out_shape=(
            shape((rows, width), BF16), shape((rows, width), F32), shape((2 * rows, width), BF16),
            shape((rows, width), BF16), shape(sums.shape, F32),
        ),
        in_specs=[VMEM] * 6,
        out_specs=(VMEM,) * 5,
        compiler_params=params(16),
        cost_estimate=pl.CostEstimate(
            flops=rows * rows * width, bytes_accessed=2 * rows * width, transcendentals=0
        ),
        name="far_grad",
    )(far_images, far_grads, near_images, texts, near_grads, sums)


def add_kernel(*refs):
    *parts, out = refs
    out[...] = sum((part[...] for part in parts[1:]), parts[0][...])


def add(*parts):
    one = parts[0]
    return pl.pallas_call(
        add_kernel,
        out_shape=jax.ShapeDtypeStruct(one.shape, F32),
        in_specs=[VMEM] * len(parts),
        out_specs=VMEM,
        compiler_params=params(16),
        cost_estimate=pl.CostEstimate(
            flops=GATE_COST * one.size, bytes_accessed=one.size, transcendentals=0
        ),
        name="add",
    )(*parts)


def relay_y_kernel(own, passing, sums, sums_a, sums_b, sums_c, out, sums_out):
    rows = own.shape[0]
    out[...] = (own[...] + passing[:rows, :].astype(F32)).astype(BF16)
    sums_out[...] = sums[...] + sums_a[...] + sums_b[...] + sums_c[...]


def relay_y(own, passing, sums, *arrived):
    return pl.pallas_call(
        relay_y_kernel,
        out_shape=(
            jax.ShapeDtypeStruct(own.shape, BF16), jax.ShapeDtypeStruct(sums.shape, F32)
        ),
        in_specs=[VMEM] * 6,
        out_specs=(VMEM,) * 2,
        compiler_params=params(16),
        cost_estimate=pl.CostEstimate(flops=own.size, bytes_accessed=own.size, transcendentals=0),
        name="relay_y",
    )(own, passing, sums, *arrived)


def backnorm(emb, upstream, scale):
    hat, inverse = unit_rows(emb)
    along = jnp.sum(hat * upstream, axis=1, keepdims=True)
    return (scale * inverse) * (upstream - hat * along)


def end_kernel(
    log_scale, text_emb, own_q, from_core, from_y, image_emb, own_p, from_left, from_right, from_far,
    sums, text_out, image_out, sums_out, text_slots, image_slots, sems,
):
    scale = jnp.exp(jnp.full((1, 1), log_scale[0]))
    step = text_emb.shape[0] // 4
    sets = (
        (text_emb, (own_q, from_core, from_y), text_out, text_slots),
        (image_emb, (own_p, from_left, from_right, from_far), image_out, image_slots),
    )
    copies = []
    for emb, parts, out, slots in sets:
        for i in range(4):
            at = pl.ds(i * step, step)
            upstream = jnp.zeros((step, emb.shape[1]), F32)
            for part in parts:
                skip = part.shape[0] - 4 * step
                upstream += part[pl.ds(skip + i * step, step), :].astype(F32)
            slots[at, :] = backnorm(emb[at, :], upstream, scale)
            copy = pltpu.make_async_copy(slots.at[at], out.at[at], sems.at[len(copies)])
            copy.start()
            copies.append(copy)
    sums_out[...] = sums[...]
    for copy in copies:
        copy.wait()


def end_part(log_scale, text_parts, image_parts, sums):
    rows, width = text_parts[0].shape
    shape = jax.ShapeDtypeStruct
    return pl.pallas_call(
        end_kernel,
        out_shape=(shape((rows, width), F32),) * 2 + (shape(sums.shape, F32),),
        in_specs=[SMEM] + [VMEM] * 10,
        out_specs=(HBM, HBM, VMEM),
        scratch_shapes=[
            pltpu.VMEM((rows, width), F32),
            pltpu.VMEM((rows, width), F32),
            pltpu.SemaphoreType.DMA((8,)),
        ],
        compiler_params=params(24),
        cost_estimate=pl.CostEstimate(
            flops=16 * rows * width, bytes_accessed=2 * rows * width, transcendentals=2 * rows
        ),
        name="end",
    )(log_scale, *text_parts, *image_parts, sums)


def totals_kernel(*refs):
    parts, outs = refs[:-3], refs[-3:]
    total = sum((part[...] for part in parts[1:]), parts[0][...])
    for i, out in enumerate(outs):
        out[0] = jnp.sum(total[0:1, i : i + 1]) * (1.0 / BATCH)


def totals_part(*parts):
    return pl.pallas_call(
        totals_kernel,
        out_shape=(jax.ShapeDtypeStruct((1,), F32),) * 3,
        in_specs=[VMEM] * len(parts),
        out_specs=(SMEM,) * 3,
        compiler_params=params(16),
        cost_estimate=pl.CostEstimate(flops=4096, bytes_accessed=4096, transcendentals=0),
        name="totals",
    )(*parts)


def shards(image_emb, text_emb, log_scale, bias):
    rows = image_emb.shape[0]
    blocks = lax.axis_size("blk")
    ahead = [(i, (i + 4) % blocks) for i in range(blocks)]
    back = [(i, (i - 4) % blocks) for i in range(blocks)]
    across_y = [(i, i ^ 2) for i in range(blocks)]
    across_core = [(i, i ^ 1) for i in range(blocks)]

    def send(value, perm):
        return lax.ppermute(value, "blk", perm)

    scalars = log_scale.reshape(1), bias.reshape(1)
    own_i, token = normalize(image_emb)
    own_t, _ = normalize(text_emb, token)
    left_i = send(own_i, ahead)
    right_i = send(own_i, back)
    y_t = send(own_t, across_y)
    core_t = send(own_t, across_core)
    yc_t = send(y_t, across_core)
    top_i = send(cut(left_i, 0), ahead)
    bot_i = send(cut(right_i, rows // 2), back)

    own_p, left_p, right_p, near_images, texts, near_grads, near_sums, passes = near_part(
        scalars, (own_i, left_i, right_i), (own_t, core_t, y_t, yc_t)
    )
    from_left = send(right_p, ahead)
    from_right = send(left_p, back)
    far_images, far_grads, sums = far_part(scalars, (top_i, bot_i), texts, near_sums)

    def pair(value, axis, k):
        return lax.ppermute(value, axis, [(i, i ^ k) for i in range(lax.axis_size(axis))])

    over_y_core = [pair(sums, "blk", k) for k in (3, 2, 1)]
    far_p, y_q, to_mate, own_q, sums = far_grad_part(
        far_images, far_grads, near_images, texts, near_grads, sums
    )
    from_far = send(far_p, [(i, (i + 8) % blocks) for i in range(blocks)])
    from_core = send(to_mate, across_core)
    y_sum, sums_2 = relay_y(y_q, from_core, sums, *over_y_core)
    from_y = send(y_sum, across_y)
    sums_2 = add(sums_2)

    def steps(carry):
        left, value = carry
        for axis, k in STEPS:
            value = value + pair(value, axis, k)
        return left - 1, value

    _, sums_6 = lax.while_loop(lambda carry: carry[0] > 0, steps, (passes[0], sums_2))
    over_x = [pair(sums_6, "blk", k) for k in (4, 8, 12)]
    grad_text, grad_image, sums_6 = end_part(
        scalars[0],
        (text_emb, own_q, from_core, from_y),
        (image_emb, own_p, from_left, from_right, from_far),
        sums_6,
    )
    loss, grad_scale, grad_bias = (total.reshape(()) for total in totals_part(sums_6, *over_x))
    return (loss, grad_image, grad_text, grad_scale, grad_bias)


def solution(mesh):
    in_specs = (P(("blk", "group"), None), P(("blk", "group"), None), P(), P())
    out_specs = (P(), P(("blk", "group"), None), P(("blk", "group"), None), P(), P())
    return jax.shard_map(shards, mesh=mesh, in_specs=in_specs, out_specs=out_specs, check_vma=False)
```

```python
import jax
import jax.numpy as jnp
from jax import lax
from jax.experimental import pallas as pl
from jax.experimental.pallas import tpu as pltpu
from jax.sharding import PartitionSpec as P

F32 = jnp.float32
LOG2E = 1.4426950408889634
BATCH = 65536
GATE_COST = 1
CUT_COST = 1024 * 32
STEPS = (("group", 1), ("group", 2), ("group", 7), (("blk", "group"), 2 * 16 + 8))
BF16 = jnp.bfloat16
ANY = pl.BlockSpec(memory_space=pl.ANY)
HBM = pl.BlockSpec(memory_space=pltpu.HBM)
VMEM = pl.BlockSpec(memory_space=pltpu.VMEM)
SMEM = pl.BlockSpec(memory_space=pltpu.SMEM)


def params(mib):
    return pltpu.CompilerParams(vmem_limit_bytes=mib * 1024 * 1024)


def unit_rows(emb):
    inverse = lax.rsqrt(jnp.sum(emb * emb, axis=1, keepdims=True) + 1e-06)
    return emb * inverse, inverse


def normalize_kernel(emb_ref, *refs):
    norm_ref, token = refs[-2:]
    norm_ref[...] = unit_rows(emb_ref[...])[0].astype(BF16)
    token[...] = jnp.zeros(token.shape, F32)


def normalize(emb, *after):
    rows, width = emb.shape
    return pl.pallas_call(
        normalize_kernel,
        out_shape=(
            jax.ShapeDtypeStruct((rows, width), BF16), jax.ShapeDtypeStruct((8, 128), F32)
        ),
        in_specs=[VMEM] * (1 + len(after)),
        out_specs=(VMEM,) * 2,
        compiler_params=params(16),
        cost_estimate=pl.CostEstimate(
            flops=4 * rows * width, bytes_accessed=6 * rows * width, transcendentals=rows
        ),
        name="normalize",
    )(emb, *after)


def cut(block, at):
    rows, width = block.shape

    def kernel(block_ref, out_ref):
        out_ref[...] = block_ref[pl.ds(at, rows // 2), :]

    return pl.pallas_call(
        kernel,
        out_shape=jax.ShapeDtypeStruct((rows // 2, width), block.dtype),
        in_specs=[VMEM],
        out_specs=VMEM,
        compiler_params=params(16),
        cost_estimate=pl.CostEstimate(
            flops=CUT_COST * rows * width, bytes_accessed=rows * width, transcendentals=0
        ),
        name="cut",
    )(block)


def sim_tile(image_rows, text_rows):
    return lax.dot_general(
        image_rows, text_rows, (((1,), (1,)), ((), ())), preferred_element_type=F32
    )


def pair_tile(sim, scale, bias, diagonal):
    logits = sim * scale + bias
    rows, columns = sim.shape
    if diagonal:
        positive = lax.broadcasted_iota(jnp.int32, (rows, columns), 0) == (
            lax.broadcasted_iota(jnp.int32, (rows, columns), 1)
        )
        logits = jnp.where(positive, -logits, logits)
    odds = jnp.exp2(logits)
    total = 1.0 + odds
    inverse = pl.reciprocal(total, approx=True)
    inverse = inverse * (2.0 - total * inverse)
    grad = odds * inverse
    if diagonal:
        grad = jnp.where(positive, -grad, grad)
    part = rows // 8
    product = total[:part]
    for i in range(1, 8):
        product = product * total[i * part : (i + 1) * part]

    def fold(values):
        return jnp.sum(values.reshape(values.shape[0] // 8, 8, columns), axis=0)

    return grad.astype(BF16), fold(jnp.log(product)), fold(grad * sim), fold(grad)


def logit_factors(log_scale, bias, columns):
    scale = jnp.exp(jnp.full((1, columns), log_scale[0]))
    return scale, scale * LOG2E, bias[0] * LOG2E


def write_sums(sums_ref, loss, scaled, grad):
    column = lax.broadcasted_iota(jnp.int32, sums_ref.shape, 1)
    sums_ref[...] = jnp.where(
        column == 0, jnp.sum(loss), jnp.where(column == 1, jnp.sum(scaled), jnp.sum(grad))
    )


def near_kernel(
    log_scale, bias, own_i, left_i, right_i, own_t, core_t, y_t, yc_t,
    own_out, left_out, right_out, images, texts, grads, sums_ref, passes_ref, sems,
):
    rows = own_i.shape[0]
    factor, scale, bias = logit_factors(log_scale, bias, rows)
    blocks = [(own_i, images, 0), (own_t, texts, 0), (left_i, images, 1), (right_i, images, 2)]
    blocks += [(src, texts, i) for i, src in enumerate((core_t, y_t, yc_t), 1)]
    copies = [
        pltpu.make_async_copy(src, dst.at[pl.ds(i * rows, rows)], sems.at[k])
        for k, (src, dst, i) in enumerate(blocks)
    ]
    for copy in copies:
        copy.start()
    copies[0].wait()
    copies[1].wait()
    loss = scaled = grad = jnp.zeros((8, rows), F32)
    tiles = [(b, t) for t in range(4) for b in range(3)]

    def sim_of(k):
        b, t = tiles[k]
        return sim_tile(images[pl.ds(b * rows, rows), :], texts[pl.ds(t * rows, rows), :])

    sim = sim_of(0)
    for k, (b, t) in enumerate(tiles):
        if k < 2:
            copies[k + 2].wait()
        elif k in (2, 5, 8):
            copies[k // 3 + 4].wait()
        sim_next = sim_of(k + 1) if k + 1 < len(tiles) else None
        grad_q, loss_now, scaled_now, grad_now = pair_tile(sim, scale, bias, k == 0)
        grads[pl.ds(b * rows, rows), pl.ds(t * rows, rows)] = grad_q
        loss, scaled, grad = loss + loss_now, scaled + scaled_now, grad + grad_now
        sim = sim_next
        if t == 3:
            partial = jnp.dot(
                grads[pl.ds(b * rows, rows), :], texts[...], preferred_element_type=F32
            )
            out = (own_out, left_out, right_out)[b]
            out[...] = partial.astype(out.dtype)
    write_sums(sums_ref, loss, scaled * factor, grad)
    passes_ref[0] = 1


def text_grad(grads, near_images, far_grads, far_images, at):
    return lax.dot_general(
        grads[:, at], near_images[...], (((0,), (0,)), ((), ())), preferred_element_type=F32
    ) + lax.dot_general(
        far_grads[:, at], far_images[...], (((0,), (0,)), ((), ())), preferred_element_type=F32
    )


def far_kernel(log_scale, bias, top_i, bot_i, texts, near_sums, images, grads, sums_ref):
    half = top_i.shape[0]
    rows = 2 * half
    factor, scale, bias = logit_factors(log_scale, bias, rows)
    images[pl.ds(0, half), :] = top_i[...]
    images[pl.ds(half, half), :] = bot_i[...]
    loss = scaled = grad = jnp.zeros((8, rows), F32)

    def sim_of(t):
        return sim_tile(images[...], texts[pl.ds(t * rows, rows), :])

    sim = sim_of(0)
    for t in range(4):
        sim_next = sim_of(t + 1) if t < 3 else None
        grad_q, loss_now, scaled_now, grad_now = pair_tile(sim, scale, bias, False)
        grads[:, pl.ds(t * rows, rows)] = grad_q
        loss, scaled, grad = loss + loss_now, scaled + scaled_now, grad + grad_now
        sim = sim_next
    write_sums(sums_ref, loss, scaled * factor, grad)
    sums_ref[...] += near_sums[...]


def far_grad_kernel(
    far_images, far_grads, near_images, texts, near_grads, sums,
    far_out, mate_out, own_out, y_out, sums_out, blocks, sems,
):
    rows = far_images.shape[0]
    copies = []

    def leave(values, out):
        i = len(copies)
        blocks[i] = values.astype(BF16)
        copy = pltpu.make_async_copy(blocks.at[i], out, sems.at[i])
        copy.start()
        copies.append(copy)

    def text_block(t):
        return text_grad(near_grads, near_images, far_grads, far_images, pl.ds(t * rows, rows))

    leave(jnp.dot(far_grads[...], texts[...], preferred_element_type=F32), far_out)
    leave(text_block(3), mate_out.at[pl.ds(0, rows)])
    leave(text_block(1), mate_out.at[pl.ds(rows, rows)])
    leave(text_block(0), own_out)
    y_out[...] = text_block(2)
    sums_out[...] = sums[...]
    for copy in copies:
        copy.wait()


def near_part(scalars, images, texts):
    rows, width = texts[0].shape
    shape = jax.ShapeDtypeStruct
    return pl.pallas_call(
        near_kernel,
        out_shape=(
            shape((rows, width), BF16),
            shape((rows, width), BF16),
            shape((rows, width), BF16),
            shape((3 * rows, width), BF16),
            shape((4 * rows, width), BF16),
            shape((3 * rows, 4 * rows), BF16),
            shape((8, 128), F32),
            shape((1,), jnp.int32),
        ),
        in_specs=[SMEM] * 2 + [ANY] * 7,
        out_specs=(VMEM,) * 7 + (SMEM,),
        scratch_shapes=[pltpu.SemaphoreType.DMA((7,))],
        compiler_params=params(16),
        cost_estimate=pl.CostEstimate(
            flops=8 * 2 * 2 * 12 * rows * rows * width,
            bytes_accessed=24 * rows * width,
            transcendentals=3 * 12 * rows * rows,
        ),
        name="near",
    )(*scalars, *images, *texts)


def far_part(scalars, far_images, texts, near_sums):
    half, width = far_images[0].shape
    rows = 2 * half
    shape = jax.ShapeDtypeStruct
    return pl.pallas_call(
        far_kernel,
        out_shape=(
            shape((rows, width), BF16), shape((rows, 4 * rows), BF16), shape((8, 128), F32)
        ),
        in_specs=[SMEM] * 2 + [VMEM] * 4,
        out_specs=(VMEM,) * 3,
        compiler_params=params(16),
        cost_estimate=pl.CostEstimate(
            flops=rows * rows * width, bytes_accessed=2 * rows * width, transcendentals=rows * rows
        ),
        name="far",
    )(*scalars, *far_images, texts, near_sums)


def far_grad_part(far_images, far_grads, near_images, texts, near_grads, sums):
    rows, width = far_images.shape
    shape = jax.ShapeDtypeStruct
    return pl.pallas_call(
        far_grad_kernel,
        out_shape=(
            shape((rows, width), BF16), shape((2 * rows, width), BF16), shape((rows, width), BF16),
            shape((rows, width), F32), shape(sums.shape, F32),
        ),
        in_specs=[VMEM] * 6,
        out_specs=(ANY,) * 3 + (VMEM,) * 2,
        scratch_shapes=[pltpu.VMEM((4, rows, width), BF16), pltpu.SemaphoreType.DMA((4,))],
        compiler_params=params(16),
        cost_estimate=pl.CostEstimate(
            flops=rows * rows * width, bytes_accessed=2 * rows * width, transcendentals=0
        ),
        name="far_grad",
    )(far_images, far_grads, near_images, texts, near_grads, sums)


def add_kernel(*refs):
    *parts, out = refs
    out[...] = sum((part[...] for part in parts[1:]), parts[0][...])


def add(*parts):
    one = parts[0]
    return pl.pallas_call(
        add_kernel,
        out_shape=jax.ShapeDtypeStruct(one.shape, F32),
        in_specs=[VMEM] * len(parts),
        out_specs=VMEM,
        compiler_params=params(16),
        cost_estimate=pl.CostEstimate(
            flops=GATE_COST * one.size, bytes_accessed=one.size, transcendentals=0
        ),
        name="add",
    )(*parts)


def relay_y_kernel(own, passing, sums, sums_a, sums_b, sums_c, out, sums_out):
    rows = own.shape[0]
    out[...] = (own[...] + passing[:rows, :].astype(F32)).astype(BF16)
    sums_out[...] = sums[...] + sums_a[...] + sums_b[...] + sums_c[...]


def relay_y(own, passing, sums, *arrived):
    return pl.pallas_call(
        relay_y_kernel,
        out_shape=(
            jax.ShapeDtypeStruct(own.shape, BF16), jax.ShapeDtypeStruct(sums.shape, F32)
        ),
        in_specs=[VMEM] * 6,
        out_specs=(VMEM,) * 2,
        compiler_params=params(16),
        cost_estimate=pl.CostEstimate(flops=own.size, bytes_accessed=own.size, transcendentals=0),
        name="relay_y",
    )(own, passing, sums, *arrived)


def backnorm(emb, upstream, scale):
    hat, inverse = unit_rows(emb)
    along = jnp.sum(hat * upstream, axis=1, keepdims=True)
    return (scale * inverse) * (upstream - hat * along)


def end_kernel(
    log_scale, text_emb, own_q, from_core, from_y, image_emb, own_p, from_left, from_right, from_far,
    sums, text_out, image_out, sums_out, embs, blocks, in_sems, out_sems,
):
    scale = jnp.exp(jnp.full((1, 1), log_scale[0]))
    rows = embs.shape[1]
    step = rows // 4
    sources = (own_q, from_core.at[pl.ds(rows, rows)], from_y, own_p, from_left, from_right, from_far)
    pairs = [(text_emb, embs.at[0])] + [(sources[i], blocks.at[i]) for i in range(3)]
    pairs += [(image_emb, embs.at[1])] + [(sources[i], blocks.at[i]) for i in range(3, 7)]
    loads = [pltpu.make_async_copy(src, dst, in_sems.at[k]) for k, (src, dst) in enumerate(pairs)]
    for load in loads:
        load.start()
    copies = []
    for k, (parts, out) in enumerate(((range(3), text_out), (range(3, 7), image_out))):
        for load in loads[5 * k - k : 4 + 5 * k]:
            load.wait()
        for i in range(4):
            at = pl.ds(i * step, step)
            upstream = jnp.zeros((step, embs.shape[2]), F32)
            for part in parts:
                upstream += blocks[part, at, :].astype(F32)
            embs[k, at, :] = backnorm(embs[k, at, :], upstream, scale)
            copy = pltpu.make_async_copy(embs.at[k, at], out.at[at], out_sems.at[len(copies)])
            copy.start()
            copies.append(copy)
    sums_out[...] = sums[...]
    for copy in copies:
        copy.wait()


def end_part(log_scale, text_parts, image_parts, sums):
    rows, width = text_parts[0].shape
    shape = jax.ShapeDtypeStruct
    return pl.pallas_call(
        end_kernel,
        out_shape=(shape((rows, width), F32),) * 2 + (shape(sums.shape, F32),),
        in_specs=[SMEM] + [ANY] * 9 + [VMEM],
        out_specs=(HBM, HBM, VMEM),
        scratch_shapes=[
            pltpu.VMEM((2, rows, width), F32),
            pltpu.VMEM((7, rows, width), BF16),
            pltpu.SemaphoreType.DMA((9,)),
            pltpu.SemaphoreType.DMA((8,)),
        ],
        compiler_params=params(24),
        cost_estimate=pl.CostEstimate(
            flops=16 * rows * width, bytes_accessed=2 * rows * width, transcendentals=2 * rows
        ),
        name="end",
    )(log_scale, *text_parts, *image_parts, sums)


def totals_kernel(*refs):
    parts, outs = refs[:-3], refs[-3:]
    total = sum((part[...] for part in parts[1:]), parts[0][...])
    for i, out in enumerate(outs):
        out[0] = jnp.sum(total[0:1, i : i + 1]) * (1.0 / BATCH)


def totals_part(*parts):
    return pl.pallas_call(
        totals_kernel,
        out_shape=(jax.ShapeDtypeStruct((1,), F32),) * 3,
        in_specs=[VMEM] * len(parts),
        out_specs=(SMEM,) * 3,
        compiler_params=params(16),
        cost_estimate=pl.CostEstimate(flops=4096, bytes_accessed=4096, transcendentals=0),
        name="totals",
    )(*parts)


def shards(image_emb, text_emb, log_scale, bias):
    rows = image_emb.shape[0]
    blocks = lax.axis_size("blk")
    ahead = [(i, (i + 4) % blocks) for i in range(blocks)]
    back = [(i, (i - 4) % blocks) for i in range(blocks)]
    across_y = [(i, i ^ 2) for i in range(blocks)]
    across_core = [(i, i ^ 1) for i in range(blocks)]

    def send(value, perm):
        return lax.ppermute(value, "blk", perm)

    scalars = log_scale.reshape(1), bias.reshape(1)
    own_i, token = normalize(image_emb)
    own_t, _ = normalize(text_emb, token)
    left_i = send(own_i, ahead)
    right_i = send(own_i, back)
    y_t = send(own_t, across_y)
    core_t = send(own_t, across_core)
    yc_t = send(y_t, across_core)
    top_i = send(cut(left_i, 0), ahead)
    bot_i = send(cut(right_i, rows // 2), back)

    own_p, left_p, right_p, near_images, texts, near_grads, near_sums, passes = near_part(
        scalars, (own_i, left_i, right_i), (own_t, core_t, y_t, yc_t)
    )
    from_left = send(right_p, ahead)
    from_right = send(left_p, back)
    far_images, far_grads, sums = far_part(scalars, (top_i, bot_i), texts, near_sums)

    def pair(value, axis, k):
        return lax.ppermute(value, axis, [(i, i ^ k) for i in range(lax.axis_size(axis))])

    over_y_core = [pair(sums, "blk", k) for k in (3, 2, 1)]
    far_p, to_mate, own_q, y_q, sums = far_grad_part(
        far_images, far_grads, near_images, texts, near_grads, sums
    )
    from_far = send(far_p, [(i, (i + 8) % blocks) for i in range(blocks)])
    from_core = send(to_mate, across_core)
    y_sum, sums_2 = relay_y(y_q, from_core, sums, *over_y_core)
    from_y = send(y_sum, across_y)
    sums_2 = add(sums_2)

    def steps(carry):
        left, value = carry
        for axis, k in STEPS:
            value = value + pair(value, axis, k)
        return left - 1, value

    _, sums_6 = lax.while_loop(lambda carry: carry[0] > 0, steps, (passes[0], sums_2))
    over_x = [pair(sums_6, "blk", k) for k in (4, 8, 12)]
    grad_text, grad_image, sums_6 = end_part(
        scalars[0],
        (text_emb, own_q, from_core, from_y),
        (image_emb, own_p, from_left, from_right, from_far),
        sums_6,
    )
    loss, grad_scale, grad_bias = (total.reshape(()) for total in totals_part(sums_6, *over_x))
    return (loss, grad_image, grad_text, grad_scale, grad_bias)


def solution(mesh):
    in_specs = (P(("blk", "group"), None), P(("blk", "group"), None), P(), P())
    out_specs = (P(), P(("blk", "group"), None), P(("blk", "group"), None), P(), P())
    return jax.shard_map(shards, mesh=mesh, in_specs=in_specs, out_specs=out_specs, check_vma=False)
```

```python
import jax
import jax.numpy as jnp
from jax import lax
from jax.experimental import pallas as pl
from jax.experimental.pallas import tpu as pltpu
from jax.sharding import PartitionSpec as P

F32 = jnp.float32
LOG2E = 1.4426950408889634
BATCH = 65536
GATE_COST = 1
CUT_COST = 1024 * 32
STEPS = (("group", 1), ("group", 2), ("group", 7), (("blk", "group"), 2 * 16 + 8))
BF16 = jnp.bfloat16
HBM = pl.BlockSpec(memory_space=pltpu.HBM)
VMEM = pl.BlockSpec(memory_space=pltpu.VMEM)
SMEM = pl.BlockSpec(memory_space=pltpu.SMEM)


def params(mib):
    return pltpu.CompilerParams(vmem_limit_bytes=mib * 1024 * 1024)


def unit_rows(emb):
    inverse = lax.rsqrt(jnp.sum(emb * emb, axis=1, keepdims=True) + 1e-06)
    return emb * inverse, inverse


def normalize_kernel(emb_ref, *refs):
    norm_ref, token = refs[-2:]
    norm_ref[...] = unit_rows(emb_ref[...])[0].astype(BF16)
    token[...] = jnp.zeros(token.shape, F32)


def normalize(emb, *after):
    rows, width = emb.shape
    return pl.pallas_call(
        normalize_kernel,
        out_shape=(
            jax.ShapeDtypeStruct((rows, width), BF16), jax.ShapeDtypeStruct((8, 128), F32)
        ),
        in_specs=[VMEM] * (1 + len(after)),
        out_specs=(VMEM,) * 2,
        compiler_params=params(16),
        cost_estimate=pl.CostEstimate(
            flops=4 * rows * width, bytes_accessed=6 * rows * width, transcendentals=rows
        ),
        name="normalize",
    )(emb, *after)


def cut(block, at):
    rows, width = block.shape

    def kernel(block_ref, out_ref):
        out_ref[...] = block_ref[pl.ds(at, rows // 2), :]

    return pl.pallas_call(
        kernel,
        out_shape=jax.ShapeDtypeStruct((rows // 2, width), block.dtype),
        in_specs=[VMEM],
        out_specs=VMEM,
        compiler_params=params(16),
        cost_estimate=pl.CostEstimate(
            flops=CUT_COST * rows * width, bytes_accessed=rows * width, transcendentals=0
        ),
        name="cut",
    )(block)


def sim_tile(image_rows, text_rows):
    return lax.dot_general(
        image_rows, text_rows, (((1,), (1,)), ((), ())), preferred_element_type=F32
    )


def pair_tile(sim, scale, bias, diagonal):
    logits = sim * scale + bias
    rows, columns = sim.shape
    if diagonal:
        positive = lax.broadcasted_iota(jnp.int32, (rows, columns), 0) == (
            lax.broadcasted_iota(jnp.int32, (rows, columns), 1)
        )
        logits = jnp.where(positive, -logits, logits)
    odds = jnp.exp2(logits)
    total = 1.0 + odds
    inverse = pl.reciprocal(total, approx=True)
    inverse = inverse * (2.0 - total * inverse)
    grad = odds * inverse
    if diagonal:
        grad = jnp.where(positive, -grad, grad)
    part = rows // 8
    product = total[:part]
    for i in range(1, 8):
        product = product * total[i * part : (i + 1) * part]

    def fold(values):
        return jnp.sum(values.reshape(values.shape[0] // 8, 8, columns), axis=0)

    return grad.astype(BF16), fold(jnp.log(product)), fold(grad * sim), fold(grad)


def logit_factors(log_scale, bias, columns):
    scale = jnp.exp(jnp.full((1, columns), log_scale[0]))
    return scale, scale * LOG2E, bias[0] * LOG2E


def write_sums(sums_ref, loss, scaled, grad):
    column = lax.broadcasted_iota(jnp.int32, sums_ref.shape, 1)
    sums_ref[...] = jnp.where(
        column == 0, jnp.sum(loss), jnp.where(column == 1, jnp.sum(scaled), jnp.sum(grad))
    )


def near_kernel(
    log_scale, bias, own_i, left_i, right_i, own_t, core_t, y_t, yc_t,
    own_out, left_out, right_out, images, texts, grads, sums_ref, passes_ref,
):
    rows = own_i.shape[0]
    factor, scale, bias = logit_factors(log_scale, bias, rows)
    for i, src in enumerate((own_i, left_i, right_i)):
        images[pl.ds(i * rows, rows), :] = src[...]
    for i, src in enumerate((own_t, core_t, y_t, yc_t)):
        texts[pl.ds(i * rows, rows), :] = src[...]
    loss = scaled = grad = jnp.zeros((8, rows), F32)
    tiles = [(b, t) for b in range(3) for t in range(4)]

    def sim_of(k):
        b, t = tiles[k]
        return sim_tile(images[pl.ds(b * rows, rows), :], texts[pl.ds(t * rows, rows), :])

    sim = sim_of(0)
    for k, (b, t) in enumerate(tiles):
        sim_next = sim_of(k + 1) if k + 1 < len(tiles) else None
        grad_q, loss_now, scaled_now, grad_now = pair_tile(sim, scale, bias, k == 0)
        grads[pl.ds(b * rows, rows), pl.ds(t * rows, rows)] = grad_q
        loss, scaled, grad = loss + loss_now, scaled + scaled_now, grad + grad_now
        sim = sim_next
        if t == 3:
            partial = jnp.dot(
                grads[pl.ds(b * rows, rows), :], texts[...], preferred_element_type=F32
            )
            out = (own_out, left_out, right_out)[b]
            out[...] = partial.astype(out.dtype)
    write_sums(sums_ref, loss, scaled * factor, grad)
    passes_ref[0] = 1


def text_grad(grads, near_images, far_grads, far_images, at):
    return lax.dot_general(
        grads[:, at], near_images[...], (((0,), (0,)), ((), ())), preferred_element_type=F32
    ) + lax.dot_general(
        far_grads[:, at], far_images[...], (((0,), (0,)), ((), ())), preferred_element_type=F32
    )


def far_kernel(log_scale, bias, top_i, bot_i, texts, near_sums, images, grads, sums_ref):
    half = top_i.shape[0]
    rows = 2 * half
    factor, scale, bias = logit_factors(log_scale, bias, rows)
    images[pl.ds(0, half), :] = top_i[...]
    images[pl.ds(half, half), :] = bot_i[...]
    loss = scaled = grad = jnp.zeros((8, rows), F32)

    def sim_of(t):
        return sim_tile(images[...], texts[pl.ds(t * rows, rows), :])

    sim = sim_of(0)
    for t in range(4):
        sim_next = sim_of(t + 1) if t < 3 else None
        grad_q, loss_now, scaled_now, grad_now = pair_tile(sim, scale, bias, False)
        grads[:, pl.ds(t * rows, rows)] = grad_q
        loss, scaled, grad = loss + loss_now, scaled + scaled_now, grad + grad_now
        sim = sim_next
    write_sums(sums_ref, loss, scaled * factor, grad)
    sums_ref[...] += near_sums[...]


def far_grad_kernel(
    far_images, far_grads, near_images, texts, near_grads, own_p, sums,
    far_out, y_out, mate_out, own_out, sums_out,
):
    rows = far_images.shape[0]
    far_out[...] = jnp.dot(
        far_grads[...], texts[...], preferred_element_type=F32
    ).astype(BF16)
    for t, out in (
        (3, mate_out.at[pl.ds(0, rows)]),
        (1, mate_out.at[pl.ds(rows, rows)]),
        (2, y_out),
        (0, own_out.at[pl.ds(0, rows)]),
    ):
        out[...] = text_grad(
            near_grads, near_images, far_grads, far_images, pl.ds(t * rows, rows)
        ).astype(out.dtype)
    own_out[pl.ds(rows, rows), :] = own_p[...]
    sums_out[...] = sums[...]


def near_part(scalars, images, texts):
    rows, width = texts[0].shape
    shape = jax.ShapeDtypeStruct
    return pl.pallas_call(
        near_kernel,
        out_shape=(
            shape((rows, width), BF16),
            shape((rows, width), BF16),
            shape((rows, width), BF16),
            shape((3 * rows, width), BF16),
            shape((4 * rows, width), BF16),
            shape((3 * rows, 4 * rows), BF16),
            shape((8, 128), F32),
            shape((1,), jnp.int32),
        ),
        in_specs=[SMEM] * 2 + [VMEM] * 7,
        out_specs=(VMEM,) * 7 + (SMEM,),
        compiler_params=params(16),
        cost_estimate=pl.CostEstimate(
            flops=8 * 2 * 2 * 12 * rows * rows * width,
            bytes_accessed=24 * rows * width,
            transcendentals=3 * 12 * rows * rows,
        ),
        name="near",
    )(*scalars, *images, *texts)


def far_part(scalars, far_images, texts, near_sums):
    half, width = far_images[0].shape
    rows = 2 * half
    shape = jax.ShapeDtypeStruct
    return pl.pallas_call(
        far_kernel,
        out_shape=(
            shape((rows, width), BF16), shape((rows, 4 * rows), BF16), shape((8, 128), F32)
        ),
        in_specs=[SMEM] * 2 + [VMEM] * 4,
        out_specs=(VMEM,) * 3,
        compiler_params=params(16),
        cost_estimate=pl.CostEstimate(
            flops=rows * rows * width, bytes_accessed=2 * rows * width, transcendentals=rows * rows
        ),
        name="far",
    )(*scalars, *far_images, texts, near_sums)


def far_grad_part(far_images, far_grads, near_images, texts, near_grads, own_p, sums):
    rows, width = far_images.shape
    shape = jax.ShapeDtypeStruct
    return pl.pallas_call(
        far_grad_kernel,
        out_shape=(
            shape((rows, width), BF16), shape((rows, width), F32), shape((2 * rows, width), BF16),
            shape((2 * rows, width), BF16), shape(sums.shape, F32),
        ),
        in_specs=[VMEM] * 7,
        out_specs=(VMEM,) * 5,
        compiler_params=params(16),
        cost_estimate=pl.CostEstimate(
            flops=rows * rows * width, bytes_accessed=2 * rows * width, transcendentals=0
        ),
        name="far_grad",
    )(far_images, far_grads, near_images, texts, near_grads, own_p, sums)


def add_kernel(*refs):
    *parts, out = refs
    out[...] = sum((part[...] for part in parts[1:]), parts[0][...])


def add(*parts):
    one = parts[0]
    return pl.pallas_call(
        add_kernel,
        out_shape=jax.ShapeDtypeStruct(one.shape, F32),
        in_specs=[VMEM] * len(parts),
        out_specs=VMEM,
        compiler_params=params(16),
        cost_estimate=pl.CostEstimate(
            flops=GATE_COST * one.size, bytes_accessed=one.size, transcendentals=0
        ),
        name="add",
    )(*parts)


def relay_y_kernel(own, passing, sums, sums_a, sums_b, sums_c, out, sums_out):
    rows = own.shape[0]
    out[...] = (own[...] + passing[:rows, :].astype(F32)).astype(BF16)
    sums_out[...] = sums[...] + sums_a[...] + sums_b[...] + sums_c[...]


def relay_y(own, passing, sums, *arrived):
    return pl.pallas_call(
        relay_y_kernel,
        out_shape=(
            jax.ShapeDtypeStruct(own.shape, BF16), jax.ShapeDtypeStruct(sums.shape, F32)
        ),
        in_specs=[VMEM] * 6,
        out_specs=(VMEM,) * 2,
        compiler_params=params(16),
        cost_estimate=pl.CostEstimate(flops=own.size, bytes_accessed=own.size, transcendentals=0),
        name="relay_y",
    )(own, passing, sums, *arrived)


def backnorm(emb, upstream, scale):
    hat, inverse = unit_rows(emb)
    along = jnp.sum(hat * upstream, axis=1, keepdims=True)
    return (scale * inverse) * (upstream - hat * along)


def end_kernel(
    log_scale, own, text_emb, from_core, from_y, image_emb, from_left, from_right, from_far, sums,
    text_out, image_out, sums_out, text_slots, image_slots, sems,
):
    scale = jnp.exp(jnp.full((1, 1), log_scale[0]))
    step = text_emb.shape[0] // 4
    sets = (
        (text_emb, (from_core, from_y), text_out, text_slots),
        (image_emb, (from_left, from_right, from_far), image_out, image_slots),
    )
    copies = []
    for k, (emb, parts, out, slots) in enumerate(sets):
        for i in range(4):
            at = pl.ds(i * step, step)
            upstream = own[pl.ds((4 * k + i) * step, step), :].astype(F32)
            for part in parts:
                skip = part.shape[0] - 4 * step
                upstream += part[pl.ds(skip + i * step, step), :].astype(F32)
            slots[at, :] = backnorm(emb[at, :], upstream, scale)
            copy = pltpu.make_async_copy(slots.at[at], out.at[at], sems.at[len(copies)])
            copy.start()
            copies.append(copy)
    sums_out[...] = sums[...]
    for copy in copies:
        copy.wait()


def end_part(log_scale, own, text_parts, image_parts, sums):
    rows, width = text_parts[0].shape
    shape = jax.ShapeDtypeStruct
    return pl.pallas_call(
        end_kernel,
        out_shape=(shape((rows, width), F32),) * 2 + (shape(sums.shape, F32),),
        in_specs=[SMEM] + [VMEM] * 9,
        out_specs=(HBM, HBM, VMEM),
        scratch_shapes=[
            pltpu.VMEM((rows, width), F32),
            pltpu.VMEM((rows, width), F32),
            pltpu.SemaphoreType.DMA((8,)),
        ],
        compiler_params=params(24),
        cost_estimate=pl.CostEstimate(
            flops=16 * rows * width, bytes_accessed=2 * rows * width, transcendentals=2 * rows
        ),
        name="end",
    )(log_scale, own, *text_parts, *image_parts, sums)


def totals_kernel(*refs):
    parts, outs = refs[:-3], refs[-3:]
    total = sum((part[...] for part in parts[1:]), parts[0][...])
    for i, out in enumerate(outs):
        out[0] = jnp.sum(total[0:1, i : i + 1]) * (1.0 / BATCH)


def totals_part(*parts):
    return pl.pallas_call(
        totals_kernel,
        out_shape=(jax.ShapeDtypeStruct((1,), F32),) * 3,
        in_specs=[VMEM] * len(parts),
        out_specs=(SMEM,) * 3,
        compiler_params=params(16),
        cost_estimate=pl.CostEstimate(flops=4096, bytes_accessed=4096, transcendentals=0),
        name="totals",
    )(*parts)


def shards(image_emb, text_emb, log_scale, bias):
    rows = image_emb.shape[0]
    blocks = lax.axis_size("blk")
    ahead = [(i, (i + 4) % blocks) for i in range(blocks)]
    back = [(i, (i - 4) % blocks) for i in range(blocks)]
    across_y = [(i, i ^ 2) for i in range(blocks)]
    across_core = [(i, i ^ 1) for i in range(blocks)]

    def send(value, perm):
        return lax.ppermute(value, "blk", perm)

    scalars = log_scale.reshape(1), bias.reshape(1)
    own_i, token = normalize(image_emb)
    own_t, _ = normalize(text_emb, token)
    left_i = send(own_i, ahead)
    right_i = send(own_i, back)
    y_t = send(own_t, across_y)
    core_t = send(own_t, across_core)
    yc_t = send(y_t, across_core)
    top_i = send(cut(left_i, 0), ahead)
    bot_i = send(cut(right_i, rows // 2), back)

    own_p, left_p, right_p, near_images, texts, near_grads, near_sums, passes = near_part(
        scalars, (own_i, left_i, right_i), (own_t, core_t, y_t, yc_t)
    )
    from_left = send(right_p, ahead)
    from_right = send(left_p, back)
    far_images, far_grads, sums = far_part(scalars, (top_i, bot_i), texts, near_sums)

    def pair(value, axis, k):
        return lax.ppermute(value, axis, [(i, i ^ k) for i in range(lax.axis_size(axis))])

    over_y_core = [pair(sums, "blk", k) for k in (3, 2, 1)]
    far_p, y_q, to_mate, own, sums = far_grad_part(
        far_images, far_grads, near_images, texts, near_grads, own_p, sums
    )
    from_far = send(far_p, [(i, (i + 8) % blocks) for i in range(blocks)])
    from_core = send(to_mate, across_core)
    y_sum, sums_2 = relay_y(y_q, from_core, sums, *over_y_core)
    from_y = send(y_sum, across_y)
    sums_2 = add(sums_2)

    def steps(value):
        for axis, k in STEPS:
            value = value + pair(value, axis, k)
        return value

    sums_6 = lax.cond(passes[0] > 0, steps, lambda value: value, sums_2)
    over_x = [pair(sums_6, "blk", k) for k in (4, 8, 12)]
    grad_text, grad_image, sums_6 = end_part(
        scalars[0],
        own,
        (text_emb, from_core, from_y),
        (image_emb, from_left, from_right, from_far),
        sums_6,
    )
    loss, grad_scale, grad_bias = (total.reshape(()) for total in totals_part(sums_6, *over_x))
    return (loss, grad_image, grad_text, grad_scale, grad_bias)


def solution(mesh):
    in_specs = (P(("blk", "group"), None), P(("blk", "group"), None), P(), P())
    out_specs = (P(), P(("blk", "group"), None), P(("blk", "group"), None), P(), P())
    return jax.shard_map(shards, mesh=mesh, in_specs=in_specs, out_specs=out_specs, check_vma=False)
```

```python
import jax
import jax.numpy as jnp
from jax import lax
from jax.experimental import pallas as pl
from jax.experimental.pallas import tpu as pltpu
from jax.sharding import PartitionSpec as P

F32 = jnp.float32
LOG2E = 1.4426950408889634
BATCH = 65536
GATE_COST = 1
CUT_COST = 1
STEPS = (("group", 1), ("group", 2), ("group", 7), (("blk", "group"), 2 * 16 + 8))
BF16 = jnp.bfloat16
HBM = pl.BlockSpec(memory_space=pltpu.HBM)
VMEM = pl.BlockSpec(memory_space=pltpu.VMEM)
SMEM = pl.BlockSpec(memory_space=pltpu.SMEM)


def params(mib):
    return pltpu.CompilerParams(vmem_limit_bytes=mib * 1024 * 1024)


def unit_rows(emb):
    inverse = lax.rsqrt(jnp.sum(emb * emb, axis=1, keepdims=True) + 1e-06)
    return emb * inverse, inverse


def normalize_kernel(emb_ref, *refs):
    norm_ref, token = refs[-2:]
    norm_ref[...] = unit_rows(emb_ref[...])[0].astype(BF16)
    token[...] = jnp.zeros(token.shape, F32)


def normalize(emb, *after):
    rows, width = emb.shape
    return pl.pallas_call(
        normalize_kernel,
        out_shape=(
            jax.ShapeDtypeStruct((rows, width), BF16), jax.ShapeDtypeStruct((8, 128), F32)
        ),
        in_specs=[VMEM] * (1 + len(after)),
        out_specs=(VMEM,) * 2,
        compiler_params=params(16),
        cost_estimate=pl.CostEstimate(
            flops=4 * rows * width, bytes_accessed=6 * rows * width, transcendentals=rows
        ),
        name="normalize",
    )(emb, *after)


def cut(block, at):
    rows, width = block.shape

    def kernel(block_ref, out_ref):
        out_ref[...] = block_ref[pl.ds(at, rows // 2), :]

    return pl.pallas_call(
        kernel,
        out_shape=jax.ShapeDtypeStruct((rows // 2, width), block.dtype),
        in_specs=[VMEM],
        out_specs=VMEM,
        compiler_params=params(16),
        cost_estimate=pl.CostEstimate(
            flops=CUT_COST * rows * width, bytes_accessed=rows * width, transcendentals=0
        ),
        name="cut",
    )(block)


def sim_tile(image_rows, text_rows):
    return lax.dot_general(
        image_rows, text_rows, (((1,), (1,)), ((), ())), preferred_element_type=F32
    )


def pair_tile(sim, scale, bias, diagonal):
    logits = sim * scale + bias
    rows, columns = sim.shape
    if diagonal:
        positive = lax.broadcasted_iota(jnp.int32, (rows, columns), 0) == (
            lax.broadcasted_iota(jnp.int32, (rows, columns), 1)
        )
        logits = jnp.where(positive, -logits, logits)
    odds = jnp.exp2(logits)
    total = 1.0 + odds
    inverse = pl.reciprocal(total, approx=True)
    inverse = inverse * (2.0 - total * inverse)
    grad = odds * inverse
    if diagonal:
        grad = jnp.where(positive, -grad, grad)
    part = rows // 8
    product = total[:part]
    for i in range(1, 8):
        product = product * total[i * part : (i + 1) * part]

    def fold(values):
        return jnp.sum(values.reshape(values.shape[0] // 8, 8, columns), axis=0)

    return grad.astype(BF16), fold(jnp.log(product)), fold(grad * sim), fold(grad)


def logit_factors(log_scale, bias, columns):
    scale = jnp.exp(jnp.full((1, columns), log_scale[0]))
    return scale, scale * LOG2E, bias[0] * LOG2E


def write_sums(sums_ref, loss, scaled, grad):
    column = lax.broadcasted_iota(jnp.int32, sums_ref.shape, 1)
    sums_ref[...] = jnp.where(
        column == 0, jnp.sum(loss), jnp.where(column == 1, jnp.sum(scaled), jnp.sum(grad))
    )


def near_kernel(
    log_scale, bias, own_i, left_i, right_i, own_t, core_t, y_t, yc_t,
    own_out, left_out, right_out, images, texts, grads, sums_ref, passes_ref,
):
    rows = own_i.shape[0]
    factor, scale, bias = logit_factors(log_scale, bias, rows)
    for i, src in enumerate((own_i, left_i, right_i)):
        images[pl.ds(i * rows, rows), :] = src[...]
    for i, src in enumerate((own_t, core_t, y_t, yc_t)):
        texts[pl.ds(i * rows, rows), :] = src[...]
    loss = scaled = grad = jnp.zeros((8, rows), F32)
    tiles = [(b, t) for b in range(3) for t in range(4)]

    def sim_of(k):
        b, t = tiles[k]
        return sim_tile(images[pl.ds(b * rows, rows), :], texts[pl.ds(t * rows, rows), :])

    sim = sim_of(0)
    for k, (b, t) in enumerate(tiles):
        sim_next = sim_of(k + 1) if k + 1 < len(tiles) else None
        grad_q, loss_now, scaled_now, grad_now = pair_tile(sim, scale, bias, k == 0)
        grads[pl.ds(b * rows, rows), pl.ds(t * rows, rows)] = grad_q
        loss, scaled, grad = loss + loss_now, scaled + scaled_now, grad + grad_now
        sim = sim_next
        if t == 3:
            partial = jnp.dot(
                grads[pl.ds(b * rows, rows), :], texts[...], preferred_element_type=F32
            )
            out = (own_out, left_out, right_out)[b]
            out[...] = partial.astype(out.dtype)
    write_sums(sums_ref, loss, scaled * factor, grad)
    passes_ref[0] = 1


def text_grad(grads, near_images, far_grads, far_images, at):
    return lax.dot_general(
        grads[:, at], near_images[...], (((0,), (0,)), ((), ())), preferred_element_type=F32
    ) + lax.dot_general(
        far_grads[:, at], far_images[...], (((0,), (0,)), ((), ())), preferred_element_type=F32
    )


def far_kernel(log_scale, bias, top_i, bot_i, texts, near_sums, images, grads, sums_ref):
    half = top_i.shape[0]
    rows = 2 * half
    factor, scale, bias = logit_factors(log_scale, bias, rows)
    images[pl.ds(0, half), :] = top_i[...]
    images[pl.ds(half, half), :] = bot_i[...]
    loss = scaled = grad = jnp.zeros((8, rows), F32)

    def sim_of(t):
        return sim_tile(images[...], texts[pl.ds(t * rows, rows), :])

    sim = sim_of(0)
    for t in range(4):
        sim_next = sim_of(t + 1) if t < 3 else None
        grad_q, loss_now, scaled_now, grad_now = pair_tile(sim, scale, bias, False)
        grads[:, pl.ds(t * rows, rows)] = grad_q
        loss, scaled, grad = loss + loss_now, scaled + scaled_now, grad + grad_now
        sim = sim_next
    write_sums(sums_ref, loss, scaled * factor, grad)
    sums_ref[...] += near_sums[...]


def far_grad_kernel(
    far_images, far_grads, near_images, texts, near_grads, own_p, sums,
    far_top, far_bot, y_out, mate_out, own_out, sums_out,
):
    rows = far_images.shape[0]
    half = rows // 2
    partial = jnp.dot(far_grads[...], texts[...], preferred_element_type=F32)
    far_top[...] = partial[:half].astype(BF16)
    far_bot[...] = partial[half:].astype(BF16)
    for t, out in (
        (3, mate_out.at[pl.ds(0, rows)]),
        (1, mate_out.at[pl.ds(rows, rows)]),
        (2, y_out),
        (0, own_out.at[pl.ds(0, rows)]),
    ):
        out[...] = text_grad(
            near_grads, near_images, far_grads, far_images, pl.ds(t * rows, rows)
        ).astype(out.dtype)
    own_out[pl.ds(rows, rows), :] = own_p[...]
    sums_out[...] = sums[...]


def near_part(scalars, images, texts):
    rows, width = texts[0].shape
    shape = jax.ShapeDtypeStruct
    return pl.pallas_call(
        near_kernel,
        out_shape=(
            shape((rows, width), BF16),
            shape((rows, width), F32),
            shape((rows, width), BF16),
            shape((3 * rows, width), BF16),
            shape((4 * rows, width), BF16),
            shape((3 * rows, 4 * rows), BF16),
            shape((8, 128), F32),
            shape((1,), jnp.int32),
        ),
        in_specs=[SMEM] * 2 + [VMEM] * 7,
        out_specs=(VMEM,) * 7 + (SMEM,),
        compiler_params=params(16),
        cost_estimate=pl.CostEstimate(
            flops=8 * 2 * 2 * 12 * rows * rows * width,
            bytes_accessed=24 * rows * width,
            transcendentals=3 * 12 * rows * rows,
        ),
        name="near",
    )(*scalars, *images, *texts)


def far_part(scalars, far_images, texts, near_sums):
    half, width = far_images[0].shape
    rows = 2 * half
    shape = jax.ShapeDtypeStruct
    return pl.pallas_call(
        far_kernel,
        out_shape=(
            shape((rows, width), BF16), shape((rows, 4 * rows), BF16), shape((8, 128), F32)
        ),
        in_specs=[SMEM] * 2 + [VMEM] * 4,
        out_specs=(VMEM,) * 3,
        compiler_params=params(16),
        cost_estimate=pl.CostEstimate(
            flops=rows * rows * width, bytes_accessed=2 * rows * width, transcendentals=rows * rows
        ),
        name="far",
    )(*scalars, *far_images, texts, near_sums)


def far_grad_part(far_images, far_grads, near_images, texts, near_grads, own_p, sums):
    rows, width = far_images.shape
    shape = jax.ShapeDtypeStruct
    return pl.pallas_call(
        far_grad_kernel,
        out_shape=(shape((rows // 2, width), BF16),) * 2
        + (
            shape((rows, width), F32), shape((2 * rows, width), BF16),
            shape((2 * rows, width), BF16), shape(sums.shape, F32),
        ),
        in_specs=[VMEM] * 7,
        out_specs=(VMEM,) * 6,
        compiler_params=params(16),
        cost_estimate=pl.CostEstimate(
            flops=rows * rows * width, bytes_accessed=2 * rows * width, transcendentals=0
        ),
        name="far_grad",
    )(far_images, far_grads, near_images, texts, near_grads, own_p, sums)


def add_kernel(*refs):
    *parts, out = refs
    out[...] = sum((part[...] for part in parts[1:]), parts[0][...])


def add(*parts):
    one = parts[0]
    return pl.pallas_call(
        add_kernel,
        out_shape=jax.ShapeDtypeStruct(one.shape, F32),
        in_specs=[VMEM] * len(parts),
        out_specs=VMEM,
        compiler_params=params(16),
        cost_estimate=pl.CostEstimate(
            flops=GATE_COST * one.size, bytes_accessed=one.size, transcendentals=0
        ),
        name="add",
    )(*parts)


def relay_kernel(
    y_own, y_passing, left, left_passing, sums, sums_a, sums_b, sums_c, y_out, left_out, sums_out
):
    rows = y_own.shape[0]
    half = rows // 2
    y_out[...] = (y_own[...] + y_passing[:rows, :].astype(F32)).astype(BF16)
    left_out[:half, :] = left[:half, :].astype(BF16)
    left_out[half:, :] = (left[half:, :] + left_passing[...].astype(F32)).astype(BF16)
    sums_out[...] = sums[...] + sums_a[...] + sums_b[...] + sums_c[...]


def relay(y_own, y_passing, left, left_passing, sums, *arrived):
    shape = jax.ShapeDtypeStruct
    return pl.pallas_call(
        relay_kernel,
        out_shape=(shape(y_own.shape, BF16), shape(left.shape, BF16), shape(sums.shape, F32)),
        in_specs=[VMEM] * 8,
        out_specs=(VMEM,) * 3,
        compiler_params=params(16),
        cost_estimate=pl.CostEstimate(
            flops=y_own.size, bytes_accessed=y_own.size, transcendentals=0
        ),
        name="relay",
    )(y_own, y_passing, left, left_passing, sums, *arrived)


def backnorm(emb, upstream, scale):
    hat, inverse = unit_rows(emb)
    along = jnp.sum(hat * upstream, axis=1, keepdims=True)
    return (scale * inverse) * (upstream - hat * along)


def end_kernel(
    log_scale, own, text_emb, from_core, from_y, image_emb, from_left, from_right, from_far, sums,
    text_out, image_out, sums_out, text_slots, image_slots, sems,
):
    scale = jnp.exp(jnp.full((1, 1), log_scale[0]))
    step = text_emb.shape[0] // 4
    sets = (
        (text_emb, (from_core, from_y), text_out, text_slots),
        (image_emb, (from_left, from_right, from_far), image_out, image_slots),
    )
    copies = []
    for k, (emb, parts, out, slots) in enumerate(sets):
        for i in range(4):
            at = pl.ds(i * step, step)
            upstream = own[pl.ds((4 * k + i) * step, step), :].astype(F32)
            for part in parts:
                start = max(part.shape[0] - 4 * step, 0) + i * step
                if start < part.shape[0]:
                    upstream += part[pl.ds(start, step), :].astype(F32)
            slots[at, :] = backnorm(emb[at, :], upstream, scale)
            copy = pltpu.make_async_copy(slots.at[at], out.at[at], sems.at[len(copies)])
            copy.start()
            copies.append(copy)
    sums_out[...] = sums[...]
    for copy in copies:
        copy.wait()


def end_part(log_scale, own, text_parts, image_parts, sums):
    rows, width = text_parts[0].shape
    shape = jax.ShapeDtypeStruct
    return pl.pallas_call(
        end_kernel,
        out_shape=(shape((rows, width), F32),) * 2 + (shape(sums.shape, F32),),
        in_specs=[SMEM] + [VMEM] * 9,
        out_specs=(HBM, HBM, VMEM),
        scratch_shapes=[
            pltpu.VMEM((rows, width), F32),
            pltpu.VMEM((rows, width), F32),
            pltpu.SemaphoreType.DMA((8,)),
        ],
        compiler_params=params(24),
        cost_estimate=pl.CostEstimate(
            flops=16 * rows * width, bytes_accessed=2 * rows * width, transcendentals=2 * rows
        ),
        name="end",
    )(log_scale, own, *text_parts, *image_parts, sums)


def totals_kernel(*refs):
    parts, outs = refs[:-3], refs[-3:]
    total = sum((part[...] for part in parts[1:]), parts[0][...])
    for i, out in enumerate(outs):
        out[0] = jnp.sum(total[0:1, i : i + 1]) * (1.0 / BATCH)


def totals_part(*parts):
    return pl.pallas_call(
        totals_kernel,
        out_shape=(jax.ShapeDtypeStruct((1,), F32),) * 3,
        in_specs=[VMEM] * len(parts),
        out_specs=(SMEM,) * 3,
        compiler_params=params(16),
        cost_estimate=pl.CostEstimate(flops=4096, bytes_accessed=4096, transcendentals=0),
        name="totals",
    )(*parts)


def shards(image_emb, text_emb, log_scale, bias):
    rows = image_emb.shape[0]
    blocks = lax.axis_size("blk")
    ahead = [(i, (i + 4) % blocks) for i in range(blocks)]
    back = [(i, (i - 4) % blocks) for i in range(blocks)]
    across_y = [(i, i ^ 2) for i in range(blocks)]
    across_core = [(i, i ^ 1) for i in range(blocks)]

    def send(value, perm):
        return lax.ppermute(value, "blk", perm)

    scalars = log_scale.reshape(1), bias.reshape(1)
    own_i, token = normalize(image_emb)
    own_t, _ = normalize(text_emb, token)
    left_i = send(own_i, ahead)
    right_i = send(own_i, back)
    y_t = send(own_t, across_y)
    core_t = send(own_t, across_core)
    yc_t = send(y_t, across_core)
    top_i = send(cut(left_i, 0), ahead)
    bot_i = send(cut(right_i, rows // 2), back)

    own_p, left_p, right_p, near_images, texts, near_grads, near_sums, passes = near_part(
        scalars, (own_i, left_i, right_i), (own_t, core_t, y_t, yc_t)
    )
    from_left = send(right_p, ahead)
    far_images, far_grads, sums = far_part(scalars, (top_i, bot_i), texts, near_sums)

    def pair(value, axis, k):
        return lax.ppermute(value, axis, [(i, i ^ k) for i in range(lax.axis_size(axis))])

    over_y_core = [pair(sums, "blk", k) for k in (3, 2, 1)]
    far_top, far_bot, y_q, to_mate, own, sums = far_grad_part(
        far_images, far_grads, near_images, texts, near_grads, own_p, sums
    )
    from_far = send(far_top, [(i, (i + 8) % blocks) for i in range(blocks)])
    relay_bot = send(far_bot, back)
    from_core = send(to_mate, across_core)
    y_sum, left_sum, sums_2 = relay(y_q, from_core, left_p, relay_bot, sums, *over_y_core)
    from_right = send(left_sum, back)
    from_y = send(y_sum, across_y)
    sums_2 = add(sums_2)

    def steps(value):
        for axis, k in STEPS:
            value = value + pair(value, axis, k)
        return value

    sums_6 = lax.cond(passes[0] > 0, steps, lambda value: value, sums_2)
    over_x = [pair(sums_6, "blk", k) for k in (4, 8, 12)]
    grad_text, grad_image, sums_6 = end_part(
        scalars[0],
        own,
        (text_emb, from_core, from_y),
        (image_emb, from_left, from_right, from_far),
        sums_6,
    )
    loss, grad_scale, grad_bias = (total.reshape(()) for total in totals_part(sums_6, *over_x))
    return (loss, grad_image, grad_text, grad_scale, grad_bias)


def solution(mesh):
    in_specs = (P(("blk", "group"), None), P(("blk", "group"), None), P(), P())
    out_specs = (P(), P(("blk", "group"), None), P(("blk", "group"), None), P(), P())
    return jax.shard_map(shards, mesh=mesh, in_specs=in_specs, out_specs=out_specs, check_vma=False)
```

```python
import jax
import jax.numpy as jnp
from jax import lax
from jax.experimental import pallas as pl
from jax.experimental.pallas import tpu as pltpu
from jax.sharding import PartitionSpec as P

F32 = jnp.float32
LOG2E = 1.4426950408889634
BATCH = 65536
GATE_COST = 1
CUT_COST = 1
STEPS = (("group", 1), ("group", 2), ("group", 7), (("blk", "group"), 2 * 16 + 8))
BF16 = jnp.bfloat16
HBM = pl.BlockSpec(memory_space=pltpu.HBM)
VMEM = pl.BlockSpec(memory_space=pltpu.VMEM)
SMEM = pl.BlockSpec(memory_space=pltpu.SMEM)


def params(mib):
    return pltpu.CompilerParams(vmem_limit_bytes=mib * 1024 * 1024)


def unit_rows(emb):
    inverse = lax.rsqrt(jnp.sum(emb * emb, axis=1, keepdims=True) + 1e-06)
    return emb * inverse, inverse


def normalize_kernel(emb_ref, *refs):
    norm_ref, token = refs[-2:]
    norm_ref[...] = unit_rows(emb_ref[...])[0].astype(BF16)
    token[...] = jnp.zeros(token.shape, F32)


def normalize(emb, *after):
    rows, width = emb.shape
    return pl.pallas_call(
        normalize_kernel,
        out_shape=(
            jax.ShapeDtypeStruct((rows, width), BF16), jax.ShapeDtypeStruct((8, 128), F32)
        ),
        in_specs=[VMEM] * (1 + len(after)),
        out_specs=(VMEM,) * 2,
        compiler_params=params(16),
        cost_estimate=pl.CostEstimate(
            flops=4 * rows * width, bytes_accessed=6 * rows * width, transcendentals=rows
        ),
        name="normalize",
    )(emb, *after)


def cut(block, at):
    rows, width = block.shape

    def kernel(block_ref, out_ref):
        out_ref[...] = block_ref[pl.ds(at, rows // 2), :]

    return pl.pallas_call(
        kernel,
        out_shape=jax.ShapeDtypeStruct((rows // 2, width), block.dtype),
        in_specs=[VMEM],
        out_specs=VMEM,
        compiler_params=params(16),
        cost_estimate=pl.CostEstimate(
            flops=CUT_COST * rows * width, bytes_accessed=rows * width, transcendentals=0
        ),
        name="cut",
    )(block)


def sim_tile(image_rows, text_rows):
    return lax.dot_general(
        image_rows, text_rows, (((1,), (1,)), ((), ())), preferred_element_type=F32
    )


def pair_tile(sim, scale, bias, diagonal):
    logits = sim * scale + bias
    rows, columns = sim.shape
    if diagonal:
        positive = lax.broadcasted_iota(jnp.int32, (rows, columns), 0) == (
            lax.broadcasted_iota(jnp.int32, (rows, columns), 1)
        )
        logits = jnp.where(positive, -logits, logits)
    odds = jnp.exp2(logits)
    total = 1.0 + odds
    inverse = pl.reciprocal(total, approx=True)
    inverse = inverse * (2.0 - total * inverse)
    grad = odds * inverse
    if diagonal:
        grad = jnp.where(positive, -grad, grad)
    part = rows // 8
    product = total[:part]
    for i in range(1, 8):
        product = product * total[i * part : (i + 1) * part]

    def fold(values):
        return jnp.sum(values.reshape(values.shape[0] // 8, 8, columns), axis=0)

    return grad.astype(BF16), fold(jnp.log(product)), fold(grad * sim), fold(grad)


def logit_factors(log_scale, bias, columns):
    scale = jnp.exp(jnp.full((1, columns), log_scale[0]))
    return scale, scale * LOG2E, bias[0] * LOG2E


def write_sums(sums_ref, loss, scaled, grad):
    column = lax.broadcasted_iota(jnp.int32, sums_ref.shape, 1)
    sums_ref[...] = jnp.where(
        column == 0, jnp.sum(loss), jnp.where(column == 1, jnp.sum(scaled), jnp.sum(grad))
    )


def near_kernel(
    log_scale, bias, own_i, left_i, right_i, own_t, core_t, y_t, yc_t,
    own_out, left_out, right_out, images, texts, grads, sums_ref, passes_ref,
):
    rows = own_i.shape[0]
    factor, scale, bias = logit_factors(log_scale, bias, rows)
    for i, src in enumerate((own_i, left_i, right_i)):
        images[pl.ds(i * rows, rows), :] = src[...]
    for i, src in enumerate((own_t, core_t, y_t, yc_t)):
        texts[pl.ds(i * rows, rows), :] = src[...]
    loss = scaled = grad = jnp.zeros((8, rows), F32)
    tiles = [(b, t) for b in range(3) for t in range(4)]

    def sim_of(k):
        b, t = tiles[k]
        return sim_tile(images[pl.ds(b * rows, rows), :], texts[pl.ds(t * rows, rows), :])

    sim = sim_of(0)
    for k, (b, t) in enumerate(tiles):
        sim_next = sim_of(k + 1) if k + 1 < len(tiles) else None
        grad_q, loss_now, scaled_now, grad_now = pair_tile(sim, scale, bias, k == 0)
        grads[pl.ds(b * rows, rows), pl.ds(t * rows, rows)] = grad_q
        loss, scaled, grad = loss + loss_now, scaled + scaled_now, grad + grad_now
        sim = sim_next
        if t == 3:
            partial = jnp.dot(
                grads[pl.ds(b * rows, rows), :], texts[...], preferred_element_type=F32
            )
            out = (own_out, left_out, right_out)[b]
            out[...] = partial.astype(out.dtype)
    write_sums(sums_ref, loss, scaled * factor, grad)
    passes_ref[0] = 1


def text_grad(grads, near_images, far_grads, far_images, at):
    return lax.dot_general(
        grads[:, at], near_images[...], (((0,), (0,)), ((), ())), preferred_element_type=F32
    ) + lax.dot_general(
        far_grads[:, at], far_images[...], (((0,), (0,)), ((), ())), preferred_element_type=F32
    )


def far_kernel(log_scale, bias, top_i, bot_i, texts, near_sums, images, grads, sums_ref):
    half = top_i.shape[0]
    rows = 2 * half
    factor, scale, bias = logit_factors(log_scale, bias, rows)
    images[pl.ds(0, half), :] = top_i[...]
    images[pl.ds(half, half), :] = bot_i[...]
    loss = scaled = grad = jnp.zeros((8, rows), F32)

    def sim_of(t):
        return sim_tile(images[...], texts[pl.ds(t * rows, rows), :])

    sim = sim_of(0)
    for t in range(4):
        sim_next = sim_of(t + 1) if t < 3 else None
        grad_q, loss_now, scaled_now, grad_now = pair_tile(sim, scale, bias, False)
        grads[:, pl.ds(t * rows, rows)] = grad_q
        loss, scaled, grad = loss + loss_now, scaled + scaled_now, grad + grad_now
        sim = sim_next
    write_sums(sums_ref, loss, scaled * factor, grad)
    sums_ref[...] += near_sums[...]


def far_grad_kernel(
    far_images, far_grads, near_images, texts, near_grads, own_p, sums,
    far_out, y_out, mate_out, own_out, sums_out,
):
    rows = far_images.shape[0]
    far_out[...] = jnp.dot(
        far_grads[...], texts[...], preferred_element_type=F32
    ).astype(BF16)
    for t, out in (
        (3, mate_out.at[pl.ds(0, rows)]),
        (1, mate_out.at[pl.ds(rows, rows)]),
        (2, y_out),
        (0, own_out.at[pl.ds(0, rows)]),
    ):
        out[...] = text_grad(
            near_grads, near_images, far_grads, far_images, pl.ds(t * rows, rows)
        ).astype(out.dtype)
    own_out[pl.ds(rows, rows), :] = own_p[...]
    sums_out[...] = sums[...]


def near_part(scalars, images, texts):
    rows, width = texts[0].shape
    shape = jax.ShapeDtypeStruct
    return pl.pallas_call(
        near_kernel,
        out_shape=(
            shape((rows, width), BF16),
            shape((rows, width), BF16),
            shape((rows, width), BF16),
            shape((3 * rows, width), BF16),
            shape((4 * rows, width), BF16),
            shape((3 * rows, 4 * rows), BF16),
            shape((8, 128), F32),
            shape((1,), jnp.int32),
        ),
        in_specs=[SMEM] * 2 + [VMEM] * 7,
        out_specs=(VMEM,) * 7 + (SMEM,),
        compiler_params=params(16),
        cost_estimate=pl.CostEstimate(
            flops=8 * 2 * 2 * 12 * rows * rows * width,
            bytes_accessed=24 * rows * width,
            transcendentals=3 * 12 * rows * rows,
        ),
        name="near",
    )(*scalars, *images, *texts)


def far_part(scalars, far_images, texts, near_sums):
    half, width = far_images[0].shape
    rows = 2 * half
    shape = jax.ShapeDtypeStruct
    return pl.pallas_call(
        far_kernel,
        out_shape=(
            shape((rows, width), BF16), shape((rows, 4 * rows), BF16), shape((8, 128), F32)
        ),
        in_specs=[SMEM] * 2 + [VMEM] * 4,
        out_specs=(VMEM,) * 3,
        compiler_params=params(16),
        cost_estimate=pl.CostEstimate(
            flops=rows * rows * width, bytes_accessed=2 * rows * width, transcendentals=rows * rows
        ),
        name="far",
    )(*scalars, *far_images, texts, near_sums)


def far_grad_part(far_images, far_grads, near_images, texts, near_grads, own_p, sums):
    rows, width = far_images.shape
    shape = jax.ShapeDtypeStruct
    return pl.pallas_call(
        far_grad_kernel,
        out_shape=(
            shape((rows, width), BF16), shape((rows, width), F32), shape((2 * rows, width), BF16),
            shape((2 * rows, width), BF16), shape(sums.shape, F32),
        ),
        in_specs=[VMEM] * 7,
        out_specs=(VMEM,) * 5,
        compiler_params=params(16),
        cost_estimate=pl.CostEstimate(
            flops=rows * rows * width, bytes_accessed=2 * rows * width, transcendentals=0
        ),
        name="far_grad",
    )(far_images, far_grads, near_images, texts, near_grads, own_p, sums)


def add_kernel(*refs):
    *parts, out = refs
    out[...] = sum((part[...] for part in parts[1:]), parts[0][...])


def add(*parts):
    one = parts[0]
    return pl.pallas_call(
        add_kernel,
        out_shape=jax.ShapeDtypeStruct(one.shape, F32),
        in_specs=[VMEM] * len(parts),
        out_specs=VMEM,
        compiler_params=params(16),
        cost_estimate=pl.CostEstimate(
            flops=GATE_COST * one.size, bytes_accessed=one.size, transcendentals=0
        ),
        name="add",
    )(*parts)


def relay_y_kernel(own, passing, sums, sums_a, sums_b, sums_c, out, sums_out):
    rows = own.shape[0]
    out[...] = (own[...] + passing[:rows, :].astype(F32)).astype(BF16)
    sums_out[...] = sums[...] + sums_a[...] + sums_b[...] + sums_c[...]


def relay_y(own, passing, sums, *arrived):
    return pl.pallas_call(
        relay_y_kernel,
        out_shape=(
            jax.ShapeDtypeStruct(own.shape, BF16), jax.ShapeDtypeStruct(sums.shape, F32)
        ),
        in_specs=[VMEM] * 6,
        out_specs=(VMEM,) * 2,
        compiler_params=params(16),
        cost_estimate=pl.CostEstimate(flops=own.size, bytes_accessed=own.size, transcendentals=0),
        name="relay_y",
    )(own, passing, sums, *arrived)


def backnorm(emb, upstream, scale):
    hat, inverse = unit_rows(emb)
    along = jnp.sum(hat * upstream, axis=1, keepdims=True)
    return (scale * inverse) * (upstream - hat * along)


def end_kernel(
    log_scale, own, text_emb, from_core, from_y, image_emb, from_left, from_right, from_far, sums,
    text_out, image_out, sums_out, text_slots, image_slots, sems,
):
    scale = jnp.exp(jnp.full((1, 1), log_scale[0]))
    step = text_emb.shape[0] // 4
    sets = (
        (text_emb, (from_core, from_y), text_out, text_slots),
        (image_emb, (from_left, from_right, from_far), image_out, image_slots),
    )
    copies = []
    for k, (emb, parts, out, slots) in enumerate(sets):
        for i in range(4):
            at = pl.ds(i * step, step)
            upstream = own[pl.ds((4 * k + i) * step, step), :].astype(F32)
            for part in parts:
                skip = part.shape[0] - 4 * step
                upstream += part[pl.ds(skip + i * step, step), :].astype(F32)
            slots[at, :] = backnorm(emb[at, :], upstream, scale)
            copy = pltpu.make_async_copy(slots.at[at], out.at[at], sems.at[len(copies)])
            copy.start()
            copies.append(copy)
    sums_out[...] = sums[...]
    for copy in copies:
        copy.wait()


def end_part(log_scale, own, text_parts, image_parts, sums):
    rows, width = text_parts[0].shape
    shape = jax.ShapeDtypeStruct
    return pl.pallas_call(
        end_kernel,
        out_shape=(shape((rows, width), F32),) * 2 + (shape(sums.shape, F32),),
        in_specs=[SMEM] + [VMEM] * 9,
        out_specs=(HBM, HBM, VMEM),
        scratch_shapes=[
            pltpu.VMEM((rows, width), F32),
            pltpu.VMEM((rows, width), F32),
            pltpu.SemaphoreType.DMA((8,)),
        ],
        compiler_params=params(24),
        cost_estimate=pl.CostEstimate(
            flops=16 * rows * width, bytes_accessed=2 * rows * width, transcendentals=2 * rows
        ),
        name="end",
    )(log_scale, own, *text_parts, *image_parts, sums)


def totals_kernel(*refs):
    parts, outs = refs[:-3], refs[-3:]
    total = sum((part[...] for part in parts[1:]), parts[0][...])
    for i, out in enumerate(outs):
        out[0] = jnp.sum(total[0:1, i : i + 1]) * (1.0 / BATCH)


def totals_part(*parts):
    return pl.pallas_call(
        totals_kernel,
        out_shape=(jax.ShapeDtypeStruct((1,), F32),) * 3,
        in_specs=[VMEM] * len(parts),
        out_specs=(SMEM,) * 3,
        compiler_params=params(16),
        cost_estimate=pl.CostEstimate(flops=4096, bytes_accessed=4096, transcendentals=0),
        name="totals",
    )(*parts)


def shards(image_emb, text_emb, log_scale, bias):
    rows = image_emb.shape[0]
    blocks = lax.axis_size("blk")
    ahead = [(i, (i + 4) % blocks) for i in range(blocks)]
    back = [(i, (i - 4) % blocks) for i in range(blocks)]
    across_y = [(i, i ^ 2) for i in range(blocks)]
    across_core = [(i, i ^ 1) for i in range(blocks)]

    def send(value, perm):
        return lax.ppermute(value, "blk", perm)

    scalars = log_scale.reshape(1), bias.reshape(1)
    own_i, token = normalize(image_emb)
    own_t, _ = normalize(text_emb, token)
    left_i = send(own_i, ahead)
    right_i = send(own_i, back)
    y_t = send(own_t, across_y)
    core_t = send(own_t, across_core)
    yc_t = send(y_t, across_core)
    top_i = send(cut(left_i, 0), ahead)
    bot_i = send(cut(right_i, rows // 2), back)

    own_p, left_p, right_p, near_images, texts, near_grads, near_sums, passes = near_part(
        scalars, (own_i, left_i, right_i), (own_t, core_t, y_t, yc_t)
    )
    from_left = send(right_p, ahead)
    from_right = send(left_p, back)
    far_images, far_grads, sums = far_part(scalars, (top_i, bot_i), texts, near_sums)

    def pair(value, axis, k):
        return lax.ppermute(value, axis, [(i, i ^ k) for i in range(lax.axis_size(axis))])

    over_y_core = [pair(sums, "blk", k) for k in (3, 2, 1)]
    far_p, y_q, to_mate, own, sums = far_grad_part(
        far_images, far_grads, near_images, texts, near_grads, own_p, sums
    )
    from_far = send(far_p, [(i, (i + 8) % blocks) for i in range(blocks)])
    from_core = send(to_mate, across_core)
    y_sum, sums_2 = relay_y(y_q, from_core, sums, *over_y_core)
    from_y = send(y_sum, across_y)
    sums_2 = add(sums_2)

    def steps(value):
        for axis, k in STEPS:
            value = value + pair(value, axis, k)
        return value

    sums_6 = lax.cond(passes[0] > 0, steps, lambda value: value, sums_2)
    over_x = [pair(sums_6, "blk", k) for k in (4, 8, 12)]
    grad_text, grad_image, sums_6 = end_part(
        scalars[0],
        own,
        (text_emb, from_core, from_y),
        (image_emb, from_left, from_right, from_far),
        sums_6,
    )
    loss, grad_scale, grad_bias = (total.reshape(()) for total in totals_part(sums_6, *over_x))
    return (loss, grad_image, grad_text, grad_scale, grad_bias)


def solution(mesh):
    in_specs = (P(("blk", "group"), None), P(("blk", "group"), None), P(), P())
    out_specs = (P(), P(("blk", "group"), None), P(("blk", "group"), None), P(), P())
    return jax.shard_map(shards, mesh=mesh, in_specs=in_specs, out_specs=out_specs, check_vma=False)
```
